32 devices in a mesh: batch: 4 (over z), seq: 8 (over y, x, core).
Axes of the slice: x: 2, y: 2, z: 4, core: 2. Of those that a mesh axis runs over, the one named last changes fastest.
Arguments:
- tokens: bfloat16 [4, 1024, 768], P('batch', 'seq'), may hold values from -6 to 6
- skip_features: bfloat16 [4, 8192, 128], P('batch', 'seq'), may hold values from -6 to 6
- out_grad: bfloat16 [4, 8192, 128], P('batch', 'seq'), may hold values from -6 to 6
- crop_lengths: int32 [4, 4], P('batch'), may hold values from 1 to 61, as said below
- attend_gain: bfloat16 [768], P('seq'), may hold values from 0.25 to 1.75
- attend_shift: bfloat16 [768], P('seq'), may hold values from -4 to 4
- joint_weight: bfloat16 [768, 2304], P('seq'), may hold values from -0.21875 to 0.21875
- query_bias: bfloat16 [768], P('seq'), may hold values from -4 to 4
- value_bias: bfloat16 [768], P('seq'), may hold values from -4 to 4
- output_weight: bfloat16 [768, 768], P('seq'), may hold values from -6 to 6
- output_bias: bfloat16 [768], P('seq'), may hold values from -4 to 4
- mixer_gain: bfloat16 [768], P('seq'), may hold values from 0.25 to 1.75
- mixer_shift: bfloat16 [768], P('seq'), may hold values from -4 to 4
- expand_weight: bfloat16 [768, 3072], P('seq'), may hold values from -0.21875 to 0.21875
- expand_bias: bfloat16 [3072], P('seq'), may hold values from -4 to 4
- reduce_weight: bfloat16 [3072, 768], P('seq'), may hold values from -0.109375 to 0.109375
- reduce_bias: bfloat16 [768], P('seq'), may hold values from -4 to 4
- upsample_weight: bfloat16 [768, 1024], P('seq'), may hold values from -0.21875 to 0.21875
- kernel_first: bfloat16 [6912, 128], P('seq'), may hold values from -0.078125 to 0.078125
- kernel_second: bfloat16 [3456, 128], P('seq'), may hold values from -0.109375 to 0.109375
- residual_weight: bfloat16 [256, 128], P('seq'), may hold values from -0.375 to 0.375
Outputs:
- decoded: bfloat16 [4, 8192, 128], P('batch', 'seq')
- tokens_grad: float32 [4, 1024, 768], P('batch', 'seq')
- skip_grad: float32 [4, 8192, 128], P('batch', 'seq')
- attend_gain_grad: float32 [768], P('seq')
- attend_shift_grad: float32 [768], P('seq')
- joint_weight_grad: float32 [768, 2304], P('seq')
- query_bias_grad: float32 [768], P('seq')
- value_bias_grad: float32 [768], P('seq')
- output_weight_grad: float32 [768, 768], P('seq')
- output_bias_grad: float32 [768], P('seq')
- mixer_gain_grad: float32 [768], P('seq')
- mixer_shift_grad: float32 [768], P('seq')
- expand_weight_grad: float32 [768, 3072], P('seq')
- expand_bias_grad: float32 [3072], P('seq')
- reduce_weight_grad: float32 [3072, 768], P('seq')
- reduce_bias_grad: float32 [768], P('seq')
- upsample_weight_grad: float32 [768, 1024], P('seq')
- kernel_first_grad: float32 [6912, 128], P('seq')
- kernel_second_grad: float32 [3456, 128], P('seq')
- residual_weight_grad: float32 [256, 128], P('seq')
The draws below stay inside these ranges and needn't reach their ends.
Inputs may be any that keep to these rules, and one draw needn't show every extreme that they name: `crop_lengths`: each group's 4 crop lengths are numbers of slices summing to 64. In each group one crop starts within the first 8 slices and ends within the last 8; each of the others is no longer than the whole part of 7 / 3 slices.
All inputs are finite; a program needn't handle non-finite values.
Results may differ from the reference program's by a relative error of at most 0.028.
Values may be sent and summed in bfloat16 or wider, within the bound.
No kernel may reach another device: no remote copies, remote signals or barrier semaphores. Data moves between devices by JAX's collectives and lax.ppermute only.
A program may use at most 256 MiB of HBM per device.

```python
import math
import jax
import jax.numpy as jnp
from jax import lax

D = 768
HEADS = 12
MLP = 3072
CDEC = 128
PH = 4
SL = 8
CROPS = 4
SLICES = 64
TOKENS = 1024
POS = 8192
GROUPS = 4


def draw_crop_lengths(key, part):
    key = jax.random.fold_in(key, 7)
    small_key, place_key, pick_key = jax.random.split(key, 3)
    smalls = jax.random.randint(small_key, (GROUPS, CROPS - 1), 1, (SL - 1) // (CROPS - 1) + 1)
    chosen = jax.random.randint(pick_key, (), 0, GROUPS)
    smalls = jnp.where((jnp.arange(GROUPS) == chosen)[:, None], 1, smalls)
    longest = SLICES - jnp.sum(smalls, axis=1)
    position = jax.random.randint(place_key, (GROUPS, 1), 0, CROPS)
    slot_ids = jnp.arange(CROPS)[None, :]
    before = jnp.concatenate([smalls, smalls[:, -1:]], axis=1)
    behind = jnp.concatenate([smalls[:, :1], smalls], axis=1)
    lengths = jnp.where(slot_ids < position, before, jnp.where(slot_ids == position, longest[:, None], behind))
    return lengths.astype(jnp.int32)


def block_scale(key, shape, cuts, smallest, top_value):
    level, own = 1.0, jax.random.fold_in(key, 6)
    for dim, shards_of in cuts:
        draws = jnp.exp(jax.random.uniform(jax.random.fold_in(own, dim), (shards_of,), jnp.float32, smallest / len(cuts), top_value / len(cuts)))
        level = level * jnp.repeat(draws, shape[dim] // shards_of).reshape([-1 if axis == dim else 1 for axis in range(len(shape))])
    return level


def scatter_about(own_key, extent, width, bound, cuts=(), kind=jnp.bfloat16):
    entries = width * jax.random.normal(own_key, extent, jnp.float32)
    if cuts:
        entries = entries * block_scale(own_key, extent, cuts, -0.22, 0.18)
    return jnp.clip(entries, -bound, bound).astype(kind)


def setup_inputs(seed: int = 0) -> dict:
    seeds = jax.random.split(jax.random.key(seed), 22)
    tokens = scatter_about(seeds[0], (GROUPS, TOKENS, D), 1.0, 6.0, ((0, 4), (1, 8)))
    skip_features = scatter_about(seeds[1], (GROUPS, POS, CDEC), 1.0, 6.0, ((0, 4), (1, 8)))
    out_grad = scatter_about(seeds[2], (GROUPS, POS, CDEC), 1.0, 6.0, ((0, 4), (1, 8)))
    crop_lengths = draw_crop_lengths(jax.random.fold_in(seeds[21], 71), 0)
    attend_gain = jnp.clip(1.0 + 0.15 * jax.random.normal(seeds[4], (D,), jnp.float32), 0.25, 1.75).astype(jnp.bfloat16)
    attend_shift = scatter_about(seeds[5], (D,), 0.3, 4.0, ((0, 8),))
    joint_weight = scatter_about(seeds[6], (D, 3 * D), D ** -0.5, 0.21875, ((0, 8),))
    query_bias = scatter_about(seeds[7], (D,), 0.3, 4.0, ((0, 8),))
    value_bias = scatter_about(seeds[8], (D,), 0.3, 4.0, ((0, 8),))
    output_weight = scatter_about(seeds[9], (D, D), 1.0, 6.0, ((0, 8),))
    output_bias = scatter_about(seeds[10], (D,), 0.3, 4.0, ((0, 8),))
    mixer_gain = jnp.clip(1.0 + 0.15 * jax.random.normal(seeds[11], (D,), jnp.float32), 0.25, 1.75).astype(jnp.bfloat16)
    mixer_shift = scatter_about(seeds[12], (D,), 0.3, 4.0, ((0, 8),))
    expand_weight = scatter_about(seeds[13], (D, MLP), D ** -0.5, 0.21875, ((0, 8),))
    expand_bias = scatter_about(seeds[14], (MLP,), 0.3, 4.0, ((0, 8),))
    reduce_weight = scatter_about(seeds[15], (MLP, D), MLP ** -0.5, 0.109375, ((0, 8),))
    reduce_bias = scatter_about(seeds[16], (D,), 0.3, 4.0, ((0, 8),))
    upsample_weight = scatter_about(seeds[17], (D, 8 * CDEC), D ** -0.5, 0.21875, ((0, 8),))
    kernel_first = scatter_about(seeds[18], (54 * CDEC, CDEC), (54 * CDEC) ** -0.5, 0.078125, ((0, 8),))
    kernel_second = scatter_about(seeds[19], (27 * CDEC, CDEC), (27 * CDEC) ** -0.5, 0.109375, ((0, 8),))
    residual_weight = scatter_about(seeds[20], (2 * CDEC, CDEC), (2 * CDEC) ** -0.5, 0.375, ((0, 8),))
    return dict(tokens=tokens, skip_features=skip_features, out_grad=out_grad, crop_lengths=crop_lengths, attend_gain=attend_gain, attend_shift=attend_shift, joint_weight=joint_weight, query_bias=query_bias, value_bias=value_bias, output_weight=output_weight, output_bias=output_bias, mixer_gain=mixer_gain, mixer_shift=mixer_shift, expand_weight=expand_weight, expand_bias=expand_bias, reduce_weight=reduce_weight, reduce_bias=reduce_bias, upsample_weight=upsample_weight, kernel_first=kernel_first, kernel_second=kernel_second, residual_weight=residual_weight)


@jax.custom_vjp
def low(v):
    return lax.optimization_barrier(v.astype(jnp.bfloat16)).astype(jnp.float32)

@jax.custom_vjp
def low_back(v):
    return v

def low_keep(v):
    return (low(v), None)

def low_pass(kept, grad):
    return (grad,)

def back_keep(v):
    return (v, None)

def back_low(kept, grad):
    return (low(grad),)
low.defvjp(low_keep, low_pass)
low_back.defvjp(back_keep, back_low)
PRECISE = lax.Precision.HIGHEST
EPS_LAYER = 1e-06
EPS_CROP = 1e-05

def exact_dot(first_arg, second_arg):
    return jnp.dot(first_arg, second_arg, precision=PRECISE)

def spread_rows(member, per_crop):
    return lax.dot_general(member, per_crop, (((0,), (0,)), ((), ())), precision=PRECISE)

def crops_of(lengths, indices):
    crop_ends = jnp.cumsum(lengths)
    return lax.optimization_barrier(jnp.sum((indices[:, None] >= crop_ends[None, :]).astype(jnp.int32), axis=1)).astype(jnp.int32)

def layer_norm(values, gain_vec, shift_vec):
    average = lax.optimization_barrier(jnp.mean(values, axis=-1, keepdims=True))
    centred = values - average
    inv_std = lax.rsqrt(lax.optimization_barrier(jnp.mean(centred * centred, axis=-1, keepdims=True)) + EPS_LAYER)
    return centred * inv_std * gain_vec + shift_vec

def gelu_exact(values):
    return jax.nn.gelu(values, approximate=False)

def planes(padded, keep_mask, layer_idx):
    depth_rows = keep_mask.shape[0]
    grid_high = padded.shape[1] - 2
    grid_wide = padded.shape[2] - 2
    slab_rows = padded[layer_idx:layer_idx + depth_rows] * keep_mask[:, None, None, None]
    pieces = [slab_rows[:, row_off:row_off + grid_high, col_off:col_off + grid_wide, :] for row_off in range(3) for col_off in range(3)]
    return jnp.concatenate(pieces, axis=-1).reshape(depth_rows * grid_high * grid_wide, -1)

def stencil(grid_field, keep_masks, weight):
    padded = jnp.pad(grid_field, ((1, 1), (1, 1), (1, 1), (0, 0)))
    block_len = weight.shape[0] // 3
    running = None
    for layer_idx in range(3):
        term = exact_dot(planes(padded, keep_masks[layer_idx], layer_idx), weight[layer_idx * block_len:(layer_idx + 1) * block_len])
        running = term if running is None else running + term
    return running

def crop_norm(values, member, counts):
    average = exact_dot(member, values) / counts
    centred = values - spread_rows(member, average)
    spread = exact_dot(member, centred * centred) / counts
    return centred * spread_rows(member, lax.rsqrt(spread + EPS_CROP))

def attend(queries, key_rows, value_rows, tok_crop):
    tok_total = queries.shape[0]
    head_dim = D // HEADS
    score_scale = 1.0 / math.sqrt(head_dim)
    block_len = math.gcd(tok_total, 512)
    key_heads = key_rows.reshape(tok_total, HEADS, head_dim)
    value_heads = value_rows.reshape(tok_total, HEADS, head_dim)

    def one_block(row_start):
        query_block = lax.dynamic_slice_in_dim(queries, row_start, block_len, 0).reshape(block_len, HEADS, head_dim)
        crop_block = lax.dynamic_slice_in_dim(tok_crop, row_start, block_len, 0)
        scores = low_back(jnp.einsum('the,lhe->htl', query_block, key_heads, precision=PRECISE) * score_scale)
        scores = jnp.where((crop_block[:, None] == tok_crop[None, :])[None], scores, -1000000000.0)
        probability = low(jax.nn.softmax(scores, axis=-1))
        return jnp.einsum('htl,lhe->the', probability, value_heads, precision=PRECISE).reshape(block_len, D)
    starts = jnp.arange(tok_total // block_len, dtype=jnp.int32) * block_len
    return lax.map(jax.checkpoint(one_block), starts).reshape(tok_total, D)

def forward(group_tokens, group_skip, lengths, params):
    gain_a, shift_a, joint_w, query_b, value_b, out_w, out_b, gain_m, shift_m, expand_w, expand_b, reduce_w, reduce_b, upsample_w, kernel_one, kernel_two, residual_w = params
    plane_size = PH * PH
    tok_total = group_tokens.shape[0]
    slices = tok_total // plane_size
    tok_crop = jnp.repeat(crops_of(lengths, jnp.arange(slices, dtype=jnp.int32)), plane_size)
    normed = low(layer_norm(group_tokens, gain_a, shift_a))
    joint_out = exact_dot(normed, joint_w)
    queries = low(low_back(joint_out[:, :D] + query_b))
    key_rows = low(low_back(joint_out[:, D:2 * D]))
    value_rows = low(low_back(joint_out[:, 2 * D:] + value_b))
    attended = low(low_back(attend(queries, key_rows, value_rows, tok_crop)))
    branch = low_back(exact_dot(attended, out_w) + out_b)
    middle = group_tokens + branch
    inner = low(layer_norm(middle, gain_m, shift_m))
    expanded = low_back(exact_dot(inner, expand_w) + expand_b)
    activated = low(gelu_exact(expanded))
    mixed_out = low_back(exact_dot(activated, reduce_w) + reduce_b)
    encoded = low(middle + mixed_out)
    up_rows = exact_dot(encoded, upsample_w).reshape(slices, PH, PH, 2, 2, 2, CDEC)
    upsampled = up_rows.transpose(0, 3, 1, 4, 2, 5, 6).reshape(2 * slices, 2 * PH, 2 * PH, CDEC)
    upsampled = low(low_back(upsampled))
    depth_rows = 2 * slices
    joined = jnp.concatenate([upsampled, group_skip.reshape(depth_rows, 2 * PH, 2 * PH, CDEC)], axis=-1)
    up_crop = crops_of(lengths, (jnp.arange(depth_rows + 2, dtype=jnp.int32) - 1) // 2)
    keep_masks = [(up_crop[layer_idx:layer_idx + depth_rows] == up_crop[1:1 + depth_rows]).astype(jnp.float32) for layer_idx in range(3)]
    pos_crop = jnp.repeat(up_crop[1:1 + depth_rows], 4 * plane_size)
    member = (jnp.arange(CROPS, dtype=jnp.int32)[:, None] == pos_crop[None, :]).astype(jnp.float32)
    counts = (lengths * 8 * plane_size).astype(jnp.float32)[:, None]
    first_conv = low_back(stencil(joined, keep_masks, kernel_one))
    act_one = low(gelu_exact(crop_norm(first_conv, member, counts)))
    second_conv = low_back(stencil(act_one.reshape(depth_rows, 2 * PH, 2 * PH, CDEC), keep_masks, kernel_two))
    residual = low_back(exact_dot(joined.reshape(-1, 2 * CDEC), residual_w))
    return gelu_exact(crop_norm(second_conv, member, counts) + residual)

def reference(tokens, skip_features, out_grad, crop_lengths, attend_gain, attend_shift, joint_weight, query_bias, value_bias, output_weight, output_bias, mixer_gain, mixer_shift, expand_weight, expand_bias, reduce_weight, reduce_bias, upsample_weight, kernel_first, kernel_second, residual_weight):
    params = tuple((weight.astype(jnp.float32) for weight in (attend_gain, attend_shift, joint_weight, query_bias, value_bias, output_weight, output_bias, mixer_gain, mixer_shift, expand_weight, expand_bias, reduce_weight, reduce_bias, upsample_weight, kernel_first, kernel_second, residual_weight)))

    def per_group(running, group_slice):
        group_tokens, group_skip, group_cot, lengths = group_slice

        def wrapped(tok_values, skip_values, weights):
            return forward(tok_values, skip_values, lengths, weights)
        outputs, pullback = jax.vjp(wrapped, group_tokens.astype(jnp.float32), group_skip.astype(jnp.float32), params)
        tok_grad, skip_part, weight_grads = pullback(group_cot.astype(jnp.float32))
        running = jax.tree.map(jnp.add, running, weight_grads)
        return (running, (outputs.astype(jnp.bfloat16), tok_grad, skip_part))
    zeros = jax.tree.map(jnp.zeros_like, params)
    grads, (decoded, tokens_grad, skip_grad) = lax.scan(per_group, zeros, (tokens, skip_features, out_grad, crop_lengths))
    return (decoded, tokens_grad, skip_grad, grads[0], grads[1], grads[2], grads[3], grads[4], grads[5], grads[6], grads[7], grads[8], grads[9], grads[10], grads[11], grads[12], grads[13], grads[14], grads[15], grads[16])
```

```python
import math

import jax
import jax.numpy as jnp
from jax import lax
from jax.sharding import PartitionSpec as P

HEADS = 12
PH = 4
CROPS = 4


PRECISE = lax.Precision.HIGHEST
EPS_LAYER = 1e-06
EPS_CROP = 1e-05
BF = jnp.bfloat16
F32 = jnp.float32


def exact_dot(first_arg, second_arg):
    return jnp.dot(first_arg, second_arg, precision=PRECISE)


def bf_dot(first_arg, second_arg):
    return jnp.dot(first_arg, second_arg, preferred_element_type=F32)


def cross_dot(first_arg, second_arg):
    return lax.dot_general(
        first_arg, second_arg, (((0,), (0,)), ((), ())), preferred_element_type=F32
    )


def back_dot(first_arg, second_arg):
    return lax.dot_general(
        first_arg, second_arg, (((1,), (1,)), ((), ())), preferred_element_type=F32
    )


def spread_rows(member, per_crop):
    return lax.dot_general(member, per_crop, (((0,), (0,)), ((), ())), precision=PRECISE)


def crops_of(lengths, indices):
    crop_ends = jnp.cumsum(lengths)
    return jnp.sum((indices[:, None] >= crop_ends[None, :]).astype(jnp.int32), axis=1)


def layer_norm(values, gain_vec, shift_vec):
    average = jnp.mean(values, axis=-1, keepdims=True)
    centred = values - average
    inv_std = lax.rsqrt(jnp.mean(centred * centred, axis=-1, keepdims=True) + EPS_LAYER)
    unit_rows = centred * inv_std
    return (unit_rows * gain_vec + shift_vec, unit_rows, inv_std)


def layer_back(upstream, unit_rows, inv_std, gain_vec):
    scaled = upstream * gain_vec
    return inv_std * (
        scaled
        - jnp.mean(scaled, axis=-1, keepdims=True)
        - unit_rows * jnp.mean(scaled * unit_rows, axis=-1, keepdims=True)
    )


def gelu_exact(values):
    return jax.nn.gelu(values, approximate=False)


def gelu_back(values, upstream):
    return jax.vjp(gelu_exact, values)[1](upstream)[0]


def swap(values, axis, mask):
    count = lax.axis_size(axis)
    return lax.ppermute(values, axis, [(i, i ^ mask) for i in range(count)])


def gather_rel(values, axis, stride, count):
    return jnp.stack([values] + [swap(values, axis, m * stride) for m in range(1, count)])


def pick(blocks, index):
    return lax.dynamic_index_in_dim(blocks, index, 0, keepdims=False)


def unxor(blocks, index):
    count = blocks.shape[0]
    bits = count.bit_length() - 1
    tail = blocks.shape[1:]
    cube = blocks.reshape((2,) * bits + tail)
    for bit in range(bits):
        dim = bits - 1 - bit
        cube = jnp.where(((index >> bit) & 1) == 1, jnp.flip(cube, dim), cube)
    return cube.reshape(blocks.shape)


def deal_rel(blocks, axis, stride, index):
    count = blocks.shape[0]
    return [pick(blocks, index)] + [
        swap(pick(blocks, index ^ m), axis, m * stride) for m in range(1, count)
    ]


def sum_list(parts):
    total = parts[0].astype(F32)
    for part in parts[1:]:
        total = total + part.astype(F32)
    return total


def batch_sum(values):
    count = lax.axis_size("batch")
    if count == 1:
        return values.astype(F32)
    index = lax.axis_index("batch")
    rows = values.shape[0]
    piece = -(-rows // count)
    if piece * count > rows:
        values = jnp.pad(values, ((0, piece * count - rows), (0, 0)))
    pieces = values.reshape((count, piece) + values.shape[1:])
    own = sum_list(deal_rel(pieces, "batch", 1, index)).astype(BF)
    total = unxor(gather_rel(own, "batch", 1, count), index)
    return total.reshape(values.shape)[:rows].astype(F32)


def with_rims(grid_field):
    count = lax.axis_size("seq")
    ends = count - 1
    head = grid_field[:1]
    tail = grid_field[-1:]
    extended = jnp.concatenate(
        [
            lax.ppermute(tail, "seq", [(i, (i + 1) % count) for i in range(ends)]),
            grid_field,
            lax.ppermute(head, "seq", [((i + 1) % count, i) for i in range(ends)]),
        ],
        axis=0,
    )
    return jnp.pad(extended, ((0, 0), (1, 1), (1, 1), (0, 0)))


def planes(padded, keep_mask, layer_idx):
    depth_rows = keep_mask.shape[0]
    grid_high = padded.shape[1] - 2
    grid_wide = padded.shape[2] - 2
    slab_rows = padded[layer_idx : layer_idx + depth_rows] * keep_mask[:, None, None, None]
    pieces = [
        slab_rows[:, row_off : row_off + grid_high, col_off : col_off + grid_wide, :]
        for row_off in range(3)
        for col_off in range(3)
    ]
    return jnp.concatenate(pieces, axis=-1).reshape(depth_rows * grid_high * grid_wide, -1)


def forward_taps(weight):
    block_len = weight.shape[0] // 3
    return [weight[layer_idx * block_len : (layer_idx + 1) * block_len] for layer_idx in range(3)]


def backward_taps(weight, in_chans):
    cube = weight.reshape(3, 3, 3, in_chans, weight.shape[1])[::-1, ::-1, ::-1]
    turned = jnp.swapaxes(cube, 3, 4)
    return [turned[layer_idx].reshape(9 * weight.shape[1], in_chans) for layer_idx in range(3)]


def stencil(padded, keep_masks, matrices):
    running = None
    for layer_idx in range(3):
        term = bf_dot(planes(padded, keep_masks[layer_idx], layer_idx), matrices[layer_idx])
        running = term if running is None else running + term
    return running


def weight_grad(padded, keep_masks, upstream):
    return jnp.concatenate(
        [
            cross_dot(planes(padded, keep_masks[layer_idx], layer_idx), upstream)
            for layer_idx in range(3)
        ],
        axis=0,
    )


def on_device(
    tokens,
    skip_features,
    out_grad,
    crop_lengths,
    attend_gain,
    attend_shift,
    joint_weight,
    query_bias,
    value_bias,
    output_weight,
    output_bias,
    mixer_gain,
    mixer_shift,
    expand_weight,
    expand_bias,
    reduce_weight,
    reduce_bias,
    upsample_weight,
    kernel_first,
    kernel_second,
    residual_weight,
):
    count = lax.axis_size("seq")
    high = math.gcd(HEADS, count)
    low = count // high
    seq_index = lax.axis_index("seq")
    hi = seq_index // low
    lo = seq_index % low
    width = tokens.shape[2]
    shard = joint_weight.shape[0]
    head_dim = width // HEADS
    heads = HEADS // high
    span = heads * head_dim
    hidden = expand_weight.shape[1]
    hid_span = hidden // high
    hid_shard = hidden // count
    channels = residual_weight.shape[1]
    score_scale = 1.0 / math.sqrt(head_dim)
    plane_size = PH * PH
    tok_rows = tokens.shape[1]
    rows = high * tok_rows
    slices = tok_rows // plane_size
    depth_rows = 2 * slices
    positions = depth_rows * 4 * plane_size
    lengths = crop_lengths[0]

    def plane_gather(values):
        return gather_rel(values, "seq", low, high)

    def plane_deal(blocks):
        return deal_rel(blocks, "seq", low, hi)

    def chip_gather(values):
        return gather_rel(values, "seq", 1, low)

    def chip_sum(blocks):
        return sum_list(deal_rel(blocks, "seq", 1, lo)).astype(BF)

    def plane_sum(blocks):
        return sum_list(
            [blocks[0]] + [swap(blocks[m].astype(BF), "seq", m * low) for m in range(1, high)]
        )

    def all_gather(values):
        return lax.all_gather(values, "seq", axis=0, tiled=True)

    def owners(rel_hi, rel_lo):
        return (hi ^ rel_hi) * low + (lo ^ rel_lo)

    gathered_tokens = plane_gather(tokens[0]).reshape(rows, width)
    vec_own = jnp.concatenate(
        [
            jnp.stack(
                [
                    attend_gain,
                    attend_shift,
                    query_bias,
                    value_bias,
                    output_bias,
                    mixer_gain,
                    mixer_shift,
                    reduce_bias,
                ]
            ),
            expand_bias.reshape(hid_shard // shard, shard),
        ],
        axis=0,
    )
    vec_rel = chip_gather(plane_gather(vec_own))
    vec_abs = unxor(jnp.swapaxes(unxor(vec_rel, lo), 0, 1), hi).reshape(count, -1, shard)
    vecs = vec_abs.astype(F32).transpose(1, 0, 2)
    flat = vecs[:8].reshape(8, width)
    gain_a, shift_a, query_b, value_b, out_b, gain_m, shift_m, reduce_b = [
        flat[j] for j in range(8)
    ]
    expand_b = vec_abs[:, 8:].astype(F32).reshape(hidden)

    def own_span(vector, length):
        return lax.dynamic_slice_in_dim(vector, hi * length, length)

    def columns_for(weight, parts):
        per = weight.shape[1] // (parts * high)
        cut = weight.reshape(shard, parts, high, per).transpose(2, 0, 1, 3)
        cut = cut.reshape(high, shard, parts * per)
        rel = chip_gather(jnp.stack(plane_deal(cut)))
        natural = unxor(jnp.swapaxes(unxor(rel, lo), 0, 1), hi)
        return natural.reshape(width, parts * per)

    joint_w = columns_for(joint_weight, 3)
    out_rel = unxor(chip_gather(plane_gather(output_weight)), lo)
    out_w = jnp.swapaxes(out_rel, 0, 1).reshape(width, width)
    expand_w = columns_for(expand_weight, 1)
    reduce_w = unxor(chip_gather(reduce_weight), lo).reshape(hid_span, width)
    upsample_w = all_gather(upsample_weight)
    conv_shards = jnp.concatenate([kernel_first, kernel_second, residual_weight], axis=0)
    conv_all = lax.all_gather(conv_shards, "seq", axis=0)
    cut_one = kernel_first.shape[0]
    cut_two = cut_one + kernel_second.shape[0]
    kernel_one = conv_all[:, :cut_one].reshape(-1, channels)
    kernel_two = conv_all[:, cut_one:cut_two].reshape(-1, channels)
    residual_w = conv_all[:, cut_two:].reshape(-1, channels)

    def token_crops(rel_lo):
        starts = jnp.stack([owners(m, rel_lo) for m in range(high)]) * slices
        ids = starts[:, None] + jnp.arange(slices, dtype=jnp.int32)[None, :]
        return jnp.repeat(crops_of(lengths, ids.reshape(-1)), plane_size)

    own_crop = token_crops(0)
    all_crop = jnp.concatenate([token_crops(s) for s in range(low)])
    same_crop = (own_crop[:, None] == all_crop[None, :])[None]

    def split_heads(row_block):
        return row_block.reshape(row_block.shape[0], heads, head_dim)

    normed_a, unit_a, inv_a = layer_norm(gathered_tokens.astype(F32), gain_a, shift_a)
    normed_low = normed_a.astype(BF)
    joint_out = bf_dot(normed_low, joint_w)
    queries = (joint_out[:, :span] + own_span(query_b, span)).astype(BF)
    key_rows = joint_out[:, span : 2 * span].astype(BF)
    value_rows = (joint_out[:, 2 * span :] + own_span(value_b, span)).astype(BF)
    kv_all = chip_gather(jnp.concatenate([key_rows, value_rows], axis=1))
    kv_all = kv_all.reshape(low * rows, 2 * span)
    key_heads = split_heads(kv_all[:, :span])
    value_heads = split_heads(kv_all[:, span:])
    query_heads = split_heads(queries)
    scores = (
        jnp.einsum("the,lhe->htl", query_heads, key_heads, preferred_element_type=F32)
        * score_scale
    )
    masked = jnp.where(same_crop, scores, -1000000000.0)
    highest = jnp.max(masked, axis=-1, keepdims=True)
    exp_scores = jnp.exp(masked - highest)
    totals = jnp.sum(exp_scores, axis=-1, keepdims=True)
    log_total = highest + jnp.log(totals)
    probability = (exp_scores / totals).astype(BF)
    attended = (
        jnp.einsum("htl,lhe->the", probability, value_heads, preferred_element_type=F32)
        .reshape(rows, span)
        .astype(BF)
    )
    att_blocks = attended.reshape(high, tok_rows, span)
    att_rel = [att_blocks[0]] + [swap(att_blocks[m], "seq", m * low) for m in range(1, high)]
    inputs = tokens[0].astype(F32)
    middle = inputs + bf_dot(jnp.concatenate(att_rel, axis=1), out_w) + out_b
    normed_m, unit_m, inv_m = layer_norm(middle, gain_m, shift_m)
    inner_low = plane_gather(normed_m.astype(BF)).reshape(rows, width)
    expanded = bf_dot(inner_low, expand_w) + own_span(expand_b, hid_span)
    activated = gelu_exact(expanded).astype(BF)
    mixed_part = bf_dot(activated, reduce_w).reshape(high, tok_rows, width)
    encoded = (middle + plane_sum(mixed_part) + reduce_b).astype(BF)
    up_rows = bf_dot(encoded, upsample_w).reshape(slices, PH, PH, 2, 2, 2, channels)
    upsampled = (
        up_rows.transpose(0, 3, 1, 4, 2, 5, 6)
        .reshape(depth_rows, 2 * PH, 2 * PH, channels)
        .astype(BF)
    )

    joined = jnp.concatenate(
        [upsampled, skip_features[0].reshape(depth_rows, 2 * PH, 2 * PH, channels)], axis=-1
    )
    up_index = seq_index * depth_rows - 1 + jnp.arange(depth_rows + 2, dtype=jnp.int32)
    up_crop = crops_of(lengths, up_index // 2)
    keep_masks = [
        (up_crop[layer_idx : layer_idx + depth_rows] == up_crop[1 : 1 + depth_rows]).astype(BF)
        for layer_idx in range(3)
    ]
    pos_crop = jnp.repeat(up_crop[1 : 1 + depth_rows], 4 * plane_size)
    member = (jnp.arange(CROPS, dtype=jnp.int32)[:, None] == pos_crop[None, :]).astype(F32)
    counts = (lengths * 8 * plane_size).astype(F32)[:, None]

    crop_ends = jnp.cumsum(lengths)
    dev_rel = jnp.stack([owners(m, s) for s in range(low) for m in range(high)])
    first = (dev_rel * slices)[:, None]
    shared = jnp.minimum(crop_ends[None], first + slices) - jnp.maximum(
        (crop_ends - lengths)[None], first
    )
    dev_counts = (jnp.maximum(shared, 0) * 8 * plane_size).astype(F32)[:, :, None]
    own_counts = dev_counts[0]

    def stat_gather(first_part, second_part):
        pair = jnp.concatenate([first_part, second_part], axis=0)
        return chip_gather(plane_gather(pair)).reshape(count, 2, CROPS, -1)

    def crop_norm(values):
        local_sum = exact_dot(member, values)
        local_mean = local_sum / jnp.maximum(own_counts, 1.0)
        about = values - spread_rows(member, local_mean)
        local_dev = exact_dot(member, about * about)
        both = stat_gather(local_sum, local_dev)
        average = jnp.sum(both[:, 0], axis=0) / counts
        off = both[:, 0] / jnp.maximum(dev_counts, 1.0) - average
        spread = jnp.sum(both[:, 1] + dev_counts * off * off, axis=0) / counts
        inv_rows = spread_rows(member, lax.rsqrt(spread + EPS_CROP))
        return ((values - spread_rows(member, average)) * inv_rows, inv_rows)

    def crop_backnorm(upstream, unit_rows, inv_rows):
        both = stat_gather(exact_dot(member, upstream), exact_dot(member, upstream * unit_rows))
        sums = jnp.sum(both, axis=0) / counts
        return inv_rows * (
            upstream - spread_rows(member, sums[0]) - unit_rows * spread_rows(member, sums[1])
        )

    joined_rim = with_rims(joined)
    first_conv = stencil(joined_rim, keep_masks, forward_taps(kernel_one))
    first_unit, first_inv = crop_norm(first_conv)
    act_one = gelu_exact(first_unit).astype(BF)
    act_rim = with_rims(act_one.reshape(depth_rows, 2 * PH, 2 * PH, channels))
    second_conv = stencil(act_rim, keep_masks, forward_taps(kernel_two))
    second_unit, second_inv = crop_norm(second_conv)
    joined_rows = joined.reshape(positions, 2 * channels)
    summed = second_unit + bf_dot(joined_rows, residual_w)
    decoded = gelu_exact(summed).astype(BF)
    grad_summed = gelu_back(summed, out_grad[0].astype(F32))
    grad_resid = grad_summed.astype(BF)
    grad_second = crop_backnorm(grad_summed, second_unit, second_inv).astype(BF)
    residual_grad = cross_dot(joined_rows, grad_resid)
    second_rim = with_rims(grad_second.reshape(depth_rows, 2 * PH, 2 * PH, channels))
    kernel_two_grad = weight_grad(act_rim, keep_masks, grad_second)
    grad_act = stencil(second_rim, keep_masks, backward_taps(kernel_two, channels))
    grad_first = crop_backnorm(gelu_back(first_unit, grad_act), first_unit, first_inv).astype(BF)
    kernel_one_grad = weight_grad(joined_rim, keep_masks, grad_first)
    first_rim = with_rims(grad_first.reshape(depth_rows, 2 * PH, 2 * PH, channels))
    grad_joined = stencil(
        first_rim, keep_masks, backward_taps(kernel_one, 2 * channels)
    ) + back_dot(grad_resid, residual_w)
    skip_grad = grad_joined[:, channels:]
    grad_up = grad_joined[:, :channels].astype(BF).reshape(slices, 2, PH, 2, PH, 2, channels)
    grad_up_rows = grad_up.transpose(0, 2, 4, 1, 3, 5, 6).reshape(tok_rows, 8 * channels)

    def shard_sum(partial):
        blocks = partial.astype(BF).reshape((high, low, -1) + partial.shape[1:])
        own = chip_sum(jnp.swapaxes(blocks, 0, 1))
        return sum_list(plane_deal(own)).astype(BF)

    conv_part = jnp.concatenate(
        [
            kernel_one_grad.astype(BF).reshape(count, -1, channels),
            kernel_two_grad.astype(BF).reshape(count, -1, channels),
            residual_grad.astype(BF).reshape(count, -1, channels),
        ],
        axis=1,
    )
    conv_sum = batch_sum(shard_sum(conv_part.reshape(-1, channels)))
    upsample_grad = batch_sum(shard_sum(cross_dot(encoded, grad_up_rows)))
    grad_encoded = back_dot(grad_up_rows, upsample_w)
    own_mixed = grad_encoded.astype(BF)
    grad_mixed = plane_gather(own_mixed).reshape(rows, width)
    reduce_bias_grad = jnp.sum(own_mixed.astype(F32), axis=0)
    reduce_part = cross_dot(activated, grad_mixed).astype(BF).reshape(low, hid_shard, width)
    reduce_grad = batch_sum(chip_sum(reduce_part))
    grad_expanded = gelu_back(expanded, back_dot(grad_mixed, reduce_w)).astype(BF)

    def column_grad(partial, parts):
        blocks = partial.astype(BF).reshape(high, low, shard, -1)
        own = chip_sum(jnp.swapaxes(blocks, 0, 1))
        cols = unxor(jnp.stack(plane_deal(own)), hi)
        cols = cols.reshape(high, shard, parts, -1).transpose(1, 2, 0, 3)
        return cols.reshape(shard, -1)

    expand_grad = batch_sum(column_grad(cross_dot(inner_low, grad_expanded), 1))
    expand_bias_part = jnp.sum(grad_expanded.astype(F32), axis=0).astype(BF)
    inner_part = back_dot(grad_expanded, expand_w).reshape(high, tok_rows, width)
    grad_inner = plane_sum(inner_part)
    mixer_gain_grad = jnp.sum(grad_inner * unit_m, axis=0)
    mixer_shift_grad = jnp.sum(grad_inner, axis=0)
    grad_middle = grad_encoded + layer_back(grad_inner, unit_m, inv_m, gain_m)
    own_branch = grad_middle.astype(BF)
    grad_branch = plane_gather(own_branch).reshape(rows, width)
    output_bias_grad = jnp.sum(own_branch.astype(F32), axis=0)
    output_part = cross_dot(attended, grad_branch).astype(BF).reshape(low, shard, width)
    output_grad = batch_sum(chip_sum(output_part))
    own_out_w = out_w[:span]
    grad_attended = back_dot(grad_branch, own_out_w).astype(BF)
    again_scores = (
        jnp.einsum("the,lhe->htl", query_heads, key_heads, preferred_element_type=F32)
        * score_scale
    )
    again_prob = jnp.exp(jnp.where(same_crop, again_scores, -1000000000.0) - log_total)
    attended_heads = split_heads(grad_attended)
    grad_weights = jnp.einsum(
        "the,lhe->htl", attended_heads, value_heads, preferred_element_type=F32
    )
    inner_sum = jnp.sum(again_prob * grad_weights, axis=-1, keepdims=True)
    grad_scores = (again_prob * (grad_weights - inner_sum)).astype(BF)
    grad_queries = (
        (
            jnp.einsum("htl,lhe->the", grad_scores, key_heads, preferred_element_type=F32)
            * score_scale
        )
        .reshape(rows, span)
        .astype(BF)
    )
    prob_low = again_prob.astype(BF)
    key_part = (
        jnp.einsum("htl,the->lhe", grad_scores, query_heads, preferred_element_type=F32)
        * score_scale
    )
    value_part = jnp.einsum("htl,the->lhe", prob_low, attended_heads, preferred_element_type=F32)
    kv_part = jnp.concatenate(
        [key_part.reshape(low, rows, span), value_part.reshape(low, rows, span)], axis=2
    )
    kv_grad = sum_list(
        [kv_part[0]] + [swap(kv_part[s].astype(BF), "seq", s) for s in range(1, low)]
    ).astype(BF)
    grad_joint = jnp.concatenate([grad_queries, kv_grad], axis=1)
    joint_part = column_grad(cross_dot(normed_low, grad_joint), 3)
    joint_grad = batch_sum(joint_part)
    normed_part = back_dot(grad_joint, joint_w)
    attend_gain_grad = jnp.sum(normed_part * unit_a, axis=0)
    attend_shift_grad = jnp.sum(normed_part, axis=0)
    grad_normed = plane_sum(normed_part.reshape(high, tok_rows, width))
    tokens_grad = grad_middle + layer_back(grad_normed, unit_a[:tok_rows], inv_a[:tok_rows], gain_a)

    joint_bias = jnp.sum(grad_joint.astype(F32), axis=0)
    whole = jnp.stack(
        [
            attend_gain_grad,
            attend_shift_grad,
            output_bias_grad,
            mixer_gain_grad,
            mixer_shift_grad,
            reduce_bias_grad,
        ]
    )
    whole = whole.astype(BF).reshape(6, count, shard).transpose(1, 0, 2).reshape(count, -1)
    whole = sum_list(
        plane_deal(chip_sum(jnp.swapaxes(whole.reshape(high, low, -1), 0, 1)))
    ).astype(BF)
    part = chip_sum(
        jnp.concatenate(
            [
                joint_bias[:span].astype(BF).reshape(low, shard),
                joint_bias[2 * span :].astype(BF).reshape(low, shard),
                expand_bias_part.reshape(low, hid_shard),
            ],
            axis=1,
        )
    )
    vec_sum = jnp.concatenate([whole, part])
    nb = lax.axis_size("batch")
    vec_sum = sum_list([vec_sum] + [swap(vec_sum, "batch", m) for m in range(1, nb)])
    six = vec_sum[: 6 * shard].reshape(6, shard)
    rest = vec_sum[6 * shard :]
    return (
        decoded[None],
        tokens_grad[None],
        skip_grad[None],
        six[0],
        six[1],
        joint_grad,
        rest[:shard],
        rest[shard : 2 * shard],
        output_grad,
        six[2],
        six[3],
        six[4],
        expand_grad,
        rest[2 * shard :],
        reduce_grad,
        six[5],
        upsample_grad,
        conv_sum[:cut_one],
        conv_sum[cut_one:cut_two],
        conv_sum[cut_two:],
    )


def solution(mesh):
    rows = P("batch", "seq", None)
    vec = P("seq")
    mat = P("seq", None)
    in_specs = (rows, rows, rows, P("batch", None))
    in_specs += (vec, vec, mat, vec, vec, mat, vec, vec, vec, mat, vec, mat, vec)
    in_specs += (mat, mat, mat, mat)
    out_specs = (rows, rows, rows)
    out_specs += (vec, vec, mat, vec, vec, mat, vec, vec, vec, mat, vec, mat, vec)
    out_specs += (mat, mat, mat, mat)
    return jax.shard_map(
        on_device, mesh=mesh, in_specs=in_specs, out_specs=out_specs, check_vma=False
    )
```

```python
import functools
import math

import jax
import jax.numpy as jnp
from jax import lax
from jax.experimental import pallas as pl
from jax.experimental.pallas import tpu as pltpu
from jax.sharding import PartitionSpec as P

HEADS = 12
PH = 4
CROPS = 4


LIMITS = {
    "attend_back_kernel": 30,
    "attend_kernel": 22,
    "tap_grad_kernel": 18,
    "joint_back_kernel": 16,
}
EPS_LAYER = 1e-06
EPS_CROP = 1e-05
BF = jnp.bfloat16
F32 = jnp.float32


def crops_of(lengths, indices):
    crop_ends = jnp.cumsum(lengths)
    return jnp.sum((indices[:, None] >= crop_ends[None, :]).astype(jnp.int32), axis=1)


def swap(values, axis, mask):
    count = lax.axis_size(axis)
    return lax.ppermute(values, axis, [(i, i ^ mask) for i in range(count)])


def gather_rel(values, axis, stride, count):
    return jnp.stack([values] + [swap(values, axis, m * stride) for m in range(1, count)])


def pick(blocks, index):
    return lax.dynamic_index_in_dim(blocks, index, 0, keepdims=False)


def unxor(blocks, index):
    count = blocks.shape[0]
    bits = count.bit_length() - 1
    tail = blocks.shape[1:]
    cube = blocks.reshape((2,) * bits + tail)
    for bit in range(bits):
        dim = bits - 1 - bit
        cube = jnp.where(((index >> bit) & 1) == 1, jnp.flip(cube, dim), cube)
    return cube.reshape(blocks.shape)


def deal_rel(blocks, axis, stride, index):
    count = blocks.shape[0]
    return [pick(blocks, index)] + [
        swap(pick(blocks, index ^ m), axis, m * stride) for m in range(1, count)
    ]


def sum_list(parts):
    total = parts[0].astype(F32)
    for part in parts[1:]:
        total = total + part.astype(F32)
    return total


def batch_sum(values):
    count = lax.axis_size("batch")
    if count == 1:
        return values.astype(F32)
    index = lax.axis_index("batch")
    rows = values.shape[0]
    piece = -(-rows // count)
    if piece * count > rows:
        values = jnp.pad(values, ((0, piece * count - rows), (0, 0)))
    pieces = values.reshape((count, piece) + values.shape[1:])
    own = sum_list(deal_rel(pieces, "batch", 1, index)).astype(BF)
    total = unxor(gather_rel(own, "batch", 1, count), index)
    return total.reshape(values.shape)[:rows].astype(F32)


def call(kernel, outs, scratch, *args, smem=0):
    name = getattr(kernel, "func", kernel).__name__
    limit = LIMITS.get(name, 12)
    return pl.pallas_call(
        kernel,
        out_shape=tuple(jax.ShapeDtypeStruct(shape, kind) for shape, kind in outs),
        in_specs=[pl.BlockSpec(memory_space=pltpu.SMEM)] * smem
        + [pl.BlockSpec(memory_space=pltpu.VMEM)] * (len(args) - smem),
        scratch_shapes=[pltpu.VMEM(shape, kind) for shape, kind in scratch],
        compiler_params=pltpu.CompilerParams(vmem_limit_bytes=limit * 1024 * 1024),
        name=name,
    )(*args)


GRID = 2 * PH
CELLS = GRID * GRID
ERF_TOP = (
    0.00022905065861350646,
    0.0034082910107109506,
    0.050955695062380861,
    0.18520832239976145,
    1.128379143519084,
)
ERF_LOW = (
    -1.1791602954361697e-7,
    0.000023547966471313185,
    0.0010179625278914885,
    0.014070470171167667,
    0.11098505178285362,
    0.49746925110067538,
    1.0,
)


def normal_cdf(values):
    arg = jnp.clip(values * math.sqrt(0.5), -3.832506856900711, 3.832506856900711)
    square = arg * arg
    top = jnp.full_like(square, ERF_TOP[0])
    for coef in ERF_TOP[1:]:
        top = top * square + coef
    bottom = jnp.full_like(square, ERF_LOW[0])
    for coef in ERF_LOW[1:]:
        bottom = bottom * square + coef
    return 0.5 + 0.5 * (arg * top / bottom)


def gelu_slope(values, cdf):
    return cdf + values * (jnp.exp(-0.5 * values * values) * (1.0 / math.sqrt(2.0 * math.pi)))


def depth_shifts(cells, prev, following, up, down):
    half = cells.shape[1] // 2
    even, odd = cells[:, :half], cells[:, half:]
    row = lax.broadcasted_iota(jnp.int32, even.shape, 1)
    ahead = jnp.where(row == half - 1, following[:, None, :], pltpu.roll(even, half - 1, 1))
    behind = jnp.where(row == 0, prev[:, None, :], pltpu.roll(odd, 1, 1))
    return (
        jnp.concatenate([behind * down[None], even], axis=1),
        jnp.concatenate([odd, ahead * up[None]], axis=1),
    )


def flat_rows(cells):
    return cells.reshape(cells.shape[0] * cells.shape[1], cells.shape[2])


def deep(rows):
    return rows.reshape(CELLS, rows.shape[0] // CELLS, rows.shape[1])


def tap_add(acc_ref, field, tap, sign):
    step_i, step_j = sign * (tap // 3 - 1), sign * (tap % 3 - 1)
    depth = acc_ref.shape[2]
    field = field.reshape(GRID, GRID, depth, field.shape[1])
    low_i, high_i = max(0, -step_i), GRID - max(0, step_i)
    low_j, high_j = max(0, -step_j), GRID - max(0, step_j)
    acc_ref[low_i:high_i, low_j:high_j] += field[
        low_i + step_i : high_i + step_i, low_j + step_j : high_j + step_j
    ]


def conv_into(acc_ref, stack, weight_ref, in_chans):
    taps = [4, 0, 1, 2, 3, 5, 6, 7, 8]

    def matrix(tap):
        return jnp.concatenate(
            [
                weight_ref[(layer * 9 + tap) * in_chans : (layer * 9 + tap + 1) * in_chans, :]
                for layer in range(3)
            ],
            axis=0,
        )

    out = weight_ref.shape[1]
    acc_ref[...] = jnp.zeros_like(acc_ref)
    for start in range(0, 9, 2):
        pair = taps[start : start + 2]
        rhs = jnp.concatenate([matrix(tap) for tap in pair], axis=1)
        field = jnp.dot(stack, rhs, preferred_element_type=F32)
        for place, tap in enumerate(pair):
            tap_add(acc_ref, field[:, place * out : (place + 1) * out], tap, 1)


def turned_into(acc_ref, stack, weight_ref, in_chans):
    taps = [4, 0, 1, 2, 3, 5, 6, 7, 8]

    def matrix(tap):
        return jnp.concatenate(
            [
                weight_ref[(layer * 9 + tap) * in_chans : (layer * 9 + tap + 1) * in_chans, :]
                for layer in (2, 1, 0)
            ],
            axis=1,
        )

    acc_ref[...] = jnp.zeros_like(acc_ref)
    step = max(1, 256 // in_chans)
    for start in range(0, 9, step):
        pair = taps[start : start + step]
        rhs = jnp.concatenate([matrix(tap) for tap in pair], axis=0)
        field = lax.dot_general(
            stack, rhs, (((1,), (1,)), ((), ())), preferred_element_type=F32
        )
        for place, tap in enumerate(pair):
            tap_add(acc_ref, field[:, place * in_chans : (place + 1) * in_chans], tap, -1)


def send_slabs(values_ref, parity, even_ref, odd_ref):
    depth = values_ref.shape[0] // CELLS
    top = values_ref[pl.ds(depth - 1, CELLS, stride=depth), :]
    bottom = values_ref[pl.ds(0, CELLS, stride=depth), :]
    even_ref[...] = jnp.where(parity == 0, top, bottom)
    odd_ref[...] = jnp.where(parity == 0, bottom, top)


def place_slabs(parity, from_even, from_odd):
    return (
        jnp.where(parity == 0, from_odd, from_even),
        jnp.where(parity == 0, from_even, from_odd),
    )


def spread(onehot_ref, per_crop):
    total = onehot_ref[0] * per_crop[0:1]
    for crop in range(1, CROPS):
        total = total + onehot_ref[crop] * per_crop[crop : crop + 1]
    return total


def crop_fold(onehot_ref, per_depth):
    return [
        jnp.sum(onehot_ref[crop] * per_depth, axis=0, keepdims=True) for crop in range(CROPS)
    ]


def moment_tile(onehot_ref, count_ref, cells, tile_ref):
    per_slice = float(cells.shape[0])
    sums = jnp.sum(cells, axis=0)
    about = cells - (sums * (1.0 / per_slice))[None]
    devs = jnp.sum(about * about, axis=0)
    totals = crop_fold(onehot_ref, sums)
    for crop in range(CROPS):
        mean = totals[crop] / jnp.maximum(count_ref[0, crop : crop + 1], 1.0)
        off = sums * (1.0 / per_slice) - mean
        tile_ref[crop : crop + 1] = totals[crop]
        tile_ref[CROPS + crop : CROPS + crop + 1] = jnp.sum(
            onehot_ref[crop] * (devs + per_slice * off * off), axis=0, keepdims=True
        )


def sum_tile(onehot_ref, first, second, tile_ref):
    for start, field in ((0, first), (CROPS, second)):
        totals = crop_fold(onehot_ref, jnp.sum(field, axis=0))
        for crop in range(CROPS):
            tile_ref[start + crop : start + crop + 1] = totals[crop]


def tile_list(tile_refs, high):
    tiles = [ref[...] for ref in tile_refs[:high]]
    for ref in tile_refs[high:]:
        tiles += [ref[8 * m : 8 * m + 8, :] for m in range(high)]
    return tiles


def merged_moments(tiles, count_ref, total_ref):
    total = total_ref[...]
    sums = tiles[0][:CROPS]
    devs = tiles[0][CROPS:]
    for tile in tiles[1:]:
        sums = sums + tile[:CROPS]
        devs = devs + tile[CROPS:]
    mean = sums / total
    for place, tile in enumerate(tiles):
        held = count_ref[place]
        off = tile[:CROPS] / jnp.maximum(held, 1.0) - mean
        devs = devs + held * off * off
    return mean, lax.rsqrt(devs / total + EPS_CROP)


def merged_sums(tiles, total_ref):
    both = tiles[0]
    for tile in tiles[1:]:
        both = both + tile
    total = total_ref[...]
    return both[:CROPS] / total, both[CROPS:] / total


def stack_rows(cells, prev, following, up, down):
    behind, ahead = depth_shifts(cells, prev, following, up, down)
    return [flat_rows(part).astype(BF) for part in (behind, cells, ahead)]


def up_kernel(
    high, slices, info, middle_ref, vec_ref, weight_ref, top_ref, bottom_ref, *refs
):
    parts, (enc_ref, up_ref, even_ref, odd_ref, grid_ref) = refs[:high], refs[high:]
    encoded = (middle_ref[...] + plane_total(parts) + vec_ref[7:8, :]).astype(BF)
    enc_ref[...] = encoded
    tok_rows = encoded.shape[0]
    plane = tok_rows // slices
    chans = up_ref.shape[1]
    ordered = jnp.dot(
        token_order(tok_rows, slices, False), encoded, preferred_element_type=F32
    ).astype(BF)
    rows = jnp.dot(ordered, weight_ref[...], preferred_element_type=F32)
    depth = 2 * slices
    for cell in range(plane):
        for place in range(8):
            part_a, part_b, part_e = place // 4, (place // 2) % 2, place % 2
            at = (2 * (cell // PH) + part_b) * GRID + 2 * (cell % PH) + part_e
            grid_ref[at * depth + part_a * slices : at * depth + (part_a + 1) * slices, :] = rows[
                cell * slices : (cell + 1) * slices, place * chans : (place + 1) * chans
            ]
    parity = info[0]
    top = grid_ref[pl.ds(depth - 1, CELLS, stride=depth), :]
    bottom = grid_ref[pl.ds(0, CELLS, stride=depth), :]
    even_ref[:, :chans] = jnp.where(parity == 0, top, bottom).astype(BF)
    odd_ref[:, :chans] = jnp.where(parity == 0, bottom, top).astype(BF)

    @pl.when(parity == 0)
    def _():
        even_ref[:, chans:] = top_ref[...]
        odd_ref[:, chans:] = bottom_ref[...]

    @pl.when(parity != 0)
    def _():
        even_ref[:, chans:] = bottom_ref[...]
        odd_ref[:, chans:] = top_ref[...]

    up_ref[...] = grid_ref[...].astype(BF)


def first_kernel(
    info, onehot, count_ref, masks, up_ref, from_even, from_odd, skip_ref,
    weight_ref, conv_ref, tile_ref, even_ref, odd_ref, stack_ref, halo_ref, acc_ref,
):
    parity = info[0]
    down, up = masks[0], masks[1]
    chans = up_ref.shape[1]
    up_halo = place_slabs(
        parity, from_even[:, :chans].astype(F32), from_odd[:, :chans].astype(F32)
    )
    skip_halo = place_slabs(
        parity,
        from_even[:, chans : 2 * chans].astype(F32),
        from_odd[:, chans : 2 * chans].astype(F32),
    )
    parts_up = stack_rows(deep(up_ref[...].astype(F32)), *up_halo, up, down)
    parts_skip = stack_rows(deep(skip_ref[...].astype(F32)), *skip_halo, up, down)
    for layer in range(3):
        at = 2 * layer * chans
        stack_ref[:, at : at + chans] = parts_up[layer]
        stack_ref[:, at + chans : at + 2 * chans] = parts_skip[layer]
    for side in range(2):
        halo_ref[side * CELLS : (side + 1) * CELLS, :chans] = up_halo[side].astype(BF)
        halo_ref[side * CELLS : (side + 1) * CELLS, chans:] = skip_halo[side].astype(BF)
    conv_into(acc_ref, stack_ref[...], weight_ref, 2 * chans)
    conv_ref[...] = acc_ref[...].reshape(conv_ref.shape)
    moment_tile(onehot, count_ref, deep(conv_ref[...]), tile_ref)
    send_slabs(conv_ref, parity, even_ref, odd_ref)


def second_kernel(
    high, info, onehot, count_ref, total_ref, masks, conv_one, odd_slab, weight_ref, *refs
):
    n_out = 8
    tiles, outs = refs[: -n_out - 1], refs[-n_out - 1 :]
    conv_ref, tile_ref, even_ref, odd_ref, stack_ref, unit_ref, slab_unit_ref, scale_ref, acc_ref = outs
    parity = info[0]
    down, up = masks[0], masks[1]
    mean, inv = merged_moments(tile_list(tiles, high), count_ref, total_ref)
    mean_z, inv_z = spread(onehot, mean), spread(onehot, inv)
    scale_ref[0] = mean_z
    scale_ref[1] = inv_z
    unit = (deep(conv_one[...]) - mean_z[None]) * inv_z[None]
    unit_ref[...] = flat_rows(unit)
    act = unit * normal_cdf(unit)
    halo = place_slabs(parity, tiles[high][8 * high :, :], odd_slab[...])
    depth = mean_z.shape[0]
    sides = []
    for side, at in ((0, 0), (1, depth - 1)):
        part = (halo[side] - mean_z[at : at + 1]) * inv_z[at : at + 1]
        slab_unit_ref[side * CELLS : (side + 1) * CELLS, :] = part
        sides.append(part * normal_cdf(part))
    parts = stack_rows(act, sides[0], sides[1], up, down)
    chans = conv_one.shape[1]
    for layer in range(3):
        stack_ref[:, layer * chans : (layer + 1) * chans] = parts[layer]
    conv_into(acc_ref, stack_ref[...], weight_ref, chans)
    conv_ref[...] = acc_ref[...].reshape(conv_ref.shape)
    moment_tile(onehot, count_ref, deep(conv_ref[...]), tile_ref)
    send_slabs(conv_ref, parity, even_ref, odd_ref)


def third_kernel(
    high, info, onehot, count_ref, total_ref, conv_two, odd_slab, stack_ref, halo_ref,
    weight_ref, cot_ref, cot_even, cot_odd, *refs
):
    n_out = 7
    tiles, outs = refs[:-n_out], refs[-n_out:]
    decoded_ref, grad_ref, low_ref, unit_ref, slab_ref, tile_ref, inv_ref = outs
    parity = info[0]
    chans = conv_two.shape[1]
    mean, inv = merged_moments(tile_list(tiles, high), count_ref, total_ref)
    mean_z, inv_z = spread(onehot, mean), spread(onehot, inv)
    inv_ref[...] = inv_z
    unit = flat_rows((deep(conv_two[...]) - mean_z[None]) * inv_z[None])
    unit_ref[...] = unit
    joined = stack_ref[:, 2 * chans : 4 * chans]
    summed = unit + jnp.dot(joined, weight_ref[...], preferred_element_type=F32)
    cdf = normal_cdf(summed)
    decoded_ref[...] = (summed * cdf).astype(BF)
    grad = cot_ref[...].astype(F32) * gelu_slope(summed, cdf)
    grad_ref[...] = grad
    low_ref[...] = grad.astype(BF)
    sum_tile(onehot, deep(grad), deep(grad * unit), tile_ref)
    halo = place_slabs(parity, tiles[high][8 * high :, :], odd_slab[...])
    cots = place_slabs(
        parity, cot_even[:, 2 * chans :].astype(F32), cot_odd[:, 2 * chans :].astype(F32)
    )
    depth = mean_z.shape[0]
    for side, at in ((0, 0), (1, depth - 1)):
        rows = slice(side * CELLS, (side + 1) * CELLS)
        part = (halo[side] - mean_z[at : at + 1]) * inv_z[at : at + 1]
        both = part + jnp.dot(halo_ref[rows, :], weight_ref[...], preferred_element_type=F32)
        slab_ref[rows, :chans] = part
        slab_ref[rows, chans:] = cots[side] * gelu_slope(both, normal_cdf(both))


def fourth_kernel(
    high, info, onehot, total_ref, masks, grad_ref, unit_two, inv_two, slab_two, unit_one,
    weight_ref, *refs
):
    n_out = 5
    tiles, outs = refs[: -n_out - 1], refs[-n_out - 1 :]
    second_ref, back_ref, tile_ref, even_ref, odd_ref, acc_ref = outs
    parity = info[0]
    down, up = masks[0], masks[1]
    chans = grad_ref.shape[1]
    first, cross = merged_sums(tile_list(tiles, high), total_ref)
    first_z, cross_z, inv_z = spread(onehot, first), spread(onehot, cross), inv_two[...]
    grad = deep(grad_ref[...]) - first_z[None] - deep(unit_two[...]) * cross_z[None]
    grad = grad * inv_z[None]
    depth = inv_z.shape[0]
    sides = []
    for side, at in ((0, 0), (1, depth - 1)):
        rows = slice(side * CELLS, (side + 1) * CELLS)
        part = slab_two[rows, chans:] - first_z[at : at + 1]
        part = part - slab_two[rows, :chans] * cross_z[at : at + 1]
        sides.append(part * inv_z[at : at + 1])
    parts = stack_rows(grad, sides[0], sides[1], up, down)
    second_ref[...] = parts[1]
    turned_into(acc_ref, jnp.concatenate(parts, axis=1), weight_ref, chans)
    unit = unit_one[...]
    back = acc_ref[...].reshape(back_ref.shape) * gelu_slope(unit, normal_cdf(unit))
    back_ref[...] = back
    sum_tile(onehot, deep(back), deep(back * unit), tile_ref)
    send_slabs(back_ref, parity, even_ref, odd_ref)


def fifth_kernel(
    high, slices, info, onehot, total_ref, masks, back_ref, unit_one, scale_one, slab_one,
    odd_slab, low_ref, weight_ref, resid_ref, up_weight_ref, *refs
):
    n_out = 5
    tiles, outs = refs[: -n_out - 1], refs[-n_out - 1 :]
    first_ref, skip_ref, rows_ref, encoded_ref, mixed_ref, acc_ref = outs
    parity = info[0]
    down, up = masks[0], masks[1]
    chans = back_ref.shape[1]
    first, cross = merged_sums(tile_list(tiles, high), total_ref)
    first_z, cross_z, inv_z = spread(onehot, first), spread(onehot, cross), scale_one[1]
    grad = deep(back_ref[...]) - first_z[None] - deep(unit_one[...]) * cross_z[None]
    grad = grad * inv_z[None]
    halo = place_slabs(parity, tiles[high][8 * high :, :], odd_slab[...])
    depth = inv_z.shape[0]
    sides = []
    for side, at in ((0, 0), (1, depth - 1)):
        rows = slice(side * CELLS, (side + 1) * CELLS)
        part = halo[side] - first_z[at : at + 1] - slab_one[rows, :] * cross_z[at : at + 1]
        sides.append(part * inv_z[at : at + 1])
    parts = stack_rows(grad, sides[0], sides[1], up, down)
    first_ref[...] = parts[1]
    turned_into(acc_ref, jnp.concatenate(parts, axis=1), weight_ref, 2 * chans)
    field = acc_ref[...].reshape(back_ref.shape[0], 2 * chans) + lax.dot_general(
        low_ref[...], resid_ref[...], (((1,), (1,)), ((), ())), preferred_element_type=F32
    )
    skip_ref[...] = field[:, chans:]
    plane = PH * PH
    columns = []
    for place in range(8):
        part_a, part_b, part_e = place // 4, (place // 2) % 2, place % 2
        pieces = []
        for cell in range(plane):
            at = (2 * (cell // PH) + part_b) * GRID + 2 * (cell % PH) + part_e
            low = at * depth + part_a * slices
            pieces.append(field[low : low + slices, :chans])
        columns.append(jnp.concatenate(pieces, axis=0))
    up_rows = jnp.concatenate(columns, axis=1).astype(BF)
    rows_ref[...] = jnp.dot(
        token_order(plane * slices, slices, True), up_rows, preferred_element_type=F32
    ).astype(BF)
    encoded = lax.dot_general(
        rows_ref[...], up_weight_ref[...], (((1,), (1,)), ((), ())), preferred_element_type=F32
    )
    encoded_ref[...] = encoded
    mixed_ref[...] = encoded.astype(BF)


def tap_grad_kernel(
    in_chans, high, low, wide, info, stack_ref, grad_ref, left_ref, right_ref, *refs
):
    outs, (turned_ref, pad_ref, rows_ref, extra_ref) = refs[:low], refs[low:]
    chans = grad_ref.shape[1]
    count = high * low
    shard = 27 * in_chans // count
    depth = grad_ref.shape[0] // CELLS
    pad_ref[...] = jnp.zeros_like(pad_ref)
    pad_ref[1 : GRID + 1, 1 : GRID + 1] = grad_ref[...].reshape(GRID, GRID, depth, chans)
    for tap in range(9):
        low_i, low_j = 2 - tap // 3, 2 - tap % 3
        moved = pad_ref[low_i : low_i + GRID, low_j : low_j + GRID]
        turned_ref[tap * chans : (tap + 1) * chans, :] = moved.reshape(-1, chans).T
    for layer in range(3):
        at = layer * in_chans
        product = jnp.dot(
            turned_ref[...], stack_ref[:, at : at + in_chans], preferred_element_type=F32
        )
        for tap in range(9):
            block = product[tap * chans : (tap + 1) * chans, :].T
            start = (layer * 9 + tap) * in_chans
            done = 0
            while done < in_chans:
                owner, place = divmod(start + done, shard)
                size = min(in_chans - done, shard - place)
                rows_ref[owner, place : place + size, :] = block[done : done + size, :]
                done += size
    extra = extra_ref.shape[1]
    left = left_ref[...]
    if wide == 1:
        left = left[:, 2 * chans : 4 * chans]
    extra_ref[...] = cross_rows(left, right_ref[...]).reshape(extra_ref.shape)
    for s in range(low):
        for m in range(high):
            owner = (info[1] ^ m) * low + (info[2] ^ s)
            outs[s][m, :shard, :] = rows_ref[owner][:shard].astype(BF)
            other = extra_ref[owner].astype(BF)
            for place in range(wide):
                start = shard + place * extra
                outs[s][m, start : start + extra, :] = other[
                    :, place * chans : (place + 1) * chans
                ]


def pack_kernel(high, info, token_ref, joint_ref, expand_ref, out_w_ref, *refs):
    vecs, joints, expands = refs[: -2 * high], refs[-2 * high : -high], refs[-high:]
    span = joint_ref.shape[1] // (3 * high)
    third = joint_ref.shape[1] // 3
    wide = expand_ref.shape[1] // high
    rows = token_ref.shape[0]
    shard = joint_ref.shape[0]
    lines = [ref[...] for ref in vecs]
    lines.append(jnp.zeros((128 - sum(line.shape[0] for line in lines), shard), F32))
    columns = jnp.concatenate(lines, axis=0).T[:, :64].astype(BF)
    top = 3 * span + 64
    for own in range(high):

        @pl.when(info[1] == own)
        def _():
            for m in range(high):
                group = own ^ m
                joints[m][:rows, :] = token_ref[...]
                for part in range(3):
                    joints[m][rows:, part * span : (part + 1) * span] = joint_ref[
                        :, part * third + group * span : part * third + (group + 1) * span
                    ]
                joints[m][rows:, 3 * span : top] = columns
                if top < joints[m].shape[1]:
                    joints[m][rows:, top:] = jnp.zeros(
                        (joint_ref.shape[0], joints[m].shape[1] - top), BF
                    )
                expands[m][0] = expand_ref[:, group * wide : (group + 1) * wide]
                expands[m][1] = out_w_ref[...]


def assembled(info, high, low, natural, parts, scratch_ref):
    rows = scratch_ref.shape[1]
    for s in range(low):
        for m in range(high):
            block = parts[m][...] if s == 0 else parts[high + s - 1][m * rows : (m + 1) * rows, :]
            major = (info[1] ^ m) if natural else m
            scratch_ref[major * low + (info[2] ^ s)] = block.astype(F32)


def order_kernel(high, low, natural, slab, info, *refs):
    parts, out_ref, scratch_ref = refs[:-2], refs[-2], refs[-1]
    if slab is None:
        assembled(info, high, low, natural, parts, scratch_ref)
    else:
        for s in range(low):
            for m in range(high):
                block = parts[m][slab] if s == 0 else parts[high + s - 1][m, slab]
                major = (info[1] ^ m) if natural else m
                scratch_ref[major * low + (info[2] ^ s)] = block.astype(F32)
    out_ref[...] = scratch_ref[...].reshape(out_ref.shape).astype(BF)


def unit_rows_of(values):
    average = jnp.mean(values, axis=-1, keepdims=True)
    centred = values - average
    inv_std = lax.rsqrt(jnp.mean(centred * centred, axis=-1, keepdims=True) + EPS_LAYER)
    return centred * inv_std, inv_std


def query_kernel(high, low, info, *refs):
    tokens, partners = refs[:high], refs[high : high + low - 1]
    q_ref, kv_ref, normed_ref, weight_ref, vec_ref, own_vec_ref, scratch_ref = refs[-7:]
    width = normed_ref.shape[1]
    wide = weight_ref.shape[1]
    span = q_ref.shape[1]
    rows = normed_ref.shape[0] // high
    own_parts = [ref.at[rows:, :wide] for ref in tokens]
    assembled(info, high, low, True, own_parts + list(partners), scratch_ref)
    weight = scratch_ref[...].reshape(width, wide)
    weight_ref[...] = weight.astype(BF)
    turned = weight[:, wide - 128 :].T
    vec_ref[...] = turned[64:80, :]
    own = scratch_ref[pl.ds(info[1] * low, low), :, :][:, :, wide - 128 :]
    own_turned = own.reshape(width // high, 128).T
    own_vec_ref[...] = own_turned[64:80, :]
    gain, shift = turned[64:65, :], turned[65:66, :]
    for m in range(high):
        unit, _ = unit_rows_of(tokens[m][:rows, :].astype(F32))
        normed_ref[m * rows : (m + 1) * rows, :] = (unit * gain + shift).astype(BF)
    joint = jnp.dot(normed_ref[...], weight_ref[...], preferred_element_type=F32)
    q_ref[...] = (joint[:, :span] + own_turned[66:67, :]).astype(BF)
    kv_ref[:, :span] = joint[:, span : 2 * span].astype(BF)
    kv_ref[:, span:] = (joint[:, 2 * span : 3 * span] + own_turned[67:68, :]).astype(BF)


def head_columns(refs, start, head_dim):
    return jnp.concatenate([ref[:, start : start + head_dim] for ref in refs], axis=0)


def masked_scores(keys, queries, same):
    scores = lax.dot_general(
        keys, queries, (((1,), (1,)), ((), ())), preferred_element_type=F32
    )
    return jnp.where(same, scores, -1000000000.0)


def attend_kernel(high, head_dim, q_ref, crop_q, crop_k, *refs):
    kvs, outs = refs[: -high - 1], refs[-high - 1 :]
    log_ref = outs[-1]
    span = q_ref.shape[1]
    same = crop_k[...] == crop_q[...]
    scale = 1.0 / math.sqrt(head_dim)
    pieces = []
    for head in range(span // head_dim):
        at = head * head_dim
        queries = q_ref[:, at : at + head_dim] * jnp.asarray(scale, BF)
        scores = masked_scores(head_columns(kvs, at, head_dim), queries, same)
        highest = jnp.max(scores, axis=0, keepdims=True)
        powers = jnp.exp(scores - highest)
        sums = jnp.sum(powers, axis=0, keepdims=True)
        log_ref[head : head + 1, :] = highest + jnp.log(sums)
        share = (powers * (1.0 / sums)).astype(BF)
        values = head_columns(kvs, span + at, head_dim)
        pieces.append(jnp.dot(values.T, share, preferred_element_type=F32))
    attended = jnp.concatenate(pieces, axis=0).T.astype(BF)
    rows = outs[0].shape[0]
    for m in range(high):
        outs[m][...] = attended[m * rows : (m + 1) * rows, :]


def middle_kernel(high, token_ref, weight_ref, vec_ref, *refs):
    parts, (middle_ref, inner_ref) = refs[:high], refs[high:]
    span = parts[0].shape[1]
    middle = token_ref[...].astype(F32) + vec_ref[4:5, :]
    for m in range(high):
        middle = middle + jnp.dot(
            parts[m][...], weight_ref[m * span : (m + 1) * span, :], preferred_element_type=F32
        )
    middle_ref[...] = middle
    unit, _ = unit_rows_of(middle)
    inner_ref[...] = (unit * vec_ref[5:6, :] + vec_ref[6:7, :]).astype(BF)


def mix_kernel(high, expand_ref, reduce_ref, bias_ref, *refs):
    parts, outs = refs[:high], refs[high:]
    act_ref, slope_ref = outs[high], outs[high + 1]
    rows = parts[0].shape[0]
    for m in range(high):
        at = slice(m * rows, (m + 1) * rows)
        expanded = bias_ref[...] + jnp.dot(
            parts[m][...], expand_ref[...], preferred_element_type=F32
        )
        cdf = normal_cdf(expanded)
        act = (expanded * cdf).astype(BF)
        act_ref[at, :] = act
        slope_ref[at, :] = gelu_slope(expanded, cdf)
        mixed = jnp.dot(act, reduce_ref[...], preferred_element_type=F32)
        outs[m][...] = mixed.astype(outs[m].dtype)


def plane_total(parts):
    total = parts[0][...]
    for ref in parts[1:]:
        total = total + ref[...].astype(F32)
    return total


def token_order(tok_rows, slices, back):
    plane = tok_rows // slices
    row = lax.broadcasted_iota(jnp.int32, (tok_rows, tok_rows), 0)
    col = lax.broadcasted_iota(jnp.int32, (tok_rows, tok_rows), 1)
    if back:
        row, col = col, row
    return jnp.where(col == (row % slices) * plane + row // slices, 1.0, 0.0).astype(BF)


def mix_back_kernel(high, reduce_ref, expand_ref, slope_ref, *refs):
    parts, outs = refs[:high], refs[high:]
    grad_ref = outs[high]
    rows = parts[0].shape[0]
    for m in range(high):
        at = slice(m * rows, (m + 1) * rows)
        grad = lax.dot_general(
            parts[m][...], reduce_ref[...], (((1,), (1,)), ((), ())), preferred_element_type=F32
        )
        grad = (grad * slope_ref[at, :]).astype(BF)
        grad_ref[at, :] = grad
        back = lax.dot_general(
            grad, expand_ref[...], (((1,), (1,)), ((), ())), preferred_element_type=F32
        )
        outs[m][...] = back.astype(outs[m].dtype)


def cross_rows(first, second):
    return lax.dot_general(first, second, (((0,), (0,)), ((), ())), preferred_element_type=F32)


def deal_rows(info, high, low, scratch_ref, outs):
    shard = outs[0].shape[1]
    for s in range(low):
        for m in range(high):
            at = ((info[1] ^ m) * low + (info[2] ^ s)) * shard
            outs[s][m] = scratch_ref[pl.ds(pl.multiple_of(at, 8), shard), :].astype(BF)


def deal_chip(info, low, scratch_ref, outs):
    shard = outs[0].shape[0]
    for s in range(low):
        at = (info[2] ^ s) * shard
        outs[s][...] = scratch_ref[pl.ds(pl.multiple_of(at, 8), shard), :].astype(BF)


def mix_grad_kernel(high, low, info, act_ref, grad_ref, *refs):
    mixed = jnp.concatenate([ref[...] for ref in refs[:high]], axis=0)
    inner = jnp.concatenate([ref[...] for ref in refs[high : 2 * high]], axis=0)
    outs = refs[2 * high :]
    bias_ref, scratch_ref = outs[2 * low], outs[2 * low + 1]
    scratch_ref[...] = cross_rows(act_ref[...], mixed)
    deal_chip(info, low, scratch_ref, outs[:low])
    scratch_ref[...] = cross_rows(inner, grad_ref[...])
    deal_rows(info, high, low, scratch_ref, outs[low : 2 * low])
    bias_ref[...] = jnp.sum(grad_ref[...].astype(F32), axis=0, keepdims=True)


def norm_back(upstream, unit, inv_std, gain):
    scaled = upstream * gain
    return inv_std * (
        scaled
        - jnp.mean(scaled, axis=-1, keepdims=True)
        - unit * jnp.mean(scaled * unit, axis=-1, keepdims=True)
    )


def branch_kernel(high, middle_ref, vec_ref, encoded_ref, mixed_ref, *refs):
    parts, (grad_ref, branch_ref, sums_ref) = refs[:high], refs[high:]
    inner = plane_total(parts)
    unit, inv_std = unit_rows_of(middle_ref[...])
    grad = encoded_ref[...] + norm_back(inner, unit, inv_std, vec_ref[5:6, :])
    grad_ref[...] = grad
    branch = grad.astype(BF)
    branch_ref[...] = branch
    sums_ref[...] = jnp.zeros_like(sums_ref)
    sums_ref[4:5, :] = jnp.sum(branch.astype(F32), axis=0, keepdims=True)
    sums_ref[5:6, :] = jnp.sum(inner * unit, axis=0, keepdims=True)
    sums_ref[6:7, :] = jnp.sum(inner, axis=0, keepdims=True)
    sums_ref[7:8, :] = jnp.sum(mixed_ref[...].astype(F32), axis=0, keepdims=True)


def attend_back_kernel(high, low, head_dim, q_ref, crop_q, crop_k, log_ref, weight_ref, *refs):
    branches, kvs = refs[:high], refs[high : high + low]
    outs = refs[high + low :]
    dq_ref, dkv_refs = outs[0], outs[1:]
    span = q_ref.shape[1]
    branch = jnp.concatenate([ref[...] for ref in branches], axis=0)
    attended = lax.dot_general(
        branch, weight_ref[:span, :], (((1,), (1,)), ((), ())), preferred_element_type=F32
    ).astype(BF)
    same = crop_k[...] == crop_q[...]
    scale = 1.0 / math.sqrt(head_dim)
    rows = dq_ref.shape[0]
    pieces = []
    for head in range(span // head_dim):
        at = head * head_dim
        queries = q_ref[:, at : at + head_dim] * jnp.asarray(scale, BF)
        keys = head_columns(kvs, at, head_dim)
        values = head_columns(kvs, span + at, head_dim)
        grad_out = attended[:, at : at + head_dim]
        share = jnp.exp(masked_scores(keys, queries, same) - log_ref[head : head + 1, :])
        weights = lax.dot_general(
            values, grad_out, (((1,), (1,)), ((), ())), preferred_element_type=F32
        )
        row_dot = jnp.sum(share * weights, axis=0, keepdims=True)
        grad_scores = (share * (weights - row_dot)).astype(BF)
        grad_keys = jnp.dot(grad_scores, queries, preferred_element_type=F32)
        grad_values = jnp.dot(share.astype(BF), grad_out, preferred_element_type=F32)
        for s in range(low):
            part = slice(s * rows, (s + 1) * rows)
            kind = dkv_refs[s].dtype
            dkv_refs[s][:, at : at + head_dim] = grad_keys[part, :].astype(kind)
            dkv_refs[s][:, span + at : span + at + head_dim] = grad_values[part, :].astype(kind)
        pieces.append(jnp.dot(keys.T, grad_scores, preferred_element_type=F32) * scale)
    dq_ref[...] = jnp.concatenate(pieces, axis=0).T.astype(BF)


def output_grad_kernel(high, low, info, *refs):
    attended = jnp.concatenate([ref[...] for ref in refs[:high]], axis=0)
    branch = jnp.concatenate([ref[...] for ref in refs[high : 2 * high]], axis=0)
    outs, scratch_ref = refs[2 * high : -1], refs[-1]
    scratch_ref[...] = cross_rows(attended, branch)
    deal_chip(info, low, scratch_ref, outs)


def joint_back_kernel(high, low, info, dq_ref, normed_ref, weight_ref, vec_ref, sums_ref,
                      bias_ref, *refs):
    dkvs, tokens = refs[:low], refs[low : low + high]
    outs = refs[low + high :]
    joint_ref, scratch_ref = outs[-2], outs[-1]
    backs, dealt = outs[:high], outs[high : high + low]
    span = dq_ref.shape[1]
    joint_ref[...] = jnp.zeros_like(joint_ref)
    joint_ref[:, :span] = dq_ref[...]
    joint_ref[:, span : 3 * span] = plane_total(dkvs).astype(BF)
    rows = backs[0].shape[0]
    gain_sum, shift_sum = 0.0, 0.0
    for m in range(high):
        part = lax.dot_general(
            joint_ref[m * rows : (m + 1) * rows, :], weight_ref[...], (((1,), (1,)), ((), ())),
            preferred_element_type=F32,
        )
        backs[m][...] = part.astype(backs[m].dtype)
        unit, _ = unit_rows_of(tokens[m][:rows, :].astype(F32))
        gain_sum = gain_sum + jnp.sum(part * unit, axis=0, keepdims=True)
        shift_sum = shift_sum + jnp.sum(part, axis=0, keepdims=True)
    wide = joint_ref.shape[1]
    width = normed_ref.shape[1]
    scratch_ref[...] = cross_rows(normed_ref[...], joint_ref[...])
    whole = jnp.concatenate(
        [
            jnp.zeros((64, width), F32), gain_sum, shift_sum, sums_ref[2:8, :],
            jnp.zeros((56, width), F32),
        ],
        axis=0,
    )
    scratch_ref[:, wide - 128 :] += whole.T
    sums = jnp.sum(joint_ref[...].astype(F32), axis=0, keepdims=True)
    own = jnp.concatenate(
        [
            jnp.zeros((66, span), F32), sums[:, :span], sums[:, 2 * span : 3 * span],
            jnp.zeros((4, span), F32), bias_ref[...],
            jnp.zeros((56 - bias_ref.shape[0], span), F32),
        ],
        axis=0,
    )
    at = pl.multiple_of(info[1] * span, 8)
    scratch_ref[pl.ds(at, span), wide - 128 :] += own.T
    deal_rows(info, high, low, scratch_ref, dealt)


def chip_add_kernel(high, low, *refs):
    parts, outs = refs[:-high], refs[-high:]
    for m in range(high):
        done = 0
        for start in range(0, len(parts), low):
            total = parts[start][m].astype(F32)
            for ref in parts[start + 1 : start + low]:
                total = total + ref[m].astype(F32)
            outs[m][done : done + total.shape[0], :] = total.astype(BF)
            done += total.shape[0]
        if done < outs[m].shape[0]:
            outs[m][done:, :] = jnp.zeros((outs[m].shape[0] - done, outs[m].shape[1]), BF)


def select_kernel(info, *refs):
    count = len(refs) // 2
    for own in range(count):

        @pl.when(info[3] == own)
        def _():
            for t in range(count):
                refs[count + t][...] = refs[own ^ t][...]


def joint_final_kernel(high, info, *refs):
    parts, (out_ref, vec_ref) = refs[:high], refs[high:]
    span = out_ref.shape[1] // (3 * high)
    third = out_ref.shape[1] // 3
    for place in range(high):

        @pl.when(info[4] == place)
        def _():
            for group in range(high):
                for part in range(3):
                    out_ref[:, part * third + group * span : part * third + (group + 1) * span] = (
                        parts[place ^ group][:, part * span : (part + 1) * span].astype(F32)
                    )
    total = parts[0][...].astype(F32)
    for ref in parts[1:]:
        total = total + ref[...].astype(F32)
    vec_ref[...] = total[:, total.shape[1] - 128 :].T[64:80, :]


def expand_final_kernel(high, info, block_ref, out_ref):
    wide = out_ref.shape[1] // high
    rows = out_ref.shape[0]
    for place in range(high):

        @pl.when(info[1] == place)
        def _():
            for group in range(high):
                m = place ^ group
                out_ref[:, group * wide : (group + 1) * wide] = block_ref[
                    m * rows : (m + 1) * rows, :
                ].astype(F32)


def tokens_kernel(high, grad_ref, token_ref, vec_ref, *refs):
    parts, out_ref = refs[:high], refs[high]
    unit, inv_std = unit_rows_of(token_ref[...].astype(F32))
    out_ref[...] = grad_ref[...] + norm_back(plane_total(parts), unit, inv_std, vec_ref[0:1, :])


def on_device(
    tokens,
    skip_features,
    out_grad,
    crop_lengths,
    attend_gain,
    attend_shift,
    joint_weight,
    query_bias,
    value_bias,
    output_weight,
    output_bias,
    mixer_gain,
    mixer_shift,
    expand_weight,
    expand_bias,
    reduce_weight,
    reduce_bias,
    upsample_weight,
    kernel_first,
    kernel_second,
    residual_weight,
):
    count = lax.axis_size("seq")
    nb = lax.axis_size("batch")
    high = math.gcd(HEADS, count)
    low = count // high
    seq_index = lax.axis_index("seq")
    batch_index = lax.axis_index("batch")
    hi = seq_index // low
    lo = seq_index % low
    width = tokens.shape[2]
    shard = joint_weight.shape[0]
    head_dim = width // HEADS
    span = HEADS // high * head_dim
    wide = -(-(3 * span + 64) // 128) * 128
    hidden = expand_weight.shape[1]
    hid_span = hidden // high
    hid_shard = hidden // count
    channels = residual_weight.shape[1]
    plane_size = PH * PH
    tok_rows = tokens.shape[1]
    rows = high * tok_rows
    slices = tok_rows // plane_size
    depth_total = 2 * slices
    positions = depth_total * 4 * plane_size
    lengths = crop_lengths[0]
    own_tokens = tokens[0]
    by_place = nb == high
    place = batch_index ^ hi if by_place else hi
    info = jnp.stack([seq_index % 2, hi, lo, batch_index, place]).astype(jnp.int32)

    def plane_swaps(blocks):
        return [swap(blocks[m], "seq", m * low) for m in range(1, high)]

    def plane_copies(block):
        return [block] + [swap(block, "seq", m * low) for m in range(1, high)]

    def chip_swaps(blocks):
        return [swap(blocks[s], "seq", s) for s in range(1, low)]

    def chip_copies(block):
        return [swap(block, "seq", s) for s in range(1, low)]

    def after(values, done):
        return lax.optimization_barrier((values, tuple(done)))[0]

    def owners(rel_hi, rel_lo):
        return (hi ^ rel_hi) * low + (lo ^ rel_lo)

    def odd_swap(values):
        pairs = [(i, i + 1) for i in range(1, count - 1, 2)]
        return lax.ppermute(values, "seq", pairs + [(j, i) for i, j in pairs])

    vectors = [
        attend_gain, attend_shift, query_bias, value_bias, output_bias, mixer_gain, mixer_shift,
        reduce_bias,
    ]
    vectors = [
        jnp.stack([vec.astype(F32) for vec in vectors]),
        expand_bias.astype(F32).reshape(hid_shard // shard, shard),
    ]
    packed = call(
        functools.partial(pack_kernel, high),
        [((tok_rows + shard, width), BF)] * high + [((2, shard, width), BF)] * high,
        [],
        info, own_tokens, joint_weight, expand_weight, output_weight, *vectors, smem=1,
    )
    all_tokens = list(packed[:1]) + plane_swaps(packed[:high])
    partners = chip_copies(jnp.concatenate([part[tok_rows:, :wide] for part in all_tokens], axis=0))
    q, kv, normed, joint_w, vecs, own_vecs = call(
        functools.partial(query_kernel, high, low),
        [((rows, span), BF), ((rows, 2 * span), BF), ((rows, width), BF), ((width, wide), BF),
         ((16, width), F32), ((16, span), F32)],
        [((count, shard, wide), F32)],
        info, *all_tokens, *partners, smem=1,
    )
    kvs = [kv] + chip_copies(kv)

    def ordered(parts, natural, shape, block, slab=None):
        kernel = functools.partial(order_kernel, block[0], low, natural, slab)
        return call(
            kernel, [(shape, BF)], [((block[0] * low, block[1], shape[1]), F32)], info, *parts,
            smem=1,
        )[0]

    later_pairs = after(tuple(packed[high:]), all_tokens[1:])
    pairs = [later_pairs[0]] + plane_swaps(later_pairs)
    expand_b = own_vecs[8 : 8 + hid_shard // shard].reshape(hid_shard // shard, low, shard)
    expand_b = expand_b.transpose(1, 0, 2).reshape(1, hid_span)
    later_up, later_conv = after(
        (upsample_weight, (kernel_first, kernel_second, residual_weight)), ()
    )
    upsample_w = lax.all_gather(later_up, "seq", axis=0, tiled=True)
    conv_all = lax.all_gather(
        jnp.concatenate(later_conv, axis=0), "seq", axis=0
    )
    cut_one = kernel_first.shape[0]
    cut_two = cut_one + kernel_second.shape[0]
    kernel_one = conv_all[:, :cut_one].reshape(-1, channels)
    kernel_two = conv_all[:, cut_one:cut_two].reshape(-1, channels)
    residual_w = conv_all[:, cut_two:].reshape(-1, channels)

    def token_crops(rel_lo):
        starts = jnp.stack([owners(m, rel_lo) for m in range(high)]) * slices
        ids = starts[:, None] + jnp.arange(tok_rows, dtype=jnp.int32)[None, :] // plane_size
        return crops_of(lengths, ids.reshape(-1))

    crop_q = token_crops(0).reshape(1, rows)
    crop_k = jnp.concatenate([token_crops(s) for s in range(low)]).reshape(low * rows, 1)
    slice_ids = seq_index * slices - 1 + jnp.arange(slices + 2, dtype=jnp.int32)
    crop_ids = jnp.where(slice_ids < 0, -1, crops_of(lengths, slice_ids))
    here = crop_ids[1:-1]
    masks = jnp.stack([crop_ids[:-2] == here, crop_ids[2:] == here]).astype(F32)
    masks = jnp.broadcast_to(masks[:, :, None], (2, slices, channels))
    onehot = (jnp.arange(CROPS, dtype=jnp.int32)[:, None] == here[None, :]).astype(F32)
    onehot = jnp.broadcast_to(
        jnp.tile(onehot, (1, 2))[:, :, None], (CROPS, depth_total, channels)
    )
    total = jnp.broadcast_to(
        (lengths * 8 * plane_size).astype(F32)[:, None], (CROPS, channels)
    )
    crop_ends = jnp.cumsum(lengths)
    dev_rel = jnp.stack([owners(m, s) for s in range(low) for m in range(high)])
    first = (dev_rel * slices)[:, None]
    shared = jnp.minimum(crop_ends[None], first + slices) - jnp.maximum(
        (crop_ends - lengths)[None], first
    )
    held = (jnp.maximum(shared, 0) * 8 * plane_size).astype(F32)
    held = jnp.broadcast_to(held[:, :, None], (count, CROPS, channels))

    *attended, log_total = call(
        functools.partial(attend_kernel, high, head_dim),
        [((tok_rows, span), BF)] * high + [((8, rows), F32)],
        [],
        q, crop_q, crop_k, *kvs,
    )
    arrived = [attended[0]] + plane_swaps(attended)
    pairs = list(after(tuple(pairs), (attended[0],)))
    pairs += chip_copies(jnp.stack(pairs))
    out_w = ordered(pairs, False, (width, width), (high, shard), 1)
    middle, inner = call(
        functools.partial(middle_kernel, high),
        [((tok_rows, width), F32), ((tok_rows, width), BF)],
        [],
        own_tokens, out_w, vecs, *arrived,
    )
    inners = plane_copies(inner)
    expand_w = ordered(list(after(tuple(pairs), (inner,))), True, (width, hid_span), (high, shard), 0)
    reduces = [reduce_weight] + chip_copies(after(reduce_weight, (inner,)))
    reduce_w = ordered(reduces, False, (hid_span, width), (1, hid_shard))
    partial_kinds = [((tok_rows, width), F32)] + [((tok_rows, width), BF)] * (high - 1)
    *mixed, act, slope = call(
        functools.partial(mix_kernel, high),
        partial_kinds + [((rows, hid_span), BF), ((rows, hid_span), F32)],
        [],
        expand_w, reduce_w, expand_b, *inners,
    )
    mixed = [mixed[0]] + plane_swaps(mixed)

    def to_cells(values):
        cells = values.reshape(slices, 2, CELLS, channels)
        return cells.transpose(2, 1, 0, 3).reshape(positions, channels)

    def from_cells(values):
        cells = values.reshape(CELLS, 2, slices, channels)
        return cells.transpose(2, 1, 0, 3).reshape(positions, channels)

    skip_cells = to_cells(skip_features[0])
    cot_cells = to_cells(out_grad[0])
    side_slabs = jnp.concatenate([skip_features[0], out_grad[0]], axis=1)
    top, bottom = side_slabs[-CELLS:], side_slabs[:CELLS]

    cells_bf = ((positions, channels), BF)
    cells_f = ((positions, channels), F32)
    slab_f = ((CELLS, channels), F32)
    slab_bf = ((CELLS, 3 * channels), BF)
    slabs_f = ((2 * CELLS, channels), F32)
    tile = ((2 * CROPS, channels), F32)
    grid_acc = ((GRID, GRID, depth_total, channels), F32)

    def exchange(own_tile, even_slab=None, odd_slab=None):
        tiles = plane_copies(own_tile)
        if even_slab is None:
            return tiles + chip_copies(jnp.concatenate(tiles, axis=0)), None
        odd_slab = odd_swap(odd_slab)
        even_slab, odd_slab = lax.optimization_barrier((even_slab, odd_slab))
        return tiles + chip_copies(jnp.concatenate(tiles + [even_slab], axis=0)), odd_slab

    encoded, upsampled, up_even, up_odd = call(
        functools.partial(up_kernel, high, slices),
        [((tok_rows, width), BF), cells_bf, slab_bf, slab_bf],
        [cells_f],
        info, middle, vecs, upsample_w, top, bottom, *mixed, smem=1,
    )
    up_even, up_odd = swap(up_even, "seq", 1), odd_swap(up_odd)
    first_conv, tile_one, even_one, odd_one, joined_stack, joined_halo = call(
        first_kernel,
        [cells_f, tile, slab_f, slab_f, ((positions, 6 * channels), BF),
         ((2 * CELLS, 2 * channels), BF)],
        [grid_acc],
        info, onehot, held, masks, upsampled, up_even, up_odd, skip_cells,
        kernel_one, smem=1,
    )
    tiles, odd_one = exchange(tile_one, even_one, odd_one)
    (second_conv, tile_two, even_two, odd_two, act_stack, first_unit, slab_unit, scale_one) = call(
        functools.partial(second_kernel, high),
        [cells_f, tile, slab_f, slab_f, ((positions, 3 * channels), BF), cells_f, slabs_f,
         ((2, depth_total, channels), F32)],
        [grid_acc],
        info, onehot, held, total, masks, first_conv, odd_one, kernel_two, *tiles, smem=1,
    )
    tiles, odd_two = exchange(tile_two, even_two, odd_two)
    decoded_cells, grad_summed, grad_resid, second_unit, slab_two, tile_three, inv_two = call(
        functools.partial(third_kernel, high),
        [cells_bf, cells_f, cells_bf, cells_f, ((2 * CELLS, 2 * channels), F32), tile,
         ((depth_total, channels), F32)],
        [],
        info, onehot, held, total, second_conv, odd_two, joined_stack, joined_halo,
        residual_w, cot_cells, up_even, up_odd, *tiles, smem=1,
    )
    decoded = from_cells(decoded_cells)
    tiles, _ = exchange(tile_three)
    grad_second, grad_back, tile_four, even_four, odd_four = call(
        functools.partial(fourth_kernel, high),
        [cells_bf, cells_f, tile, slab_f, slab_f],
        [grid_acc],
        info, onehot, total, masks, grad_summed, second_unit, inv_two, slab_two, first_unit,
        kernel_two, *tiles, smem=1,
    )

    def tap_grad(stack, upstream, in_chans, left, right, wide_blocks, extra_shape):
        part = 27 * in_chans // count
        extra = extra_shape[0] // count
        dealt = call(
            functools.partial(tap_grad_kernel, in_chans, high, low, wide_blocks),
            [((high, part + wide_blocks * extra, channels), BF)] * low,
            [((9 * channels, positions), BF),
             ((GRID + 2, GRID + 2, depth_total, channels), BF),
             ((count, -(-part // 8) * 8, channels), F32),
             ((count, extra, extra_shape[1]), F32)],
            info, stack, upstream, left, right, smem=1,
        )
        return dealt

    def chip_add(*groups):
        held = sum(group[0].shape[1] for group in groups)
        kind = [((-(-held // 32) * 32, groups[0][0].shape[2]), BF)] * high
        parts = [part for group in groups for part in [group[0]] + chip_swaps(group)]
        return call(functools.partial(chip_add_kernel, high, low), kind, [], *parts)

    class Line:
        def __init__(self, values):
            self.stage, self.values = 0, values
            self.upper = batch_index >= 2
            self.outer = (batch_index == 0) | (batch_index == 3)
            if nb == 4:
                self.got = lax.ppermute(values, "batch", [(0, 1), (3, 2)])
            else:
                self.got = lax.psum(values, "batch")

        def step(self):
            if nb != 4:
                return
            self.stage += 1
            inner = [(1, 2), (2, 1)]
            if self.stage == 1:
                both = sum_list([self.values, self.got]).astype(BF)
                half = both.shape[0] // 2
                self.values = jnp.where(self.upper, both[half:], both[:half])
                sent = jnp.where(self.upper, both[:half], both[half:])
                self.got = lax.ppermute(sent, "batch", inner)
            elif self.stage == 2:
                self.values = sum_list([self.values, self.got]).astype(BF)
                self.got = lax.ppermute(self.values, "batch", inner)
            else:
                low_first = jnp.concatenate([self.values, self.got], axis=0)
                high_first = jnp.concatenate([self.got, self.values], axis=0)
                self.values = jnp.where(self.upper, high_first, low_first)
                self.got = lax.ppermute(self.values, "batch", [(1, 0), (2, 3)])

        def total(self):
            return self.got if nb != 4 else jnp.where(self.outer, self.got, self.values)

    tiles, odd_four = exchange(tile_four, even_four, odd_four)
    two_dealt = tap_grad(
        act_stack, grad_second, channels, joined_stack, grad_resid, 1, (2 * channels, channels)
    )
    tiles = after(tuple(tiles), two_dealt)
    grad_first, skip_cells_grad, grad_up_rows, grad_encoded, own_mixed = call(
        functools.partial(fifth_kernel, high, slices),
        [cells_bf, cells_f, ((tok_rows, 8 * channels), BF), ((tok_rows, width), F32),
         ((tok_rows, width), BF)],
        [((GRID, GRID, depth_total, 2 * channels), F32)],
        info, onehot, total, masks, grad_back, first_unit, scale_one, slab_unit, odd_four,
        grad_resid, kernel_one, residual_w, upsample_w, *tiles, smem=1,
    )
    skip_grad = from_cells(skip_cells_grad)

    def pin(first, second):
        return lax.optimization_barrier((first, second))

    grads_mixed = plane_copies(own_mixed)
    one_dealt = tap_grad(
        joined_stack, grad_first, 2 * channels, encoded, grad_up_rows, 8, (width, 8 * channels)
    )
    grads_mixed, one_dealt = pin(grads_mixed, one_dealt)
    *inner_parts, grad_expanded = call(
        functools.partial(mix_back_kernel, high),
        partial_kinds + [((rows, hid_span), BF)],
        [],
        reduce_w, expand_w, slope, *grads_mixed,
    )
    inner_parts = [inner_parts[0]] + plane_swaps(inner_parts)
    mix_dealt = call(
        functools.partial(mix_grad_kernel, high, low),
        [((hid_shard, width), BF)] * low + [((high, shard, hid_span), BF)] * low
        + [((1, hid_span), F32)],
        [((width, hid_span), F32)],
        info, act, grad_expanded, *grads_mixed, *inners, smem=1,
    )
    conv_dealt = after((tuple(two_dealt), tuple(one_dealt)), (grad_expanded,))
    conv_blocks = chip_add(*conv_dealt)
    inner_parts, (mix_dealt, conv_blocks) = pin(inner_parts, (tuple(mix_dealt), conv_blocks))
    grad_middle, own_branch, sums = call(
        functools.partial(branch_kernel, high),
        [((tok_rows, width), F32), ((tok_rows, width), BF), ((8, width), F32)],
        [],
        middle, vecs, grad_encoded, own_mixed, *inner_parts,
    )
    branches = plane_copies(own_branch)
    conv_blocks = after(tuple(conv_blocks), (own_branch,))
    conv_blocks = [conv_blocks[0]] + plane_swaps(conv_blocks)
    expand_blocks = chip_add(mix_dealt[low : 2 * low])
    reduce_sum = sum_list([mix_dealt[0]] + chip_swaps(mix_dealt[:low])).astype(BF)
    branches, (expand_blocks, reduce_sum) = pin(branches, (expand_blocks, reduce_sum))
    expand_blocks = [expand_blocks[0]] + plane_swaps(expand_blocks)
    reduce_line = Line(reduce_sum)
    dq, *dkvs = call(
        functools.partial(attend_back_kernel, high, low, head_dim),
        [((rows, span), BF), ((rows, 2 * span), F32)] + [((rows, 2 * span), BF)] * (low - 1),
        [],
        q, crop_q, crop_k, log_total, out_w, *branches, *kvs,
    )
    dkvs = [dkvs[0]] + chip_swaps(dkvs)
    out_dealt = call(
        functools.partial(output_grad_kernel, high, low),
        [((shard, width), BF)] * low,
        [((span, width), F32)],
        info, *attended, *branches, smem=1,
    )
    dkvs, (expand_blocks, reduce_line.got) = pin(dkvs, (expand_blocks, reduce_line.got))
    reduce_line.step()
    expand_line = Line(jnp.concatenate(expand_blocks, axis=0))
    expand_bias_part = mix_dealt[-1].reshape(low, hid_shard // shard, shard)
    expand_bias_part = expand_bias_part.transpose(1, 0, 2).reshape(hid_shard // shard, span)
    joint_outs = call(
        functools.partial(joint_back_kernel, high, low),
        partial_kinds + [((high, shard, wide), BF)] * low,
        [((rows, wide), BF), ((width, wide), F32)],
        info, dq, normed, joint_w, vecs, sums, expand_bias_part, *dkvs, *all_tokens, smem=1,
    )
    normed_parts, joint_dealt = joint_outs[:high], joint_outs[high:]

    blocks = chip_add(joint_dealt)
    output_sum = sum_list([out_dealt[0]] + chip_swaps(out_dealt)).astype(BF)
    blocks, (conv_blocks, reduce_line.got, output_sum) = pin(
        blocks, (conv_blocks, reduce_line.got, output_sum)
    )
    reduce_line.step()
    blocks = [blocks[0]] + plane_swaps(blocks)
    conv_sum = sum_list(conv_blocks).astype(BF)
    conv_sum, output_sum = lax.psum((conv_sum, output_sum), "batch")
    blocks, (reduce_line.got, expand_line.got) = pin(blocks, (reduce_line.got, expand_line.got))
    reduce_line.step()
    expand_line.step()
    normed_parts = [normed_parts[0]] + plane_swaps(normed_parts)
    if by_place:
        pieces = call(select_kernel, [((shard, wide), BF)] * nb, [], info, *blocks, smem=1)
        pieces = [pieces[0]] + [swap(pieces[t], "batch", t) for t in range(1, nb)]
        pieces, (expand_line.got, normed_parts) = pin(pieces, (expand_line.got, normed_parts))
        expand_line.step()
        own = sum_list(pieces).astype(BF)
        blocks = [own] + [swap(own, "batch", t) for t in range(1, nb)]
    else:
        summed = batch_sum(jnp.concatenate(blocks, axis=0)).astype(BF)
        blocks = [summed[m * shard : (m + 1) * shard] for m in range(high)]
        expand_line.step()
    tokens_grad = call(
        functools.partial(tokens_kernel, high),
        [((tok_rows, width), F32)],
        [],
        grad_middle, own_tokens, vecs, *normed_parts,
    )[0]
    blocks, (expand_line.got, tokens_grad) = pin(blocks, (expand_line.got, tokens_grad))
    expand_line.step()
    joint_grad, vec_grads = call(
        functools.partial(joint_final_kernel, high),
        [((shard, 3 * width), F32), ((16, shard), F32)],
        [],
        info, *blocks, smem=1,
    )
    reduce_sum, expand_sum = reduce_line.total(), expand_line.total()
    expand_grad = call(
        functools.partial(expand_final_kernel, high),
        [((shard, hidden), F32)],
        [],
        info, expand_sum, smem=1,
    )[0]
    part_two = kernel_second.shape[0]
    cut = part_two + residual_weight.shape[0]
    one_end = cut + cut_one + 8 * shard
    two_sum, one_sum = conv_sum[:cut].astype(F32), conv_sum[cut:one_end].astype(F32)
    upsample_grad = one_sum[cut_one:].reshape(8, shard, channels).transpose(1, 0, 2)
    return (
        decoded[None],
        tokens_grad[None],
        skip_grad[None],
        vec_grads[0],
        vec_grads[1],
        joint_grad,
        vec_grads[2],
        vec_grads[3],
        output_sum.astype(F32),
        vec_grads[4],
        vec_grads[5],
        vec_grads[6],
        expand_grad,
        vec_grads[8 : 8 + hid_shard // shard].reshape(hid_shard),
        reduce_sum.astype(F32),
        vec_grads[7],
        upsample_grad.reshape(shard, 8 * channels),
        one_sum[:cut_one],
        two_sum[:part_two],
        two_sum[part_two:],
    )


def solution(mesh):
    rows = P("batch", "seq", None)
    vec = P("seq")
    mat = P("seq", None)
    in_specs = (rows, rows, rows, P("batch", None))
    in_specs += (vec, vec, mat, vec, vec, mat, vec, vec, vec, mat, vec, mat, vec)
    in_specs += (mat, mat, mat, mat)
    out_specs = (rows, rows, rows)
    out_specs += (vec, vec, mat, vec, vec, mat, vec, vec, vec, mat, vec, mat, vec)
    out_specs += (mat, mat, mat, mat)
    return jax.shard_map(
        on_device, mesh=mesh, in_specs=in_specs, out_specs=out_specs, check_vma=False
    )
```

```python
import functools
import math

import jax
import jax.numpy as jnp
from jax import lax
from jax.experimental import pallas as pl
from jax.experimental.pallas import tpu as pltpu
from jax.sharding import PartitionSpec as P

HEADS = 12
PH = 4
CROPS = 4


LIMITS = {
    "attend_back_kernel": 60,
    "joint_back_kernel": 60,
    "attend_kernel": 22,
    "tap_grad_kernel": 18,
}
EPS_LAYER = 1e-06
EPS_CROP = 1e-05
BF = jnp.bfloat16
F32 = jnp.float32


def crops_of(lengths, indices):
    crop_ends = jnp.cumsum(lengths)
    return jnp.sum((indices[:, None] >= crop_ends[None, :]).astype(jnp.int32), axis=1)


def swap(values, axis, mask):
    count = lax.axis_size(axis)
    return lax.ppermute(values, axis, [(i, i ^ mask) for i in range(count)])


def gather_rel(values, axis, stride, count):
    return jnp.stack([values] + [swap(values, axis, m * stride) for m in range(1, count)])


def pick(blocks, index):
    return lax.dynamic_index_in_dim(blocks, index, 0, keepdims=False)


def unxor(blocks, index):
    count = blocks.shape[0]
    bits = count.bit_length() - 1
    tail = blocks.shape[1:]
    cube = blocks.reshape((2,) * bits + tail)
    for bit in range(bits):
        dim = bits - 1 - bit
        cube = jnp.where(((index >> bit) & 1) == 1, jnp.flip(cube, dim), cube)
    return cube.reshape(blocks.shape)


def deal_rel(blocks, axis, stride, index):
    count = blocks.shape[0]
    return [pick(blocks, index)] + [
        swap(pick(blocks, index ^ m), axis, m * stride) for m in range(1, count)
    ]


def sum_list(parts):
    total = parts[0].astype(F32)
    for part in parts[1:]:
        total = total + part.astype(F32)
    return total


def batch_sum(values):
    count = lax.axis_size("batch")
    if count == 1:
        return values.astype(F32)
    index = lax.axis_index("batch")
    rows = values.shape[0]
    piece = -(-rows // count)
    if piece * count > rows:
        values = jnp.pad(values, ((0, piece * count - rows), (0, 0)))
    pieces = values.reshape((count, piece) + values.shape[1:])
    own = sum_list(deal_rel(pieces, "batch", 1, index)).astype(BF)
    total = unxor(gather_rel(own, "batch", 1, count), index)
    return total.reshape(values.shape)[:rows].astype(F32)


def call(kernel, outs, scratch, *args, smem=0):
    name = getattr(kernel, "func", kernel).__name__
    limit = LIMITS.get(name, 12)
    return pl.pallas_call(
        kernel,
        out_shape=tuple(jax.ShapeDtypeStruct(shape, kind) for shape, kind in outs),
        in_specs=[pl.BlockSpec(memory_space=pltpu.SMEM)] * smem
        + [pl.BlockSpec(memory_space=pltpu.VMEM)] * (len(args) - smem),
        scratch_shapes=[pltpu.VMEM(shape, kind) for shape, kind in scratch],
        compiler_params=pltpu.CompilerParams(vmem_limit_bytes=limit * 1024 * 1024),
        name=name,
    )(*args)


GRID = 2 * PH
CELLS = GRID * GRID
ERF_TOP = (
    0.00022905065861350646,
    0.0034082910107109506,
    0.050955695062380861,
    0.18520832239976145,
    1.128379143519084,
)
ERF_LOW = (
    -1.1791602954361697e-7,
    0.000023547966471313185,
    0.0010179625278914885,
    0.014070470171167667,
    0.11098505178285362,
    0.49746925110067538,
    1.0,
)


def normal_cdf(values):
    arg = jnp.clip(values * math.sqrt(0.5), -3.832506856900711, 3.832506856900711)
    square = arg * arg
    top = jnp.full_like(square, ERF_TOP[0])
    for coef in ERF_TOP[1:]:
        top = top * square + coef
    bottom = jnp.full_like(square, ERF_LOW[0])
    for coef in ERF_LOW[1:]:
        bottom = bottom * square + coef
    return 0.5 + 0.5 * (arg * top / bottom)


def gelu_slope(values, cdf):
    return cdf + values * (jnp.exp(-0.5 * values * values) * (1.0 / math.sqrt(2.0 * math.pi)))


def depth_shifts(cells, prev, following, up, down):
    half = cells.shape[1] // 2
    even, odd = cells[:, :half], cells[:, half:]
    row = lax.broadcasted_iota(jnp.int32, even.shape, 1)
    ahead = jnp.where(row == half - 1, following[:, None, :], pltpu.roll(even, half - 1, 1))
    behind = jnp.where(row == 0, prev[:, None, :], pltpu.roll(odd, 1, 1))
    return (
        jnp.concatenate([behind * down[None], even], axis=1),
        jnp.concatenate([odd, ahead * up[None]], axis=1),
    )


def flat_rows(cells):
    return cells.reshape(cells.shape[0] * cells.shape[1], cells.shape[2])


def deep(rows):
    return rows.reshape(CELLS, rows.shape[0] // CELLS, rows.shape[1])


def tap_add(acc_ref, field, tap, sign):
    step_i, step_j = sign * (tap // 3 - 1), sign * (tap % 3 - 1)
    depth = acc_ref.shape[2]
    field = field.reshape(GRID, GRID, depth, field.shape[1])
    low_i, high_i = max(0, -step_i), GRID - max(0, step_i)
    low_j, high_j = max(0, -step_j), GRID - max(0, step_j)
    acc_ref[low_i:high_i, low_j:high_j] += field[
        low_i + step_i : high_i + step_i, low_j + step_j : high_j + step_j
    ]


def conv_into(acc_ref, stack, weight_ref, in_chans):
    taps = [4, 0, 1, 2, 3, 5, 6, 7, 8]

    def matrix(tap):
        return jnp.concatenate(
            [
                weight_ref[(layer * 9 + tap) * in_chans : (layer * 9 + tap + 1) * in_chans, :]
                for layer in range(3)
            ],
            axis=0,
        )

    out = weight_ref.shape[1]
    acc_ref[...] = jnp.zeros_like(acc_ref)
    for start in range(0, 9, 2):
        pair = taps[start : start + 2]
        rhs = jnp.concatenate([matrix(tap) for tap in pair], axis=1)
        field = jnp.dot(stack, rhs, preferred_element_type=F32)
        for place, tap in enumerate(pair):
            tap_add(acc_ref, field[:, place * out : (place + 1) * out], tap, 1)


def turned_into(acc_ref, stack, weight_ref, in_chans):
    taps = [4, 0, 1, 2, 3, 5, 6, 7, 8]

    def matrix(tap):
        return jnp.concatenate(
            [
                weight_ref[(layer * 9 + tap) * in_chans : (layer * 9 + tap + 1) * in_chans, :]
                for layer in (2, 1, 0)
            ],
            axis=1,
        )

    acc_ref[...] = jnp.zeros_like(acc_ref)
    step = max(1, 256 // in_chans)
    for start in range(0, 9, step):
        pair = taps[start : start + step]
        rhs = jnp.concatenate([matrix(tap) for tap in pair], axis=0)
        field = lax.dot_general(
            stack, rhs, (((1,), (1,)), ((), ())), preferred_element_type=F32
        )
        for place, tap in enumerate(pair):
            tap_add(acc_ref, field[:, place * in_chans : (place + 1) * in_chans], tap, -1)


def send_slabs(values_ref, parity, even_ref, odd_ref):
    depth = values_ref.shape[0] // CELLS
    top = values_ref[pl.ds(depth - 1, CELLS, stride=depth), :]
    bottom = values_ref[pl.ds(0, CELLS, stride=depth), :]
    even_ref[...] = jnp.where(parity == 0, top, bottom)
    odd_ref[...] = jnp.where(parity == 0, bottom, top)


def place_slabs(parity, from_even, from_odd):
    return (
        jnp.where(parity == 0, from_odd, from_even),
        jnp.where(parity == 0, from_even, from_odd),
    )


def spread(onehot_ref, per_crop):
    total = onehot_ref[0] * per_crop[0:1]
    for crop in range(1, CROPS):
        total = total + onehot_ref[crop] * per_crop[crop : crop + 1]
    return total


def crop_fold(onehot_ref, per_depth):
    return [
        jnp.sum(onehot_ref[crop] * per_depth, axis=0, keepdims=True) for crop in range(CROPS)
    ]


def moment_tile(onehot_ref, count_ref, cells, tile_ref):
    per_slice = float(cells.shape[0])
    sums = jnp.sum(cells, axis=0)
    about = cells - (sums * (1.0 / per_slice))[None]
    devs = jnp.sum(about * about, axis=0)
    totals = crop_fold(onehot_ref, sums)
    for crop in range(CROPS):
        mean = totals[crop] / jnp.maximum(count_ref[0, crop : crop + 1], 1.0)
        off = sums * (1.0 / per_slice) - mean
        tile_ref[crop : crop + 1] = totals[crop]
        tile_ref[CROPS + crop : CROPS + crop + 1] = jnp.sum(
            onehot_ref[crop] * (devs + per_slice * off * off), axis=0, keepdims=True
        )


def sum_tile(onehot_ref, first, second, tile_ref):
    for start, field in ((0, first), (CROPS, second)):
        totals = crop_fold(onehot_ref, jnp.sum(field, axis=0))
        for crop in range(CROPS):
            tile_ref[start + crop : start + crop + 1] = totals[crop]


def tile_list(tile_refs, high):
    tiles = [ref[...] for ref in tile_refs[:high]]
    for ref in tile_refs[high:]:
        tiles += [ref[8 * m : 8 * m + 8, :] for m in range(high)]
    return tiles


def merged_moments(tiles, count_ref, total_ref):
    total = total_ref[...]
    sums = tiles[0][:CROPS]
    devs = tiles[0][CROPS:]
    for tile in tiles[1:]:
        sums = sums + tile[:CROPS]
        devs = devs + tile[CROPS:]
    mean = sums / total
    for place, tile in enumerate(tiles):
        held = count_ref[place]
        off = tile[:CROPS] / jnp.maximum(held, 1.0) - mean
        devs = devs + held * off * off
    return mean, lax.rsqrt(devs / total + EPS_CROP)


def merged_sums(tiles, total_ref):
    both = tiles[0]
    for tile in tiles[1:]:
        both = both + tile
    total = total_ref[...]
    return both[:CROPS] / total, both[CROPS:] / total


def stack_rows(cells, prev, following, up, down):
    behind, ahead = depth_shifts(cells, prev, following, up, down)
    return [flat_rows(part).astype(BF) for part in (behind, cells, ahead)]


def up_kernel(
    high, slices, info, vec_ref, weight_ref, side_ref, *refs
):
    parts, (enc_ref, up_ref, even_ref, odd_ref, grid_ref) = refs[:high], refs[high:]
    encoded = (plane_total(parts) + vec_ref[7:8, :]).astype(BF)
    enc_ref[...] = encoded
    tok_rows = encoded.shape[0]
    plane = tok_rows // slices
    chans = up_ref.shape[1]
    ordered = jnp.dot(
        token_order(tok_rows, slices, False), encoded, preferred_element_type=F32
    ).astype(BF)
    rows = jnp.dot(ordered, weight_ref[...], preferred_element_type=F32)
    depth = 2 * slices
    for cell in range(plane):
        for place in range(8):
            part_a, part_b, part_e = place // 4, (place // 2) % 2, place % 2
            at = (2 * (cell // PH) + part_b) * GRID + 2 * (cell % PH) + part_e
            grid_ref[at * depth + part_a * slices : at * depth + (part_a + 1) * slices, :] = rows[
                cell * slices : (cell + 1) * slices, place * chans : (place + 1) * chans
            ]
    parity = info[0]
    top = grid_ref[pl.ds(depth - 1, CELLS, stride=depth), :]
    bottom = grid_ref[pl.ds(0, CELLS, stride=depth), :]
    even_ref[:, :chans] = jnp.where(parity == 0, top, bottom).astype(BF)
    odd_ref[:, :chans] = jnp.where(parity == 0, bottom, top).astype(BF)

    @pl.when(parity == 0)
    def _():
        even_ref[:, chans:] = side_ref[CELLS:, :]
        odd_ref[:, chans:] = side_ref[:CELLS, :]

    @pl.when(parity != 0)
    def _():
        even_ref[:, chans:] = side_ref[:CELLS, :]
        odd_ref[:, chans:] = side_ref[CELLS:, :]

    up_ref[...] = grid_ref[...].astype(BF)


def first_kernel(
    info, onehot, count_ref, masks, up_ref, from_even, from_odd, skip_ref,
    weight_ref, conv_ref, tile_ref, even_ref, odd_ref, stack_ref, halo_ref, acc_ref,
):
    parity = info[0]
    down, up = masks[0], masks[1]
    chans = up_ref.shape[1]
    up_halo = place_slabs(
        parity, from_even[:, :chans].astype(F32), from_odd[:, :chans].astype(F32)
    )
    skip_halo = place_slabs(
        parity,
        from_even[:, chans : 2 * chans].astype(F32),
        from_odd[:, chans : 2 * chans].astype(F32),
    )
    parts_up = stack_rows(deep(up_ref[...].astype(F32)), *up_halo, up, down)
    parts_skip = stack_rows(deep(skip_ref[...].astype(F32)), *skip_halo, up, down)
    for layer in range(3):
        at = 2 * layer * chans
        stack_ref[:, at : at + chans] = parts_up[layer]
        stack_ref[:, at + chans : at + 2 * chans] = parts_skip[layer]
    for side in range(2):
        halo_ref[side * CELLS : (side + 1) * CELLS, :chans] = up_halo[side].astype(BF)
        halo_ref[side * CELLS : (side + 1) * CELLS, chans:] = skip_halo[side].astype(BF)
    conv_into(acc_ref, stack_ref[...], weight_ref, 2 * chans)
    conv_ref[...] = acc_ref[...].reshape(conv_ref.shape)
    moment_tile(onehot, count_ref, deep(conv_ref[...]), tile_ref)
    send_slabs(conv_ref, parity, even_ref, odd_ref)


def second_kernel(
    high, info, onehot, count_ref, total_ref, masks, conv_one, odd_slab, weight_ref, *refs
):
    n_out = 8
    tiles, outs = refs[: -n_out - 1], refs[-n_out - 1 :]
    conv_ref, tile_ref, even_ref, odd_ref, stack_ref, unit_ref, slab_unit_ref, scale_ref, acc_ref = outs
    parity = info[0]
    down, up = masks[0], masks[1]
    mean, inv = merged_moments(tile_list(tiles, high), count_ref, total_ref)
    mean_z, inv_z = spread(onehot, mean), spread(onehot, inv)
    scale_ref[0] = mean_z
    scale_ref[1] = inv_z
    unit = (deep(conv_one[...]) - mean_z[None]) * inv_z[None]
    unit_ref[...] = flat_rows(unit)
    act = unit * normal_cdf(unit)
    halo = place_slabs(parity, tiles[high][8 * high :, :], odd_slab[...])
    depth = mean_z.shape[0]
    sides = []
    for side, at in ((0, 0), (1, depth - 1)):
        part = (halo[side] - mean_z[at : at + 1]) * inv_z[at : at + 1]
        slab_unit_ref[side * CELLS : (side + 1) * CELLS, :] = part
        sides.append(part * normal_cdf(part))
    parts = stack_rows(act, sides[0], sides[1], up, down)
    chans = conv_one.shape[1]
    for layer in range(3):
        stack_ref[:, layer * chans : (layer + 1) * chans] = parts[layer]
    conv_into(acc_ref, stack_ref[...], weight_ref, chans)
    conv_ref[...] = acc_ref[...].reshape(conv_ref.shape)
    moment_tile(onehot, count_ref, deep(conv_ref[...]), tile_ref)
    send_slabs(conv_ref, parity, even_ref, odd_ref)


def third_kernel(
    high, info, onehot, count_ref, total_ref, conv_two, odd_slab, stack_ref, halo_ref,
    weight_ref, cot_ref, cot_even, cot_odd, *refs
):
    n_out = 7
    tiles, outs = refs[:-n_out], refs[-n_out:]
    decoded_ref, grad_ref, low_ref, unit_ref, slab_ref, tile_ref, inv_ref = outs
    parity = info[0]
    chans = conv_two.shape[1]
    mean, inv = merged_moments(tile_list(tiles, high), count_ref, total_ref)
    mean_z, inv_z = spread(onehot, mean), spread(onehot, inv)
    inv_ref[...] = inv_z
    unit = flat_rows((deep(conv_two[...]) - mean_z[None]) * inv_z[None])
    unit_ref[...] = unit
    joined = stack_ref[:, 2 * chans : 4 * chans]
    summed = unit + jnp.dot(joined, weight_ref[...], preferred_element_type=F32)
    cdf = normal_cdf(summed)
    decoded_ref[...] = (summed * cdf).astype(BF)
    grad = cot_ref[...].astype(F32) * gelu_slope(summed, cdf)
    grad_ref[...] = grad
    low_ref[...] = grad.astype(BF)
    sum_tile(onehot, deep(grad), deep(grad * unit), tile_ref)
    halo = place_slabs(parity, tiles[high][8 * high :, :], odd_slab[...])
    cots = place_slabs(
        parity, cot_even[:, 2 * chans :].astype(F32), cot_odd[:, 2 * chans :].astype(F32)
    )
    depth = mean_z.shape[0]
    for side, at in ((0, 0), (1, depth - 1)):
        rows = slice(side * CELLS, (side + 1) * CELLS)
        part = (halo[side] - mean_z[at : at + 1]) * inv_z[at : at + 1]
        both = part + jnp.dot(halo_ref[rows, :], weight_ref[...], preferred_element_type=F32)
        slab_ref[rows, :chans] = part
        slab_ref[rows, chans:] = cots[side] * gelu_slope(both, normal_cdf(both))


def fourth_kernel(
    high, info, onehot, total_ref, masks, grad_ref, unit_two, inv_two, slab_two, unit_one,
    weight_ref, *refs
):
    n_out = 5
    tiles, outs = refs[: -n_out - 1], refs[-n_out - 1 :]
    second_ref, back_ref, tile_ref, even_ref, odd_ref, acc_ref = outs
    parity = info[0]
    down, up = masks[0], masks[1]
    chans = grad_ref.shape[1]
    first, cross = merged_sums(tile_list(tiles, high), total_ref)
    first_z, cross_z, inv_z = spread(onehot, first), spread(onehot, cross), inv_two[...]
    grad = deep(grad_ref[...]) - first_z[None] - deep(unit_two[...]) * cross_z[None]
    grad = grad * inv_z[None]
    depth = inv_z.shape[0]
    sides = []
    for side, at in ((0, 0), (1, depth - 1)):
        rows = slice(side * CELLS, (side + 1) * CELLS)
        part = slab_two[rows, chans:] - first_z[at : at + 1]
        part = part - slab_two[rows, :chans] * cross_z[at : at + 1]
        sides.append(part * inv_z[at : at + 1])
    parts = stack_rows(grad, sides[0], sides[1], up, down)
    second_ref[...] = parts[1]
    turned_into(acc_ref, jnp.concatenate(parts, axis=1), weight_ref, chans)
    unit = unit_one[...]
    back = acc_ref[...].reshape(back_ref.shape) * gelu_slope(unit, normal_cdf(unit))
    back_ref[...] = back
    sum_tile(onehot, deep(back), deep(back * unit), tile_ref)
    send_slabs(back_ref, parity, even_ref, odd_ref)


def fifth_kernel(
    high, slices, info, onehot, total_ref, masks, back_ref, unit_one, scale_one, slab_one,
    odd_slab, low_ref, weight_ref, resid_ref, up_weight_ref, *refs
):
    n_out = 5
    tiles, outs = refs[: -n_out - 1], refs[-n_out - 1 :]
    first_ref, skip_ref, rows_ref, encoded_ref, mixed_ref, acc_ref = outs
    parity = info[0]
    down, up = masks[0], masks[1]
    chans = back_ref.shape[1]
    first, cross = merged_sums(tile_list(tiles, high), total_ref)
    first_z, cross_z, inv_z = spread(onehot, first), spread(onehot, cross), scale_one[1]
    grad = deep(back_ref[...]) - first_z[None] - deep(unit_one[...]) * cross_z[None]
    grad = grad * inv_z[None]
    halo = place_slabs(parity, tiles[high][8 * high :, :], odd_slab[...])
    depth = inv_z.shape[0]
    sides = []
    for side, at in ((0, 0), (1, depth - 1)):
        rows = slice(side * CELLS, (side + 1) * CELLS)
        part = halo[side] - first_z[at : at + 1] - slab_one[rows, :] * cross_z[at : at + 1]
        sides.append(part * inv_z[at : at + 1])
    parts = stack_rows(grad, sides[0], sides[1], up, down)
    first_ref[...] = parts[1]
    turned_into(acc_ref, jnp.concatenate(parts, axis=1), weight_ref, 2 * chans)
    field = acc_ref[...].reshape(back_ref.shape[0], 2 * chans) + lax.dot_general(
        low_ref[...], resid_ref[...], (((1,), (1,)), ((), ())), preferred_element_type=F32
    )
    skip_ref[...] = field[:, chans:]
    plane = PH * PH
    columns = []
    for place in range(8):
        part_a, part_b, part_e = place // 4, (place // 2) % 2, place % 2
        pieces = []
        for cell in range(plane):
            at = (2 * (cell // PH) + part_b) * GRID + 2 * (cell % PH) + part_e
            low = at * depth + part_a * slices
            pieces.append(field[low : low + slices, :chans])
        columns.append(jnp.concatenate(pieces, axis=0))
    up_rows = jnp.concatenate(columns, axis=1).astype(BF)
    rows_ref[...] = jnp.dot(
        token_order(plane * slices, slices, True), up_rows, preferred_element_type=F32
    ).astype(BF)
    encoded = lax.dot_general(
        rows_ref[...], up_weight_ref[...], (((1,), (1,)), ((), ())), preferred_element_type=F32
    )
    encoded_ref[...] = encoded
    mixed_ref[...] = encoded.astype(BF)


def tap_grad_kernel(
    in_chans, high, low, wide, info, stack_ref, grad_ref, left_ref, right_ref, *refs
):
    outs, (turned_ref, pad_ref, rows_ref, extra_ref) = refs[:low], refs[low:]
    chans = grad_ref.shape[1]
    count = high * low
    shard = 27 * in_chans // count
    depth = grad_ref.shape[0] // CELLS
    pad_ref[...] = jnp.zeros_like(pad_ref)
    pad_ref[1 : GRID + 1, 1 : GRID + 1] = grad_ref[...].reshape(GRID, GRID, depth, chans)
    for tap in range(9):
        low_i, low_j = 2 - tap // 3, 2 - tap % 3
        moved = pad_ref[low_i : low_i + GRID, low_j : low_j + GRID]
        turned_ref[tap * chans : (tap + 1) * chans, :] = moved.reshape(-1, chans).T
    for layer in range(3):
        at = layer * in_chans
        product = jnp.dot(
            turned_ref[...], stack_ref[:, at : at + in_chans], preferred_element_type=F32
        )
        for tap in range(9):
            block = product[tap * chans : (tap + 1) * chans, :].T
            start = (layer * 9 + tap) * in_chans
            done = 0
            while done < in_chans:
                owner, place = divmod(start + done, shard)
                size = min(in_chans - done, shard - place)
                rows_ref[owner, place : place + size, :] = block[done : done + size, :]
                done += size
    extra = extra_ref.shape[1]
    left = left_ref[...]
    if wide == 1:
        left = left[:, 2 * chans : 4 * chans]
    extra_ref[...] = cross_rows(left, right_ref[...]).reshape(extra_ref.shape)
    for s in range(low):
        for m in range(high):
            owner = (info[1] ^ m) * low + (info[2] ^ s)
            outs[s][m, :shard, :] = rows_ref[owner][:shard].astype(BF)
            other = extra_ref[owner].astype(BF)
            for place in range(wide):
                start = shard + place * extra
                outs[s][m, start : start + extra, :] = other[
                    :, place * chans : (place + 1) * chans
                ]


def pack_kernel(high, info, token_ref, joint_ref, expand_ref, out_w_ref, *refs):
    vecs, joints, expands = refs[: -2 * high], refs[-2 * high : -high], refs[-high:]
    span = joint_ref.shape[1] // (3 * high)
    third = joint_ref.shape[1] // 3
    wide = expand_ref.shape[1] // high
    rows = token_ref.shape[0]
    shard = joint_ref.shape[0]
    lines = [ref[...] for ref in vecs]
    lines.append(jnp.zeros((128 - sum(line.shape[0] for line in lines), shard), F32))
    columns = jnp.concatenate(lines, axis=0).T[:, :64].astype(BF)
    top = 3 * span + 64
    for own in range(high):

        @pl.when(info[1] == own)
        def _():
            for m in range(high):
                group = own ^ m
                joints[m][:rows, :] = token_ref[...]
                for part in range(3):
                    joints[m][rows:, part * span : (part + 1) * span] = joint_ref[
                        :, part * third + group * span : part * third + (group + 1) * span
                    ]
                joints[m][rows:, 3 * span : top] = columns
                if top < joints[m].shape[1]:
                    joints[m][rows:, top:] = jnp.zeros(
                        (joint_ref.shape[0], joints[m].shape[1] - top), BF
                    )
                expands[m][0] = expand_ref[:, group * wide : (group + 1) * wide]
                expands[m][1] = out_w_ref[...]


def assembled(info, high, low, natural, parts, scratch_ref):
    rows = scratch_ref.shape[1]
    for s in range(low):
        for m in range(high):
            block = parts[m][...] if s == 0 else parts[high + s - 1][m * rows : (m + 1) * rows, :]
            major = (info[1] ^ m) if natural else m
            scratch_ref[major * low + (info[2] ^ s)] = block.astype(F32)


def order_kernel(high, low, natural, info, *refs):
    parts, out_ref, scratch_ref = refs[:-2], refs[-2], refs[-1]
    assembled(info, high, low, natural, parts, scratch_ref)
    out_ref[...] = scratch_ref[...].reshape(out_ref.shape).astype(BF)


def pair_kernel(high, low, info, *refs):
    parts, (expand_ref, out_ref, scratch_ref) = refs[:-3], refs[-3:]
    for slab, natural, place in ((0, True, expand_ref), (1, False, out_ref)):
        for s in range(low):
            for m in range(high):
                block = parts[m][slab] if s == 0 else parts[high + s - 1][m, slab]
                major = (info[1] ^ m) if natural else m
                scratch_ref[major * low + (info[2] ^ s)] = block.astype(F32)
        place[...] = scratch_ref[...].reshape(place.shape).astype(BF)


def unit_rows_of(values):
    average = jnp.mean(values, axis=-1, keepdims=True)
    centred = values - average
    inv_std = lax.rsqrt(jnp.mean(centred * centred, axis=-1, keepdims=True) + EPS_LAYER)
    return centred * inv_std, inv_std


def query_kernel(high, low, info, *refs):
    tokens, partners = refs[:high], refs[high : high + low - 1]
    q_ref, kv_ref, normed_ref, weight_ref, vec_ref, own_vec_ref, scratch_ref = refs[-7:]
    width = normed_ref.shape[1]
    wide = weight_ref.shape[1]
    span = q_ref.shape[1]
    rows = normed_ref.shape[0] // (2 * high)
    own_parts = [ref.at[rows:, :wide] for ref in tokens]
    assembled(info, high, low, True, own_parts + list(partners), scratch_ref)
    weight = scratch_ref[...].reshape(width, wide)
    weight_ref[...] = weight.astype(BF)
    turned = weight[:, wide - 128 :].T
    vec_ref[...] = turned[64:80, :]
    own = scratch_ref[pl.ds(info[1] * low, low), :, :][:, :, wide - 128 :]
    own_turned = own.reshape(width // high, 128).T
    own_vec_ref[...] = own_turned[64:80, :]
    gain, shift = turned[64:65, :], turned[65:66, :]
    for m in range(high):
        unit, _ = unit_rows_of(tokens[m][:rows, :].astype(F32))
        normed_ref[m * rows : (m + 1) * rows, :] = (unit * gain + shift).astype(BF)
        normed_ref[(high + m) * rows : (high + m + 1) * rows, :] = unit.astype(BF)
    joint = jnp.dot(
        normed_ref[: high * rows, :], weight_ref[...], preferred_element_type=F32
    )
    q_ref[...] = (joint[:, :span] + own_turned[66:67, :]).astype(BF)
    kv_ref[:, :span] = joint[:, span : 2 * span].astype(BF)
    kv_ref[:, span:] = (joint[:, 2 * span : 3 * span] + own_turned[67:68, :]).astype(BF)


def head_columns(refs, start, head_dim):
    return jnp.concatenate([ref[:, start : start + head_dim] for ref in refs], axis=0)


def masked_scores(keys, queries, same):
    scores = lax.dot_general(
        keys, queries, (((1,), (1,)), ((), ())), preferred_element_type=F32
    )
    return jnp.where(same, scores, -1000000000.0)


def attend_kernel(high, head_dim, q_ref, crop_q, crop_k, *refs):
    kvs, outs = refs[: -high - 1], refs[-high - 1 :]
    log_ref = outs[-1]
    span = q_ref.shape[1]
    same = crop_k[...] == crop_q[...]
    scale = 1.0 / math.sqrt(head_dim)
    pieces = []
    for head in range(span // head_dim):
        at = head * head_dim
        queries = q_ref[:, at : at + head_dim] * jnp.asarray(scale, BF)
        scores = masked_scores(head_columns(kvs, at, head_dim), queries, same)
        highest = jnp.max(scores, axis=0, keepdims=True)
        powers = jnp.exp(scores - highest)
        sums = jnp.sum(powers, axis=0, keepdims=True)
        log_ref[head : head + 1, :] = highest + jnp.log(sums)
        share = (powers * (1.0 / sums)).astype(BF)
        values = head_columns(kvs, span + at, head_dim)
        pieces.append(jnp.dot(values.T, share, preferred_element_type=F32))
    attended = jnp.concatenate(pieces, axis=0).T.astype(BF)
    rows = outs[0].shape[0]
    for m in range(high):
        outs[m][...] = attended[m * rows : (m + 1) * rows, :]


def middle_kernel(high, token_ref, weight_ref, vec_ref, *refs):
    parts, (middle_ref, inner_ref) = refs[:high], refs[high:]
    span = parts[0].shape[1]
    middle = token_ref[...].astype(F32) + vec_ref[4:5, :]
    for m in range(high):
        middle = middle + jnp.dot(
            parts[m][...], weight_ref[m * span : (m + 1) * span, :], preferred_element_type=F32
        )
    middle_ref[...] = middle
    unit, _ = unit_rows_of(middle)
    inner_ref[...] = (unit * vec_ref[5:6, :] + vec_ref[6:7, :]).astype(BF)


def mix_kernel(high, middle_ref, expand_ref, reduce_ref, bias_ref, *refs):
    parts, outs = refs[:high], refs[high:]
    act_ref, slope_ref = outs[high], outs[high + 1]
    rows = parts[0].shape[0]
    for m in range(high):
        at = slice(m * rows, (m + 1) * rows)
        expanded = bias_ref[...] + jnp.dot(
            parts[m][...], expand_ref[...], preferred_element_type=F32
        )
        cdf = normal_cdf(expanded)
        act = (expanded * cdf).astype(BF)
        act_ref[at, :] = act
        slope_ref[at, :] = gelu_slope(expanded, cdf)
        mixed = jnp.dot(act, reduce_ref[...], preferred_element_type=F32)
        if m == 0:
            mixed = mixed + middle_ref[...]
        outs[m][...] = mixed.astype(outs[m].dtype)


def plane_total(parts):
    total = parts[0][...]
    for ref in parts[1:]:
        total = total + ref[...].astype(F32)
    return total


def token_order(tok_rows, slices, back):
    plane = tok_rows // slices
    row = lax.broadcasted_iota(jnp.int32, (tok_rows, tok_rows), 0)
    col = lax.broadcasted_iota(jnp.int32, (tok_rows, tok_rows), 1)
    if back:
        row, col = col, row
    return jnp.where(col == (row % slices) * plane + row // slices, 1.0, 0.0).astype(BF)


def mix_back_kernel(high, reduce_ref, expand_ref, slope_ref, *refs):
    parts, outs = refs[:high], refs[high:]
    grad_ref = outs[high]
    rows = parts[0].shape[0]
    for m in range(high):
        at = slice(m * rows, (m + 1) * rows)
        grad = lax.dot_general(
            parts[m][...], reduce_ref[...], (((1,), (1,)), ((), ())), preferred_element_type=F32
        )
        grad = (grad * slope_ref[at, :]).astype(BF)
        grad_ref[at, :] = grad
        back = lax.dot_general(
            grad, expand_ref[...], (((1,), (1,)), ((), ())), preferred_element_type=F32
        )
        outs[m][...] = back.astype(outs[m].dtype)


def cross_rows(first, second):
    return lax.dot_general(first, second, (((0,), (0,)), ((), ())), preferred_element_type=F32)


def deal_rows(info, high, low, scratch_ref, outs):
    shard = outs[0].shape[1]
    for s in range(low):
        for m in range(high):
            at = ((info[1] ^ m) * low + (info[2] ^ s)) * shard
            outs[s][m] = scratch_ref[pl.ds(pl.multiple_of(at, 8), shard), :].astype(BF)


def deal_chip(info, low, scratch_ref, outs):
    shard = outs[0].shape[0]
    for s in range(low):
        at = (info[2] ^ s) * shard
        outs[s][...] = scratch_ref[pl.ds(pl.multiple_of(at, 8), shard), :].astype(BF)


def mix_grad_kernel(high, low, info, act_ref, grad_ref, *refs):
    mixed = jnp.concatenate([ref[...] for ref in refs[:high]], axis=0)
    inner = jnp.concatenate([ref[...] for ref in refs[high : 2 * high]], axis=0)
    outs = refs[2 * high :]
    bias_ref, scratch_ref = outs[low], outs[low + 1]
    hid_shard = scratch_ref.shape[0] // low
    shard = (outs[0].shape[0] - hid_shard) // high
    scratch_ref[...] = cross_rows(inner, grad_ref[...])
    for s in range(low):
        for m in range(high):
            at = ((info[1] ^ m) * low + (info[2] ^ s)) * shard
            outs[s][m * shard : (m + 1) * shard, :] = scratch_ref[
                pl.ds(pl.multiple_of(at, 8), shard), :
            ].astype(BF)
    scratch_ref[...] = cross_rows(act_ref[...], mixed)
    for s in range(low):
        at = (info[2] ^ s) * hid_shard
        outs[s][high * shard :, :] = scratch_ref[
            pl.ds(pl.multiple_of(at, 8), hid_shard), :
        ].astype(BF)
    bias_ref[...] = jnp.sum(grad_ref[...].astype(F32), axis=0, keepdims=True)


def norm_back(upstream, unit, inv_std, gain):
    scaled = upstream * gain
    return inv_std * (
        scaled
        - jnp.mean(scaled, axis=-1, keepdims=True)
        - unit * jnp.mean(scaled * unit, axis=-1, keepdims=True)
    )


def branch_kernel(high, low, middle_ref, vec_ref, encoded_ref, mixed_ref, *refs):
    parts, dealt = refs[:high], refs[high : high + low]
    grad_ref, sums_ref, reduce_ref = refs[high + low : high + low + 3]
    outs = refs[high + low + 3 :]
    inner = plane_total(parts)
    unit, inv_std = unit_rows_of(middle_ref[...])
    grad = encoded_ref[...] + norm_back(inner, unit, inv_std, vec_ref[5:6, :])
    grad_ref[...] = grad
    branch = grad.astype(BF)
    rows = branch.shape[0]
    shard = outs[0].shape[0] - rows
    for m in range(high):
        outs[m][:rows, :] = branch
        total = dealt[0][m * shard : (m + 1) * shard, :].astype(F32)
        for ref in dealt[1:]:
            total = total + ref[m * shard : (m + 1) * shard, :].astype(F32)
        outs[m][rows:, :] = total.astype(BF)
    total = dealt[0][high * shard :, :].astype(F32)
    for ref in dealt[1:]:
        total = total + ref[high * shard :, :].astype(F32)
    reduce_ref[...] = total.astype(BF)
    sums_ref[...] = jnp.zeros_like(sums_ref)
    sums_ref[4:5, :] = jnp.sum(branch.astype(F32), axis=0, keepdims=True)
    sums_ref[5:6, :] = jnp.sum(inner * unit, axis=0, keepdims=True)
    sums_ref[6:7, :] = jnp.sum(inner, axis=0, keepdims=True)
    sums_ref[7:8, :] = jnp.sum(mixed_ref[...].astype(F32), axis=0, keepdims=True)


def attend_back_kernel(high, low, head_dim, q_ref, crop_q, crop_k, log_ref, weight_ref, *refs):
    branches, kvs = refs[:high], refs[high : high + low]
    outs = refs[high + low :]
    span = q_ref.shape[1]
    rows = q_ref.shape[0]
    branch = jnp.concatenate([ref[: rows // high, :] for ref in branches], axis=0)
    attended = lax.dot_general(
        branch, weight_ref[:span, :], (((1,), (1,)), ((), ())), preferred_element_type=F32
    ).astype(BF)
    same = crop_k[...] == crop_q[...]
    scale = 1.0 / math.sqrt(head_dim)
    pieces = []
    for head in range(span // head_dim):
        at = head * head_dim
        queries = q_ref[:, at : at + head_dim] * jnp.asarray(scale, BF)
        keys = head_columns(kvs, at, head_dim)
        values = head_columns(kvs, span + at, head_dim)
        grad_out = attended[:, at : at + head_dim]
        share = jnp.exp(masked_scores(keys, queries, same) - log_ref[head : head + 1, :])
        weights = lax.dot_general(
            values, grad_out, (((1,), (1,)), ((), ())), preferred_element_type=F32
        )
        row_dot = jnp.sum(share * weights, axis=0, keepdims=True)
        grad_scores = (share * (weights - row_dot)).astype(BF)
        grad_keys = jnp.dot(grad_scores, queries, preferred_element_type=F32)
        grad_values = jnp.dot(share.astype(BF), grad_out, preferred_element_type=F32)
        for s in range(low):
            part = slice(s * rows, (s + 1) * rows)
            low_at = at + span if s == 0 else at
            outs[s][:, low_at : low_at + head_dim] = grad_keys[part, :].astype(BF)
            outs[s][:, span + low_at : span + low_at + head_dim] = grad_values[part, :].astype(BF)
        pieces.append(jnp.dot(keys.T, grad_scores, preferred_element_type=F32) * scale)
    outs[0][:, :span] = jnp.concatenate(pieces, axis=0).T.astype(BF)


def output_grad_kernel(high, low, info, *refs):
    attended = jnp.concatenate([ref[...] for ref in refs[:high]], axis=0)
    rows = refs[0].shape[0]
    branch = jnp.concatenate([ref[:rows, :] for ref in refs[high : 2 * high]], axis=0)
    outs, scratch_ref = refs[2 * high : -1], refs[-1]
    scratch_ref[...] = cross_rows(attended, branch)
    deal_chip(info, low, scratch_ref, outs)


def joint_back_kernel(high, low, info, own_ref, normed_ref, weight_ref, vec_ref, sums_ref,
                      bias_ref, *refs):
    dkvs, outs = refs[: low - 1], refs[low - 1 :]
    joint_ref, scratch_ref = outs[-2], outs[-1]
    backs, dealt = outs[:high], outs[high : high + low]
    span = own_ref.shape[1] // 3
    joint_ref[...] = jnp.zeros_like(joint_ref)
    joint_ref[:, :span] = own_ref[:, :span]
    total = own_ref[:, span:].astype(F32)
    for ref in dkvs:
        total = total + ref[...].astype(F32)
    joint_ref[:, span : 3 * span] = total.astype(BF)
    rows = backs[0].shape[0]
    gain_sum, shift_sum = 0.0, 0.0
    for m in range(high):
        part = lax.dot_general(
            joint_ref[m * rows : (m + 1) * rows, :], weight_ref[...], (((1,), (1,)), ((), ())),
            preferred_element_type=F32,
        )
        backs[m][...] = part.astype(backs[m].dtype)
        unit = normed_ref[(high + m) * rows : (high + m + 1) * rows, :].astype(F32)
        gain_sum = gain_sum + jnp.sum(part * unit, axis=0, keepdims=True)
        shift_sum = shift_sum + jnp.sum(part, axis=0, keepdims=True)
    wide = joint_ref.shape[1]
    width = normed_ref.shape[1]
    scratch_ref[...] = cross_rows(normed_ref[: high * rows, :], joint_ref[...])
    whole = jnp.concatenate(
        [
            jnp.zeros((64, width), F32), gain_sum, shift_sum, sums_ref[2:8, :],
            jnp.zeros((56, width), F32),
        ],
        axis=0,
    )
    scratch_ref[:, wide - 128 :] += whole.T
    sums = jnp.sum(joint_ref[...].astype(F32), axis=0, keepdims=True)
    own = jnp.concatenate(
        [
            jnp.zeros((66, span), F32), sums[:, :span], sums[:, 2 * span : 3 * span],
            jnp.zeros((4, span), F32), bias_ref[...],
            jnp.zeros((56 - bias_ref.shape[0], span), F32),
        ],
        axis=0,
    )
    at = pl.multiple_of(info[1] * span, 8)
    scratch_ref[pl.ds(at, span), wide - 128 :] += own.T
    deal_rows(info, high, low, scratch_ref, dealt)


def chip_add_kernel(high, low, *refs):
    parts, outs = refs[:-high], refs[-high:]
    for m in range(high):
        done = 0
        for start in range(0, len(parts), low):
            total = parts[start][m].astype(F32)
            for ref in parts[start + 1 : start + low]:
                total = total + ref[m].astype(F32)
            outs[m][done : done + total.shape[0], :] = total.astype(BF)
            done += total.shape[0]
        if done < outs[m].shape[0]:
            outs[m][done:, :] = jnp.zeros((outs[m].shape[0] - done, outs[m].shape[1]), BF)


def side_pack_kernel(high, low, info, *refs):
    joints, convs, outputs = refs[:high], refs[high : 2 * high], refs[2 * high : 2 * high + low]
    pieces, pack_ref = refs[2 * high + low : -1], refs[-1]
    chans = pack_ref.shape[1]
    rows, done = joints[0].shape[0], 0
    for m in range(high):
        for at in range(0, joints[m].shape[1], chans):
            pack_ref[done : done + rows, :] = joints[m][:, at : at + chans].astype(F32)
            done += rows
    total = convs[0][...].astype(F32)
    for ref in convs[1:]:
        total = total + ref[...].astype(F32)
    pack_ref[done : done + total.shape[0], :] = total
    done += total.shape[0]
    total = outputs[0][...].astype(F32)
    for ref in outputs[1:]:
        total = total + ref[...].astype(F32)
    for at in range(0, total.shape[1], chans):
        pack_ref[done : done + rows, :] = total[:, at : at + chans]
        done += rows
    if done < pack_ref.shape[0]:
        pack_ref[done:, :] = jnp.zeros((pack_ref.shape[0] - done, chans), F32)
    size = pieces[0].shape[0]
    for t in range(len(pieces)):
        at = pl.multiple_of((info[3] ^ t) * size, 8)
        pieces[t][...] = pack_ref[pl.ds(at, size), :].astype(BF)


def mix_pack_kernel(high, rows, *refs):
    branches, reduce_ref, pack_ref = refs[:high], refs[high], refs[high + 1]
    done = 0
    for ref in branches:
        size = ref.shape[0] - rows
        pack_ref[done : done + size, :] = ref[rows:, :]
        done += size
    pack_ref[done:, :] = reduce_ref[...]


def joined_halves(upper, own_ref, other_ref, whole_ref):
    half = own_ref.shape[0]
    whole_ref[:half, :] = jnp.where(upper, other_ref[...], own_ref[...]).astype(F32)
    whole_ref[half:, :] = jnp.where(upper, own_ref[...], other_ref[...]).astype(F32)


def side_final_kernel(high, info, *refs):
    joint_ref, vec_ref, out_ref, up_ref, one_ref, two_ref, resid_ref, whole_ref = refs[-8:]
    pieces = refs[:-8]
    size = pieces[0].shape[0]
    for t in range(len(pieces)):
        at = pl.multiple_of((info[3] ^ t) * size, 8)
        whole_ref[pl.ds(at, size), :] = pieces[t][...].astype(F32)
    chans = whole_ref.shape[1]
    rows = joint_ref.shape[0]
    span = joint_ref.shape[1] // (3 * high)
    third = joint_ref.shape[1] // 3
    tiles = -(-(3 * span + 64) // chans)

    def block(m):
        return jnp.concatenate(
            [
                whole_ref[(m * tiles + j) * rows : (m * tiles + j + 1) * rows, :]
                for j in range(tiles)
            ],
            axis=1,
        )

    for place in range(high):

        @pl.when(info[1] == place)
        def _():
            for group in range(high):
                values = block(place ^ group)
                for part in range(3):
                    at = part * third + group * span
                    joint_ref[:, at : at + span] = values[:, part * span : (part + 1) * span]

    total = block(0)[:, (tiles - 1) * chans :]
    for m in range(1, high):
        total = total + block(m)[:, (tiles - 1) * chans :]
    vec_ref[...] = total.T[64:80, :]
    done = high * tiles * rows
    for ref in (two_ref, resid_ref, one_ref):
        ref[...] = whole_ref[done : done + ref.shape[0], :]
        done += ref.shape[0]
    for at in range(0, up_ref.shape[1], chans):
        up_ref[:, at : at + chans] = whole_ref[done : done + rows, :]
        done += rows
    done = high * tiles * rows + -(-(done - high * tiles * rows) // 32) * 32
    for at in range(0, out_ref.shape[1], chans):
        out_ref[:, at : at + chans] = whole_ref[done : done + rows, :]
        done += rows


def mix_final_kernel(high, info, own_ref, other_ref, expand_ref, reduce_ref, whole_ref):
    joined_halves(info[4] == 1, own_ref, other_ref, whole_ref)
    wide = expand_ref.shape[1] // high
    rows = expand_ref.shape[0]
    for place in range(high):

        @pl.when(info[1] == place)
        def _():
            for group in range(high):
                m = place ^ group
                expand_ref[:, group * wide : (group + 1) * wide] = whole_ref[
                    m * rows : (m + 1) * rows, :
                ]

    reduce_ref[...] = whole_ref[high * rows :, :]


def tokens_kernel(high, grad_ref, token_ref, vec_ref, *refs):
    parts, out_ref = refs[:high], refs[high]
    unit, inv_std = unit_rows_of(token_ref[...].astype(F32))
    out_ref[...] = grad_ref[...] + norm_back(plane_total(parts), unit, inv_std, vec_ref[0:1, :])


def on_device(
    tokens,
    skip_features,
    out_grad,
    crop_lengths,
    attend_gain,
    attend_shift,
    joint_weight,
    query_bias,
    value_bias,
    output_weight,
    output_bias,
    mixer_gain,
    mixer_shift,
    expand_weight,
    expand_bias,
    reduce_weight,
    reduce_bias,
    upsample_weight,
    kernel_first,
    kernel_second,
    residual_weight,
):
    count = lax.axis_size("seq")
    nb = lax.axis_size("batch")
    high = math.gcd(HEADS, count)
    low = count // high
    seq_index = lax.axis_index("seq")
    batch_index = lax.axis_index("batch")
    hi = seq_index // low
    lo = seq_index % low
    width = tokens.shape[2]
    shard = joint_weight.shape[0]
    head_dim = width // HEADS
    span = HEADS // high * head_dim
    wide = -(-(3 * span + 64) // 128) * 128
    hidden = expand_weight.shape[1]
    hid_span = hidden // high
    hid_shard = hidden // count
    channels = residual_weight.shape[1]
    plane_size = PH * PH
    tok_rows = tokens.shape[1]
    rows = high * tok_rows
    slices = tok_rows // plane_size
    depth_total = 2 * slices
    positions = depth_total * 4 * plane_size
    lengths = crop_lengths[0]
    own_tokens = tokens[0]
    place = batch_index % 2 if nb == 4 else 0 * hi
    info = jnp.stack([seq_index % 2, hi, lo, batch_index, place]).astype(jnp.int32)

    def plane_swaps(blocks):
        return [swap(blocks[m], "seq", m * low) for m in range(1, high)]

    def plane_copies(block):
        return [block] + [swap(block, "seq", m * low) for m in range(1, high)]

    def gather_list(block):
        return [block] + [swap(block, "batch", t) for t in range(1, nb)]

    def chip_swaps(blocks):
        return [swap(blocks[s], "seq", s) for s in range(1, low)]

    def chip_copies(block):
        return [swap(block, "seq", s) for s in range(1, low)]

    def after(values, done):
        return lax.optimization_barrier((values, tuple(done)))[0]

    def owners(rel_hi, rel_lo):
        return (hi ^ rel_hi) * low + (lo ^ rel_lo)

    def odd_swap(values):
        pairs = [(i, i + 1) for i in range(1, count - 1, 2)]
        return lax.ppermute(values, "seq", pairs + [(j, i) for i, j in pairs])

    vectors = [
        attend_gain, attend_shift, query_bias, value_bias, output_bias, mixer_gain, mixer_shift,
        reduce_bias,
    ]
    vectors = [
        jnp.stack([vec.astype(F32) for vec in vectors]),
        expand_bias.astype(F32).reshape(hid_shard // shard, shard),
    ]
    packed = call(
        functools.partial(pack_kernel, high),
        [((tok_rows + shard, width), BF)] * high + [((2, shard, width), BF)] * high,
        [],
        info, own_tokens, joint_weight, expand_weight, output_weight, *vectors, smem=1,
    )
    all_tokens = list(packed[:1]) + plane_swaps(packed[:high])
    partners = chip_copies(jnp.concatenate([part[tok_rows:, :wide] for part in all_tokens], axis=0))
    q, kv, normed, joint_w, vecs, own_vecs = call(
        functools.partial(query_kernel, high, low),
        [((rows, span), BF), ((rows, 2 * span), BF), ((2 * rows, width), BF), ((width, wide), BF),
         ((16, width), F32), ((16, span), F32)],
        [((count, shard, wide), F32)],
        info, *all_tokens, *partners, smem=1,
    )
    kvs = [kv] + chip_copies(kv)

    def ordered(parts, natural, shape, block):
        kernel = functools.partial(order_kernel, block[0], low, natural)
        return call(
            kernel, [(shape, BF)], [((block[0] * low, block[1], shape[1]), F32)], info, *parts,
            smem=1,
        )[0]

    later_pairs = after(tuple(packed[high:]), all_tokens[1:])
    pairs = [later_pairs[0]] + plane_swaps(later_pairs)
    kvs, pairs[1] = lax.optimization_barrier((kvs, pairs[1]))
    expand_b = own_vecs[8 : 8 + hid_shard // shard].reshape(hid_shard // shard, low, shard)
    expand_b = expand_b.transpose(1, 0, 2).reshape(1, hid_span)
    later_up, later_conv = after(
        (upsample_weight, (kernel_first, kernel_second, residual_weight)), ()
    )
    upsample_w = lax.all_gather(later_up, "seq", axis=0, tiled=True)
    conv_all = lax.all_gather(
        jnp.concatenate(later_conv, axis=0), "seq", axis=0
    )
    cut_one = kernel_first.shape[0]
    cut_two = cut_one + kernel_second.shape[0]
    kernel_one = conv_all[:, :cut_one].reshape(-1, channels)
    kernel_two = conv_all[:, cut_one:cut_two].reshape(-1, channels)
    residual_w = conv_all[:, cut_two:].reshape(-1, channels)

    def token_crops(rel_lo):
        starts = jnp.stack([owners(m, rel_lo) for m in range(high)]) * slices
        ids = starts[:, None] + jnp.arange(tok_rows, dtype=jnp.int32)[None, :] // plane_size
        return crops_of(lengths, ids.reshape(-1))

    crop_q = token_crops(0).reshape(1, rows)
    crop_k = jnp.concatenate([token_crops(s) for s in range(low)]).reshape(low * rows, 1)
    *attended, log_total = call(
        functools.partial(attend_kernel, high, head_dim),
        [((tok_rows, span), BF)] * high + [((8, rows), F32)],
        [],
        q, crop_q, crop_k, *kvs,
    )
    arrived = [attended[0]] + plane_swaps(attended)
    pairs = list(after(tuple(pairs), (arrived[1],)))
    pairs += chip_copies(jnp.stack(pairs))
    expand_w, out_w = call(
        functools.partial(pair_kernel, high, low),
        [((width, hid_span), BF), ((width, width), BF)],
        [((count, shard, width), F32)],
        info, *pairs, smem=1,
    )
    middle, inner = call(
        functools.partial(middle_kernel, high),
        [((tok_rows, width), F32), ((tok_rows, width), BF)],
        [],
        own_tokens, out_w, vecs, *arrived,
    )
    inners = plane_copies(inner)
    reduces = [reduce_weight] + chip_copies(after(reduce_weight, (inner,)))
    reduce_w = ordered(reduces, False, (hid_span, width), (1, hid_shard))
    partial_kinds = [((tok_rows, width), F32)] + [((tok_rows, width), BF)] * (high - 1)
    *mixed, act, slope = call(
        functools.partial(mix_kernel, high),
        partial_kinds + [((rows, hid_span), BF), ((rows, hid_span), F32)],
        [],
        middle, expand_w, reduce_w, expand_b, *inners,
    )
    mixed = [mixed[0]] + plane_swaps(mixed)

    def to_cells(values):
        cells = values.reshape(slices, 2, CELLS, channels)
        return cells.transpose(2, 1, 0, 3).reshape(positions, channels)

    def from_cells(values):
        cells = values.reshape(CELLS, 2, slices, channels)
        return cells.transpose(2, 1, 0, 3).reshape(positions, channels)

    late_lengths, late_skip, late_cot = after((lengths, skip_features[0], out_grad[0]), (act,))
    slice_ids = seq_index * slices - 1 + jnp.arange(slices + 2, dtype=jnp.int32)
    crop_ids = jnp.where(slice_ids < 0, -1, crops_of(late_lengths, slice_ids))
    here = crop_ids[1:-1]
    masks = jnp.stack([crop_ids[:-2] == here, crop_ids[2:] == here]).astype(F32)
    masks = jnp.broadcast_to(masks[:, :, None], (2, slices, channels))
    onehot = (jnp.arange(CROPS, dtype=jnp.int32)[:, None] == here[None, :]).astype(F32)
    onehot = jnp.broadcast_to(
        jnp.tile(onehot, (1, 2))[:, :, None], (CROPS, depth_total, channels)
    )
    total = jnp.broadcast_to(
        (late_lengths * 8 * plane_size).astype(F32)[:, None], (CROPS, channels)
    )
    crop_ends = jnp.cumsum(late_lengths)
    dev_rel = jnp.stack([owners(m, s) for s in range(low) for m in range(high)])
    first = (dev_rel * slices)[:, None]
    shared = jnp.minimum(crop_ends[None], first + slices) - jnp.maximum(
        (crop_ends - late_lengths)[None], first
    )
    held = (jnp.maximum(shared, 0) * 8 * plane_size).astype(F32)
    held = jnp.broadcast_to(held[:, :, None], (count, CROPS, channels))
    skip_cells = to_cells(late_skip)
    cot_cells = to_cells(late_cot)
    sides = jnp.concatenate([late_skip, late_cot], axis=1)
    sides = jnp.concatenate([sides[:CELLS], sides[-CELLS:]], axis=0)
    prepared = (
        onehot, held, masks, total, skip_cells, cot_cells, sides, kernel_one, kernel_two,
        residual_w, upsample_w,
    )
    mixed[1], prepared = lax.optimization_barrier((mixed[1], prepared))
    onehot, held, masks, total, skip_cells, cot_cells, sides = prepared[:7]
    kernel_one, kernel_two, residual_w, upsample_w = prepared[7:]

    cells_bf = ((positions, channels), BF)
    cells_f = ((positions, channels), F32)
    slab_f = ((CELLS, channels), F32)
    slab_bf = ((CELLS, 3 * channels), BF)
    slabs_f = ((2 * CELLS, channels), F32)
    tile = ((2 * CROPS, channels), F32)
    grid_acc = ((GRID, GRID, depth_total, channels), F32)

    def exchange(own_tile, even_slab=None, odd_slab=None):
        tiles = plane_copies(own_tile)
        if even_slab is None:
            return tiles + chip_copies(jnp.concatenate(tiles, axis=0)), None
        odd_slab = odd_swap(odd_slab)
        even_slab, odd_slab = lax.optimization_barrier((even_slab, odd_slab))
        return tiles + chip_copies(jnp.concatenate(tiles + [even_slab], axis=0)), odd_slab

    encoded, upsampled, up_even, up_odd = call(
        functools.partial(up_kernel, high, slices),
        [((tok_rows, width), BF), cells_bf, slab_bf, slab_bf],
        [cells_f],
        info, vecs, upsample_w, sides, *mixed, smem=1,
    )
    up_even, up_odd = swap(up_even, "seq", 1), odd_swap(up_odd)
    first_conv, tile_one, even_one, odd_one, joined_stack, joined_halo = call(
        first_kernel,
        [cells_f, tile, slab_f, slab_f, ((positions, 6 * channels), BF),
         ((2 * CELLS, 2 * channels), BF)],
        [grid_acc],
        info, onehot, held, masks, upsampled, up_even, up_odd, skip_cells,
        kernel_one, smem=1,
    )
    tiles, odd_one = exchange(tile_one, even_one, odd_one)
    (second_conv, tile_two, even_two, odd_two, act_stack, first_unit, slab_unit, scale_one) = call(
        functools.partial(second_kernel, high),
        [cells_f, tile, slab_f, slab_f, ((positions, 3 * channels), BF), cells_f, slabs_f,
         ((2, depth_total, channels), F32)],
        [grid_acc],
        info, onehot, held, total, masks, first_conv, odd_one, kernel_two, *tiles, smem=1,
    )
    tiles, odd_two = exchange(tile_two, even_two, odd_two)
    decoded_cells, grad_summed, grad_resid, second_unit, slab_two, tile_three, inv_two = call(
        functools.partial(third_kernel, high),
        [cells_bf, cells_f, cells_bf, cells_f, ((2 * CELLS, 2 * channels), F32), tile,
         ((depth_total, channels), F32)],
        [],
        info, onehot, held, total, second_conv, odd_two, joined_stack, joined_halo,
        residual_w, cot_cells, up_even, up_odd, *tiles, smem=1,
    )
    decoded = from_cells(decoded_cells)
    tiles, _ = exchange(tile_three)
    grad_second, grad_back, tile_four, even_four, odd_four = call(
        functools.partial(fourth_kernel, high),
        [cells_bf, cells_f, tile, slab_f, slab_f],
        [grid_acc],
        info, onehot, total, masks, grad_summed, second_unit, inv_two, slab_two, first_unit,
        kernel_two, *tiles, smem=1,
    )

    def tap_grad(stack, upstream, in_chans, left, right, wide_blocks, extra_shape):
        part = 27 * in_chans // count
        extra = extra_shape[0] // count
        dealt = call(
            functools.partial(tap_grad_kernel, in_chans, high, low, wide_blocks),
            [((high, part + wide_blocks * extra, channels), BF)] * low,
            [((9 * channels, positions), BF),
             ((GRID + 2, GRID + 2, depth_total, channels), BF),
             ((count, -(-part // 8) * 8, channels), F32),
             ((count, extra, extra_shape[1]), F32)],
            info, stack, upstream, left, right, smem=1,
        )
        return dealt

    def chip_add(*groups):
        held = sum(group[0].shape[1] for group in groups)
        held = -(-held // 32) * 32 if len(groups) > 1 else held
        kind = [((held, groups[0][0].shape[2]), BF)] * high
        parts = [part for group in groups for part in group]
        return call(functools.partial(chip_add_kernel, high, low), kind, [], *parts)

    class Cube:
        def __init__(self, values):
            self.stage, self.values = 0, values
            if nb == 4:
                self.got = self.split(batch_index % 2, 1)
            else:
                whole = lax.psum(values, "batch")
                half = whole.shape[0] // 2
                self.values, self.got = whole[:half], whole[half:]

        def split(self, bit, mask):
            half = self.values.shape[0] // 2
            sent = lax.dynamic_slice_in_dim(self.values, (1 - bit) * half, half)
            self.values = lax.dynamic_slice_in_dim(self.values, bit * half, half)
            return swap(sent, "batch", mask)

        def step(self):
            if nb != 4:
                return
            self.stage += 1
            if self.stage < 3:
                self.values = sum_list([self.values, self.got]).astype(BF)
            if self.stage == 1:
                self.got = self.split(batch_index // 2, 2)
            elif self.stage == 2:
                self.got = swap(self.values, "batch", 2)
            else:
                self.values = jnp.where(
                    batch_index // 2 == 1,
                    jnp.concatenate([self.got, self.values], axis=0),
                    jnp.concatenate([self.values, self.got], axis=0),
                )
                self.got = swap(self.values, "batch", 1)

    tiles, odd_four = exchange(tile_four, even_four, odd_four)
    two_dealt = tap_grad(
        act_stack, grad_second, channels, joined_stack, grad_resid, 1, (2 * channels, channels)
    )
    tiles = after(tuple(tiles), two_dealt)
    grad_first, skip_cells_grad, grad_up_rows, grad_encoded, own_mixed = call(
        functools.partial(fifth_kernel, high, slices),
        [cells_bf, cells_f, ((tok_rows, 8 * channels), BF), ((tok_rows, width), F32),
         ((tok_rows, width), BF)],
        [((GRID, GRID, depth_total, 2 * channels), F32)],
        info, onehot, total, masks, grad_back, first_unit, scale_one, slab_unit, odd_four,
        grad_resid, kernel_one, residual_w, upsample_w, *tiles, smem=1,
    )
    skip_grad = from_cells(skip_cells_grad)

    def pin(first, second):
        if not isinstance(first, (list, tuple)):
            return lax.optimization_barrier((first, second))
        last, second = lax.optimization_barrier((first[-1], second))
        return list(first[:-1]) + [last], second

    grads_mixed = plane_copies(own_mixed)
    two_dealt = [two_dealt[0]] + chip_swaps(two_dealt)
    one_dealt = list(tap_grad(
        joined_stack, grad_first, 2 * channels, encoded, grad_up_rows, 8, (width, 8 * channels)
    ))
    grads_mixed, (one_dealt[0], two_dealt[1]) = pin(grads_mixed, (one_dealt[0], two_dealt[1]))
    *inner_parts, grad_expanded = call(
        functools.partial(mix_back_kernel, high),
        partial_kinds + [((rows, hid_span), BF)],
        [],
        reduce_w, expand_w, slope, *grads_mixed,
    )
    inner_parts = [inner_parts[0]] + plane_swaps(inner_parts)
    *mix_dealt, expand_bias_part = call(
        functools.partial(mix_grad_kernel, high, low),
        [((high * shard + hid_shard, width), BF)] * low + [((1, hid_span), F32)],
        [((width, hid_span), F32)],
        info, act, grad_expanded, *grads_mixed, *inners, smem=1,
    )
    mix_dealt = [mix_dealt[0]] + chip_swaps(mix_dealt)
    one_dealt = after(tuple(one_dealt), (grad_expanded,))
    one_dealt = [one_dealt[0]] + chip_swaps(one_dealt)
    inner_parts, one_dealt[1] = pin(inner_parts, one_dealt[1])
    grad_middle, sums, reduce_sum, *branches = call(
        functools.partial(branch_kernel, high, low),
        [((tok_rows, width), F32), ((8, width), F32), ((hid_shard, width), BF)]
        + [((tok_rows + shard, width), BF)] * high,
        [],
        middle, vecs, grad_encoded, own_mixed, *inner_parts, *mix_dealt,
    )
    two_dealt, one_dealt = after((tuple(two_dealt), tuple(one_dealt)), (sums,))
    branches = [branches[0]] + plane_swaps(branches)
    conv_blocks = chip_add(two_dealt, one_dealt)
    conv_blocks = list(conv_blocks)
    branches, conv_blocks[1] = pin(branches, conv_blocks[1])
    conv_blocks = [conv_blocks[0]] + plane_swaps(conv_blocks)
    mix_cube = Cube(
        call(
            functools.partial(mix_pack_kernel, high, tok_rows),
            [((high * shard + hid_shard, width), BF)],
            [],
            *branches, reduce_sum,
        )[0]
    )
    own_dqkv, *dkvs = call(
        functools.partial(attend_back_kernel, high, low, head_dim),
        [((rows, 3 * span), BF)] + [((rows, 2 * span), BF)] * (low - 1),
        [],
        q, crop_q, crop_k, log_total, out_w, *branches, *kvs,
    )
    dkvs[-1], mix_cube.got = pin(dkvs[-1], mix_cube.got)
    dkvs = chip_swaps([own_dqkv] + dkvs)
    mix_cube.step()
    dkvs, conv_blocks[1:] = pin(dkvs, conv_blocks[1:])
    expand_bias_part = expand_bias_part.reshape(low, hid_shard // shard, shard)
    expand_bias_part = expand_bias_part.transpose(1, 0, 2).reshape(hid_shard // shard, span)
    joint_outs = call(
        functools.partial(joint_back_kernel, high, low),
        partial_kinds + [((high, shard, wide), BF)] * low,
        [((rows, wide), BF), ((width, wide), F32)],
        info, own_dqkv, normed, joint_w, vecs, sums, expand_bias_part, *dkvs, smem=1,
    )
    normed_parts, joint_dealt = joint_outs[:high], joint_outs[high:]
    joint_dealt, mix_cube.got = pin(joint_dealt, mix_cube.got)
    mix_cube.step()

    blocks = chip_add([joint_dealt[0]] + chip_swaps(joint_dealt))
    blocks = [blocks[0]] + plane_swaps(blocks)
    out_dealt = call(
        functools.partial(output_grad_kernel, high, low),
        [((shard, width), BF)] * low,
        [((span, width), F32)],
        info, *attended, *branches, smem=1,
    )
    out_dealt = [out_dealt[0]] + chip_swaps(out_dealt)
    blocks, out_dealt[1] = lax.optimization_barrier((blocks, out_dealt[1]))
    tiles = wide // channels
    side_rows = high * tiles * shard + conv_blocks[0].shape[0] + width // channels * shard
    side_size = -(-side_rows // (16 * nb)) * 16
    pieces = call(
        functools.partial(side_pack_kernel, high, low),
        [((side_size, channels), BF)] * nb,
        [((side_size * nb, channels), F32)],
        info, *blocks, *conv_blocks, *out_dealt, smem=1,
    )
    pieces = [pieces[0]] + [swap(pieces[t], "batch", t) for t in range(1, nb)]
    normed_parts = after(tuple(normed_parts), blocks[1:])
    normed_parts = [normed_parts[0]] + plane_swaps(normed_parts)
    pieces, mix_cube.got = pin(pieces, mix_cube.got)
    mix_cube.step()
    pieces = gather_list(sum_list(pieces).astype(BF))
    tokens_grad = call(
        functools.partial(tokens_kernel, high),
        [((tok_rows, width), F32)],
        [],
        grad_middle, own_tokens, vecs, *normed_parts,
    )[0]
    expand_grad, reduce_grad = call(
        functools.partial(mix_final_kernel, high),
        [((shard, hidden), F32), ((hid_shard, width), F32)],
        [((high * shard + hid_shard, width), F32)],
        info, mix_cube.values, mix_cube.got, smem=1,
    )
    pieces, (expand_grad, reduce_grad, tokens_grad) = pin(
        pieces, (expand_grad, reduce_grad, tokens_grad)
    )
    (joint_grad, vec_grads, output_grad, upsample_grad, kernel_one_grad, kernel_two_grad,
     residual_grad) = call(
        functools.partial(side_final_kernel, high),
        [((shard, 3 * width), F32), ((16, shard), F32), ((shard, width), F32),
         ((shard, 8 * channels), F32), (kernel_first.shape, F32), (kernel_second.shape, F32),
         (residual_weight.shape, F32)],
        [((side_size * nb, channels), F32)],
        info, *pieces, smem=1,
    )
    return (
        decoded[None],
        tokens_grad[None],
        skip_grad[None],
        vec_grads[0],
        vec_grads[1],
        joint_grad,
        vec_grads[2],
        vec_grads[3],
        output_grad,
        vec_grads[4],
        vec_grads[5],
        vec_grads[6],
        expand_grad,
        vec_grads[8 : 8 + hid_shard // shard].reshape(hid_shard),
        reduce_grad,
        vec_grads[7],
        upsample_grad,
        kernel_one_grad,
        kernel_two_grad,
        residual_grad,
    )


def solution(mesh):
    rows = P("batch", "seq", None)
    vec = P("seq")
    mat = P("seq", None)
    in_specs = (rows, rows, rows, P("batch", None))
    in_specs += (vec, vec, mat, vec, vec, mat, vec, vec, vec, mat, vec, mat, vec)
    in_specs += (mat, mat, mat, mat)
    out_specs = (rows, rows, rows)
    out_specs += (vec, vec, mat, vec, vec, mat, vec, vec, vec, mat, vec, mat, vec)
    out_specs += (mat, mat, mat, mat)
    return jax.shard_map(
        on_device, mesh=mesh, in_specs=in_specs, out_specs=out_specs, check_vma=False
    )
```

```python
import functools
import math

import jax
import jax.numpy as jnp
from jax import lax
from jax.experimental import pallas as pl
from jax.experimental.pallas import tpu as pltpu
from jax.sharding import PartitionSpec as P

HEADS = 12
PH = 4
CROPS = 4


LIMITS = {
    "attend_back_kernel": 60,
    "joint_back_kernel": 60,
    "attend_kernel": 22,
    "tap_grad_kernel": 18,
}
EPS_LAYER = 1e-06
EPS_CROP = 1e-05
BF = jnp.bfloat16
F32 = jnp.float32


def crops_of(lengths, indices):
    crop_ends = jnp.cumsum(lengths)
    return jnp.sum((indices[:, None] >= crop_ends[None, :]).astype(jnp.int32), axis=1)


def swap(values, axis, mask):
    count = lax.axis_size(axis)
    return lax.ppermute(values, axis, [(i, i ^ mask) for i in range(count)])


def gather_rel(values, axis, stride, count):
    return jnp.stack([values] + [swap(values, axis, m * stride) for m in range(1, count)])


def pick(blocks, index):
    return lax.dynamic_index_in_dim(blocks, index, 0, keepdims=False)


def unxor(blocks, index):
    count = blocks.shape[0]
    bits = count.bit_length() - 1
    tail = blocks.shape[1:]
    cube = blocks.reshape((2,) * bits + tail)
    for bit in range(bits):
        dim = bits - 1 - bit
        cube = jnp.where(((index >> bit) & 1) == 1, jnp.flip(cube, dim), cube)
    return cube.reshape(blocks.shape)


def deal_rel(blocks, axis, stride, index):
    count = blocks.shape[0]
    return [pick(blocks, index)] + [
        swap(pick(blocks, index ^ m), axis, m * stride) for m in range(1, count)
    ]


def sum_list(parts):
    total = parts[0].astype(F32)
    for part in parts[1:]:
        total = total + part.astype(F32)
    return total


def batch_sum(values):
    count = lax.axis_size("batch")
    if count == 1:
        return values.astype(F32)
    index = lax.axis_index("batch")
    rows = values.shape[0]
    piece = -(-rows // count)
    if piece * count > rows:
        values = jnp.pad(values, ((0, piece * count - rows), (0, 0)))
    pieces = values.reshape((count, piece) + values.shape[1:])
    own = sum_list(deal_rel(pieces, "batch", 1, index)).astype(BF)
    total = unxor(gather_rel(own, "batch", 1, count), index)
    return total.reshape(values.shape)[:rows].astype(F32)


def call(kernel, outs, scratch, *args, smem=0):
    name = getattr(kernel, "func", kernel).__name__
    limit = LIMITS.get(name, 12)
    return pl.pallas_call(
        kernel,
        out_shape=tuple(jax.ShapeDtypeStruct(shape, kind) for shape, kind in outs),
        in_specs=[pl.BlockSpec(memory_space=pltpu.SMEM)] * smem
        + [pl.BlockSpec(memory_space=pltpu.VMEM)] * (len(args) - smem),
        scratch_shapes=[pltpu.VMEM(shape, kind) for shape, kind in scratch],
        compiler_params=pltpu.CompilerParams(vmem_limit_bytes=limit * 1024 * 1024),
        name=name,
    )(*args)


GRID = 2 * PH
CELLS = GRID * GRID
ERF_TOP = (
    0.00022905065861350646,
    0.0034082910107109506,
    0.050955695062380861,
    0.18520832239976145,
    1.128379143519084,
)
ERF_LOW = (
    -1.1791602954361697e-7,
    0.000023547966471313185,
    0.0010179625278914885,
    0.014070470171167667,
    0.11098505178285362,
    0.49746925110067538,
    1.0,
)


def normal_cdf(values):
    arg = jnp.clip(values * math.sqrt(0.5), -3.832506856900711, 3.832506856900711)
    square = arg * arg
    top = jnp.full_like(square, ERF_TOP[0])
    for coef in ERF_TOP[1:]:
        top = top * square + coef
    bottom = jnp.full_like(square, ERF_LOW[0])
    for coef in ERF_LOW[1:]:
        bottom = bottom * square + coef
    return 0.5 + 0.5 * (arg * top / bottom)


def gelu_slope(values, cdf):
    return cdf + values * (jnp.exp(-0.5 * values * values) * (1.0 / math.sqrt(2.0 * math.pi)))


def depth_shifts(cells, prev, following, up, down):
    half = cells.shape[1] // 2
    even, odd = cells[:, :half], cells[:, half:]
    row = lax.broadcasted_iota(jnp.int32, even.shape, 1)
    ahead = jnp.where(row == half - 1, following[:, None, :], pltpu.roll(even, half - 1, 1))
    behind = jnp.where(row == 0, prev[:, None, :], pltpu.roll(odd, 1, 1))
    return (
        jnp.concatenate([behind * down[None], even], axis=1),
        jnp.concatenate([odd, ahead * up[None]], axis=1),
    )


def flat_rows(cells):
    return cells.reshape(cells.shape[0] * cells.shape[1], cells.shape[2])


def deep(rows):
    return rows.reshape(CELLS, rows.shape[0] // CELLS, rows.shape[1])


def tap_add(acc_ref, field, tap, sign):
    step_i, step_j = sign * (tap // 3 - 1), sign * (tap % 3 - 1)
    depth = acc_ref.shape[2]
    field = field.reshape(GRID, GRID, depth, field.shape[1])
    low_i, high_i = max(0, -step_i), GRID - max(0, step_i)
    low_j, high_j = max(0, -step_j), GRID - max(0, step_j)
    acc_ref[low_i:high_i, low_j:high_j] += field[
        low_i + step_i : high_i + step_i, low_j + step_j : high_j + step_j
    ]


def conv_into(acc_ref, stack, weight_ref, in_chans):
    taps = [4, 0, 1, 2, 3, 5, 6, 7, 8]

    def matrix(tap):
        return jnp.concatenate(
            [
                weight_ref[(layer * 9 + tap) * in_chans : (layer * 9 + tap + 1) * in_chans, :]
                for layer in range(3)
            ],
            axis=0,
        )

    out = weight_ref.shape[1]
    acc_ref[...] = jnp.zeros_like(acc_ref)
    for start in range(0, 9, 2):
        pair = taps[start : start + 2]
        rhs = jnp.concatenate([matrix(tap) for tap in pair], axis=1)
        field = jnp.dot(stack, rhs, preferred_element_type=F32)
        for place, tap in enumerate(pair):
            tap_add(acc_ref, field[:, place * out : (place + 1) * out], tap, 1)


def turned_into(acc_ref, stack, weight_ref, in_chans):
    taps = [4, 0, 1, 2, 3, 5, 6, 7, 8]

    def matrix(tap):
        return jnp.concatenate(
            [
                weight_ref[(layer * 9 + tap) * in_chans : (layer * 9 + tap + 1) * in_chans, :]
                for layer in (2, 1, 0)
            ],
            axis=1,
        )

    acc_ref[...] = jnp.zeros_like(acc_ref)
    step = max(1, 256 // in_chans)
    for start in range(0, 9, step):
        pair = taps[start : start + step]
        rhs = jnp.concatenate([matrix(tap) for tap in pair], axis=0)
        field = lax.dot_general(
            stack, rhs, (((1,), (1,)), ((), ())), preferred_element_type=F32
        )
        for place, tap in enumerate(pair):
            tap_add(acc_ref, field[:, place * in_chans : (place + 1) * in_chans], tap, -1)


def send_slabs(values_ref, parity, even_ref, odd_ref):
    depth = values_ref.shape[0] // CELLS
    top = values_ref[pl.ds(depth - 1, CELLS, stride=depth), :]
    bottom = values_ref[pl.ds(0, CELLS, stride=depth), :]
    even_ref[...] = jnp.where(parity == 0, top, bottom)
    odd_ref[...] = jnp.where(parity == 0, bottom, top)


def place_slabs(parity, from_even, from_odd):
    return (
        jnp.where(parity == 0, from_odd, from_even),
        jnp.where(parity == 0, from_even, from_odd),
    )


def spread(onehot_ref, per_crop):
    total = onehot_ref[0] * per_crop[0:1]
    for crop in range(1, CROPS):
        total = total + onehot_ref[crop] * per_crop[crop : crop + 1]
    return total


def crop_fold(onehot_ref, per_depth):
    return [
        jnp.sum(onehot_ref[crop] * per_depth, axis=0, keepdims=True) for crop in range(CROPS)
    ]


def moment_tile(onehot_ref, count_ref, cells, tile_ref):
    per_slice = float(cells.shape[0])
    sums = jnp.sum(cells, axis=0)
    about = cells - (sums * (1.0 / per_slice))[None]
    devs = jnp.sum(about * about, axis=0)
    totals = crop_fold(onehot_ref, sums)
    for crop in range(CROPS):
        mean = totals[crop] / jnp.maximum(count_ref[0, crop : crop + 1], 1.0)
        off = sums * (1.0 / per_slice) - mean
        tile_ref[crop : crop + 1] = totals[crop]
        tile_ref[CROPS + crop : CROPS + crop + 1] = jnp.sum(
            onehot_ref[crop] * (devs + per_slice * off * off), axis=0, keepdims=True
        )


def sum_tile(onehot_ref, first, second, tile_ref):
    for start, field in ((0, first), (CROPS, second)):
        totals = crop_fold(onehot_ref, jnp.sum(field, axis=0))
        for crop in range(CROPS):
            tile_ref[start + crop : start + crop + 1] = totals[crop]


def tile_list(tile_refs, high):
    tiles = [ref[...] for ref in tile_refs[:high]]
    for ref in tile_refs[high:]:
        tiles += [ref[8 * m : 8 * m + 8, :] for m in range(high)]
    return tiles


def merged_moments(tiles, count_ref, total_ref):
    total = total_ref[...]
    sums = tiles[0][:CROPS]
    devs = tiles[0][CROPS:]
    for tile in tiles[1:]:
        sums = sums + tile[:CROPS]
        devs = devs + tile[CROPS:]
    mean = sums / total
    for place, tile in enumerate(tiles):
        held = count_ref[place]
        off = tile[:CROPS] / jnp.maximum(held, 1.0) - mean
        devs = devs + held * off * off
    return mean, lax.rsqrt(devs / total + EPS_CROP)


def merged_sums(tiles, total_ref):
    both = tiles[0]
    for tile in tiles[1:]:
        both = both + tile
    total = total_ref[...]
    return both[:CROPS] / total, both[CROPS:] / total


def stack_rows(cells, prev, following, up, down):
    behind, ahead = depth_shifts(cells, prev, following, up, down)
    return [flat_rows(part).astype(BF) for part in (behind, cells, ahead)]


def up_kernel(
    high, slices, info, vec_ref, weight_ref, side_ref, *refs
):
    parts, (enc_ref, up_ref, even_ref, odd_ref, grid_ref) = refs[:high], refs[high:]
    encoded = (plane_total(parts) + vec_ref[7:8, :]).astype(BF)
    enc_ref[...] = encoded
    tok_rows = encoded.shape[0]
    plane = tok_rows // slices
    chans = up_ref.shape[1]
    ordered = jnp.dot(
        token_order(tok_rows, slices, False), encoded, preferred_element_type=F32
    ).astype(BF)
    rows = jnp.dot(ordered, weight_ref[...], preferred_element_type=F32)
    depth = 2 * slices
    for cell in range(plane):
        for place in range(8):
            part_a, part_b, part_e = place // 4, (place // 2) % 2, place % 2
            at = (2 * (cell // PH) + part_b) * GRID + 2 * (cell % PH) + part_e
            grid_ref[at * depth + part_a * slices : at * depth + (part_a + 1) * slices, :] = rows[
                cell * slices : (cell + 1) * slices, place * chans : (place + 1) * chans
            ]
    parity = info[0]
    top = grid_ref[pl.ds(depth - 1, CELLS, stride=depth), :]
    bottom = grid_ref[pl.ds(0, CELLS, stride=depth), :]
    even_ref[:, :chans] = jnp.where(parity == 0, top, bottom).astype(BF)
    odd_ref[:, :chans] = jnp.where(parity == 0, bottom, top).astype(BF)

    @pl.when(parity == 0)
    def _():
        even_ref[:, chans:] = side_ref[CELLS:, :]
        odd_ref[:, chans:] = side_ref[:CELLS, :]

    @pl.when(parity != 0)
    def _():
        even_ref[:, chans:] = side_ref[:CELLS, :]
        odd_ref[:, chans:] = side_ref[CELLS:, :]

    up_ref[...] = grid_ref[...].astype(BF)


def first_kernel(
    info, onehot, count_ref, masks, up_ref, from_even, from_odd, skip_ref,
    weight_ref, conv_ref, tile_ref, even_ref, odd_ref, stack_ref, halo_ref, acc_ref,
):
    parity = info[0]
    down, up = masks[0], masks[1]
    chans = up_ref.shape[1]
    up_halo = place_slabs(
        parity, from_even[:, :chans].astype(F32), from_odd[:, :chans].astype(F32)
    )
    skip_halo = place_slabs(
        parity,
        from_even[:, chans : 2 * chans].astype(F32),
        from_odd[:, chans : 2 * chans].astype(F32),
    )
    parts_up = stack_rows(deep(up_ref[...].astype(F32)), *up_halo, up, down)
    parts_skip = stack_rows(deep(skip_ref[...].astype(F32)), *skip_halo, up, down)
    for layer in range(3):
        at = 2 * layer * chans
        stack_ref[:, at : at + chans] = parts_up[layer]
        stack_ref[:, at + chans : at + 2 * chans] = parts_skip[layer]
    for side in range(2):
        halo_ref[side * CELLS : (side + 1) * CELLS, :chans] = up_halo[side].astype(BF)
        halo_ref[side * CELLS : (side + 1) * CELLS, chans:] = skip_halo[side].astype(BF)
    conv_into(acc_ref, stack_ref[...], weight_ref, 2 * chans)
    conv_ref[...] = acc_ref[...].reshape(conv_ref.shape)
    moment_tile(onehot, count_ref, deep(conv_ref[...]), tile_ref)
    send_slabs(conv_ref, parity, even_ref, odd_ref)


def second_kernel(
    high, info, onehot, count_ref, total_ref, masks, conv_one, odd_slab, weight_ref, *refs
):
    n_out = 8
    tiles, outs = refs[: -n_out - 1], refs[-n_out - 1 :]
    conv_ref, tile_ref, even_ref, odd_ref, stack_ref, unit_ref, slab_unit_ref, scale_ref, acc_ref = outs
    parity = info[0]
    down, up = masks[0], masks[1]
    mean, inv = merged_moments(tile_list(tiles, high), count_ref, total_ref)
    mean_z, inv_z = spread(onehot, mean), spread(onehot, inv)
    scale_ref[0] = mean_z
    scale_ref[1] = inv_z
    unit = (deep(conv_one[...]) - mean_z[None]) * inv_z[None]
    unit_ref[...] = flat_rows(unit)
    act = unit * normal_cdf(unit)
    halo = place_slabs(parity, tiles[high][8 * high :, :], odd_slab[...])
    depth = mean_z.shape[0]
    sides = []
    for side, at in ((0, 0), (1, depth - 1)):
        part = (halo[side] - mean_z[at : at + 1]) * inv_z[at : at + 1]
        slab_unit_ref[side * CELLS : (side + 1) * CELLS, :] = part
        sides.append(part * normal_cdf(part))
    parts = stack_rows(act, sides[0], sides[1], up, down)
    chans = conv_one.shape[1]
    for layer in range(3):
        stack_ref[:, layer * chans : (layer + 1) * chans] = parts[layer]
    conv_into(acc_ref, stack_ref[...], weight_ref, chans)
    conv_ref[...] = acc_ref[...].reshape(conv_ref.shape)
    moment_tile(onehot, count_ref, deep(conv_ref[...]), tile_ref)
    send_slabs(conv_ref, parity, even_ref, odd_ref)


def third_kernel(
    high, info, onehot, count_ref, total_ref, conv_two, odd_slab, stack_ref, halo_ref,
    weight_ref, cot_ref, cot_even, cot_odd, *refs
):
    n_out = 7
    tiles, outs = refs[:-n_out], refs[-n_out:]
    decoded_ref, grad_ref, low_ref, unit_ref, slab_ref, tile_ref, inv_ref = outs
    parity = info[0]
    chans = conv_two.shape[1]
    mean, inv = merged_moments(tile_list(tiles, high), count_ref, total_ref)
    mean_z, inv_z = spread(onehot, mean), spread(onehot, inv)
    inv_ref[...] = inv_z
    unit = flat_rows((deep(conv_two[...]) - mean_z[None]) * inv_z[None])
    unit_ref[...] = unit
    joined = stack_ref[:, 2 * chans : 4 * chans]
    summed = unit + jnp.dot(joined, weight_ref[...], preferred_element_type=F32)
    cdf = normal_cdf(summed)
    decoded_ref[...] = (summed * cdf).astype(BF)
    grad = cot_ref[...].astype(F32) * gelu_slope(summed, cdf)
    grad_ref[...] = grad
    low_ref[...] = grad.astype(BF)
    sum_tile(onehot, deep(grad), deep(grad * unit), tile_ref)
    halo = place_slabs(parity, tiles[high][8 * high :, :], odd_slab[...])
    cots = place_slabs(
        parity, cot_even[:, 2 * chans :].astype(F32), cot_odd[:, 2 * chans :].astype(F32)
    )
    depth = mean_z.shape[0]
    for side, at in ((0, 0), (1, depth - 1)):
        rows = slice(side * CELLS, (side + 1) * CELLS)
        part = (halo[side] - mean_z[at : at + 1]) * inv_z[at : at + 1]
        both = part + jnp.dot(halo_ref[rows, :], weight_ref[...], preferred_element_type=F32)
        slab_ref[rows, :chans] = part
        slab_ref[rows, chans:] = cots[side] * gelu_slope(both, normal_cdf(both))


def fourth_kernel(
    high, info, onehot, total_ref, masks, grad_ref, unit_two, inv_two, slab_two, unit_one,
    weight_ref, *refs
):
    n_out = 5
    tiles, outs = refs[: -n_out - 1], refs[-n_out - 1 :]
    second_ref, back_ref, tile_ref, even_ref, odd_ref, acc_ref = outs
    parity = info[0]
    down, up = masks[0], masks[1]
    chans = grad_ref.shape[1]
    first, cross = merged_sums(tile_list(tiles, high), total_ref)
    first_z, cross_z, inv_z = spread(onehot, first), spread(onehot, cross), inv_two[...]
    grad = deep(grad_ref[...]) - first_z[None] - deep(unit_two[...]) * cross_z[None]
    grad = grad * inv_z[None]
    depth = inv_z.shape[0]
    sides = []
    for side, at in ((0, 0), (1, depth - 1)):
        rows = slice(side * CELLS, (side + 1) * CELLS)
        part = slab_two[rows, chans:] - first_z[at : at + 1]
        part = part - slab_two[rows, :chans] * cross_z[at : at + 1]
        sides.append(part * inv_z[at : at + 1])
    parts = stack_rows(grad, sides[0], sides[1], up, down)
    second_ref[...] = parts[1]
    turned_into(acc_ref, jnp.concatenate(parts, axis=1), weight_ref, chans)
    unit = unit_one[...]
    back = acc_ref[...].reshape(back_ref.shape) * gelu_slope(unit, normal_cdf(unit))
    back_ref[...] = back
    sum_tile(onehot, deep(back), deep(back * unit), tile_ref)
    send_slabs(back_ref, parity, even_ref, odd_ref)


def fifth_kernel(
    high, slices, info, onehot, total_ref, masks, back_ref, unit_one, scale_one, slab_one,
    odd_slab, low_ref, weight_ref, resid_ref, up_weight_ref, *refs
):
    n_out = 5
    tiles, outs = refs[: -n_out - 1], refs[-n_out - 1 :]
    first_ref, skip_ref, rows_ref, encoded_ref, mixed_ref, acc_ref = outs
    parity = info[0]
    down, up = masks[0], masks[1]
    chans = back_ref.shape[1]
    first, cross = merged_sums(tile_list(tiles, high), total_ref)
    first_z, cross_z, inv_z = spread(onehot, first), spread(onehot, cross), scale_one[1]
    grad = deep(back_ref[...]) - first_z[None] - deep(unit_one[...]) * cross_z[None]
    grad = grad * inv_z[None]
    halo = place_slabs(parity, tiles[high][8 * high :, :], odd_slab[...])
    depth = inv_z.shape[0]
    sides = []
    for side, at in ((0, 0), (1, depth - 1)):
        rows = slice(side * CELLS, (side + 1) * CELLS)
        part = halo[side] - first_z[at : at + 1] - slab_one[rows, :] * cross_z[at : at + 1]
        sides.append(part * inv_z[at : at + 1])
    parts = stack_rows(grad, sides[0], sides[1], up, down)
    first_ref[...] = parts[1]
    turned_into(acc_ref, jnp.concatenate(parts, axis=1), weight_ref, 2 * chans)
    field = acc_ref[...].reshape(back_ref.shape[0], 2 * chans) + lax.dot_general(
        low_ref[...], resid_ref[...], (((1,), (1,)), ((), ())), preferred_element_type=F32
    )
    skip_ref[...] = field[:, chans:]
    plane = PH * PH
    columns = []
    for place in range(8):
        part_a, part_b, part_e = place // 4, (place // 2) % 2, place % 2
        pieces = []
        for cell in range(plane):
            at = (2 * (cell // PH) + part_b) * GRID + 2 * (cell % PH) + part_e
            low = at * depth + part_a * slices
            pieces.append(field[low : low + slices, :chans])
        columns.append(jnp.concatenate(pieces, axis=0))
    up_rows = jnp.concatenate(columns, axis=1).astype(BF)
    rows_ref[...] = jnp.dot(
        token_order(plane * slices, slices, True), up_rows, preferred_element_type=F32
    ).astype(BF)
    encoded = lax.dot_general(
        rows_ref[...], up_weight_ref[...], (((1,), (1,)), ((), ())), preferred_element_type=F32
    )
    encoded_ref[...] = encoded
    mixed_ref[...] = encoded.astype(BF)


def tap_grad_kernel(
    in_chans, high, low, wide, info, stack_ref, grad_ref, left_ref, right_ref, *refs
):
    outs, (turned_ref, pad_ref, rows_ref, extra_ref) = refs[:low], refs[low:]
    chans = grad_ref.shape[1]
    count = high * low
    shard = 27 * in_chans // count
    depth = grad_ref.shape[0] // CELLS
    pad_ref[...] = jnp.zeros_like(pad_ref)
    pad_ref[1 : GRID + 1, 1 : GRID + 1] = grad_ref[...].reshape(GRID, GRID, depth, chans)
    for tap in range(9):
        low_i, low_j = 2 - tap // 3, 2 - tap % 3
        moved = pad_ref[low_i : low_i + GRID, low_j : low_j + GRID]
        turned_ref[tap * chans : (tap + 1) * chans, :] = moved.reshape(-1, chans).T
    for layer in range(3):
        at = layer * in_chans
        product = jnp.dot(
            turned_ref[...], stack_ref[:, at : at + in_chans], preferred_element_type=F32
        )
        for tap in range(9):
            block = product[tap * chans : (tap + 1) * chans, :].T
            start = (layer * 9 + tap) * in_chans
            done = 0
            while done < in_chans:
                owner, place = divmod(start + done, shard)
                size = min(in_chans - done, shard - place)
                rows_ref[owner, place : place + size, :] = block[done : done + size, :]
                done += size
    extra = extra_ref.shape[1]
    left = left_ref[...]
    if wide == 1:
        left = left[:, 2 * chans : 4 * chans]
    extra_ref[...] = cross_rows(left, right_ref[...]).reshape(extra_ref.shape)
    for s in range(low):
        for m in range(high):
            owner = (info[1] ^ m) * low + (info[2] ^ s)
            outs[s][m, :shard, :] = rows_ref[owner][:shard].astype(BF)
            other = extra_ref[owner].astype(BF)
            for place in range(wide):
                start = shard + place * extra
                outs[s][m, start : start + extra, :] = other[
                    :, place * chans : (place + 1) * chans
                ]


def pack_kernel(high, info, token_ref, joint_ref, expand_ref, out_w_ref, *refs):
    vecs, joints, expands = refs[: -2 * high], refs[-2 * high : -high], refs[-high:]
    span = joint_ref.shape[1] // (3 * high)
    third = joint_ref.shape[1] // 3
    wide = expand_ref.shape[1] // high
    rows = token_ref.shape[0]
    shard = joint_ref.shape[0]
    lines = [ref[...] for ref in vecs]
    lines.append(jnp.zeros((128 - sum(line.shape[0] for line in lines), shard), F32))
    columns = jnp.concatenate(lines, axis=0).T[:, :64].astype(BF)
    top = 3 * span + 64
    for own in range(high):

        @pl.when(info[1] == own)
        def _():
            for m in range(high):
                group = own ^ m
                joints[m][:rows, :] = token_ref[...]
                for part in range(3):
                    joints[m][rows:, part * span : (part + 1) * span] = joint_ref[
                        :, part * third + group * span : part * third + (group + 1) * span
                    ]
                joints[m][rows:, 3 * span : top] = columns
                if top < joints[m].shape[1]:
                    joints[m][rows:, top:] = jnp.zeros(
                        (joint_ref.shape[0], joints[m].shape[1] - top), BF
                    )
                expands[m][0] = expand_ref[:, group * wide : (group + 1) * wide]
                expands[m][1] = out_w_ref[...]


def assembled(info, high, low, natural, parts, scratch_ref):
    rows = scratch_ref.shape[1]
    for s in range(low):
        for m in range(high):
            block = parts[m][...] if s == 0 else parts[high + s - 1][m * rows : (m + 1) * rows, :]
            major = (info[1] ^ m) if natural else m
            scratch_ref[major * low + (info[2] ^ s)] = block.astype(F32)


def order_kernel(high, low, natural, info, *refs):
    parts, out_ref, scratch_ref = refs[:-2], refs[-2], refs[-1]
    assembled(info, high, low, natural, parts, scratch_ref)
    out_ref[...] = scratch_ref[...].reshape(out_ref.shape).astype(BF)


def pair_kernel(high, low, info, *refs):
    parts, (expand_ref, out_ref, scratch_ref) = refs[:-3], refs[-3:]
    for slab, natural, place in ((0, True, expand_ref), (1, False, out_ref)):
        for s in range(low):
            for m in range(high):
                block = parts[m][slab] if s == 0 else parts[high + s - 1][m, slab]
                major = (info[1] ^ m) if natural else m
                scratch_ref[major * low + (info[2] ^ s)] = block.astype(F32)
        place[...] = scratch_ref[...].reshape(place.shape).astype(BF)


def unit_rows_of(values):
    average = jnp.mean(values, axis=-1, keepdims=True)
    centred = values - average
    inv_std = lax.rsqrt(jnp.mean(centred * centred, axis=-1, keepdims=True) + EPS_LAYER)
    return centred * inv_std, inv_std


def query_kernel(high, low, info, *refs):
    tokens, partners = refs[:high], refs[high : high + low - 1]
    q_ref, kv_ref, normed_ref, weight_ref, vec_ref, own_vec_ref, scratch_ref = refs[-7:]
    width = normed_ref.shape[1]
    wide = weight_ref.shape[1]
    span = q_ref.shape[1]
    rows = normed_ref.shape[0] // (2 * high)
    own_parts = [ref.at[rows:, :wide] for ref in tokens]
    assembled(info, high, low, True, own_parts + list(partners), scratch_ref)
    weight = scratch_ref[...].reshape(width, wide)
    weight_ref[...] = weight.astype(BF)
    turned = weight[:, wide - 128 :].T
    vec_ref[...] = turned[64:80, :]
    own = scratch_ref[pl.ds(info[1] * low, low), :, :][:, :, wide - 128 :]
    own_turned = own.reshape(width // high, 128).T
    own_vec_ref[...] = own_turned[64:80, :]
    gain, shift = turned[64:65, :], turned[65:66, :]
    for m in range(high):
        unit, _ = unit_rows_of(tokens[m][:rows, :].astype(F32))
        normed_ref[m * rows : (m + 1) * rows, :] = (unit * gain + shift).astype(BF)
        normed_ref[(high + m) * rows : (high + m + 1) * rows, :] = unit.astype(BF)
    joint = jnp.dot(
        normed_ref[: high * rows, :], weight_ref[...], preferred_element_type=F32
    )
    q_ref[...] = (joint[:, :span] + own_turned[66:67, :]).astype(BF)
    kv_ref[:, :span] = joint[:, span : 2 * span].astype(BF)
    kv_ref[:, span:] = (joint[:, 2 * span : 3 * span] + own_turned[67:68, :]).astype(BF)


def head_columns(refs, start, head_dim):
    return jnp.concatenate([ref[:, start : start + head_dim] for ref in refs], axis=0)


def masked_scores(keys, queries, same):
    scores = lax.dot_general(
        keys, queries, (((1,), (1,)), ((), ())), preferred_element_type=F32
    )
    return jnp.where(same, scores, -1000000000.0)


def attend_kernel(high, head_dim, q_ref, crop_q, crop_k, *refs):
    kvs, outs = refs[: -high - 1], refs[-high - 1 :]
    log_ref = outs[-1]
    span = q_ref.shape[1]
    same = crop_k[...] == crop_q[...]
    scale = 1.0 / math.sqrt(head_dim)
    pieces = []
    for head in range(span // head_dim):
        at = head * head_dim
        queries = q_ref[:, at : at + head_dim] * jnp.asarray(scale, BF)
        scores = masked_scores(head_columns(kvs, at, head_dim), queries, same)
        highest = jnp.max(scores, axis=0, keepdims=True)
        powers = jnp.exp(scores - highest)
        sums = jnp.sum(powers, axis=0, keepdims=True)
        log_ref[head : head + 1, :] = highest + jnp.log(sums)
        share = (powers * (1.0 / sums)).astype(BF)
        values = head_columns(kvs, span + at, head_dim)
        pieces.append(jnp.dot(values.T, share, preferred_element_type=F32))
    attended = jnp.concatenate(pieces, axis=0).T.astype(BF)
    rows = outs[0].shape[0]
    for m in range(high):
        outs[m][...] = attended[m * rows : (m + 1) * rows, :]


def middle_kernel(high, token_ref, weight_ref, vec_ref, *refs):
    parts, (middle_ref, inner_ref) = refs[:high], refs[high:]
    span = parts[0].shape[1]
    middle = token_ref[...].astype(F32) + vec_ref[4:5, :]
    for m in range(high):
        middle = middle + jnp.dot(
            parts[m][...], weight_ref[m * span : (m + 1) * span, :], preferred_element_type=F32
        )
    middle_ref[...] = middle
    unit, _ = unit_rows_of(middle)
    inner_ref[...] = (unit * vec_ref[5:6, :] + vec_ref[6:7, :]).astype(BF)


def mix_kernel(high, middle_ref, expand_ref, reduce_ref, bias_ref, *refs):
    parts, outs = refs[:high], refs[high:]
    act_ref, slope_ref = outs[high], outs[high + 1]
    rows = parts[0].shape[0]
    for m in range(high):
        at = slice(m * rows, (m + 1) * rows)
        expanded = bias_ref[...] + jnp.dot(
            parts[m][...], expand_ref[...], preferred_element_type=F32
        )
        cdf = normal_cdf(expanded)
        act = (expanded * cdf).astype(BF)
        act_ref[at, :] = act
        slope_ref[at, :] = gelu_slope(expanded, cdf)
        mixed = jnp.dot(act, reduce_ref[...], preferred_element_type=F32)
        if m == 0:
            mixed = mixed + middle_ref[...]
        outs[m][...] = mixed.astype(outs[m].dtype)


def plane_total(parts):
    total = parts[0][...]
    for ref in parts[1:]:
        total = total + ref[...].astype(F32)
    return total


def token_order(tok_rows, slices, back):
    plane = tok_rows // slices
    row = lax.broadcasted_iota(jnp.int32, (tok_rows, tok_rows), 0)
    col = lax.broadcasted_iota(jnp.int32, (tok_rows, tok_rows), 1)
    if back:
        row, col = col, row
    return jnp.where(col == (row % slices) * plane + row // slices, 1.0, 0.0).astype(BF)


def mix_back_kernel(high, reduce_ref, expand_ref, slope_ref, *refs):
    parts, outs = refs[:high], refs[high:]
    grad_ref = outs[high]
    rows = parts[0].shape[0]
    for m in range(high):
        at = slice(m * rows, (m + 1) * rows)
        grad = lax.dot_general(
            parts[m][...], reduce_ref[...], (((1,), (1,)), ((), ())), preferred_element_type=F32
        )
        grad = (grad * slope_ref[at, :]).astype(BF)
        grad_ref[at, :] = grad
        back = lax.dot_general(
            grad, expand_ref[...], (((1,), (1,)), ((), ())), preferred_element_type=F32
        )
        outs[m][...] = back.astype(outs[m].dtype)


def cross_rows(first, second):
    return lax.dot_general(first, second, (((0,), (0,)), ((), ())), preferred_element_type=F32)


def deal_rows(info, high, low, scratch_ref, outs):
    shard = outs[0].shape[1]
    for s in range(low):
        for m in range(high):
            at = ((info[1] ^ m) * low + (info[2] ^ s)) * shard
            outs[s][m] = scratch_ref[pl.ds(pl.multiple_of(at, 8), shard), :].astype(BF)


def deal_chip(info, low, scratch_ref, outs):
    shard = outs[0].shape[0]
    for s in range(low):
        at = (info[2] ^ s) * shard
        outs[s][...] = scratch_ref[pl.ds(pl.multiple_of(at, 8), shard), :].astype(BF)


def mix_grad_kernel(high, low, info, act_ref, grad_ref, *refs):
    mixed = jnp.concatenate([ref[...] for ref in refs[:high]], axis=0)
    inner = jnp.concatenate([ref[...] for ref in refs[high : 2 * high]], axis=0)
    outs = refs[2 * high :]
    bias_ref, scratch_ref = outs[low], outs[low + 1]
    hid_shard = scratch_ref.shape[0] // low
    shard = (outs[0].shape[0] - hid_shard) // high
    scratch_ref[...] = cross_rows(inner, grad_ref[...])
    for s in range(low):
        for m in range(high):
            at = ((info[1] ^ m) * low + (info[2] ^ s)) * shard
            outs[s][m * shard : (m + 1) * shard, :] = scratch_ref[
                pl.ds(pl.multiple_of(at, 8), shard), :
            ].astype(BF)
    scratch_ref[...] = cross_rows(act_ref[...], mixed)
    for s in range(low):
        at = (info[2] ^ s) * hid_shard
        outs[s][high * shard :, :] = scratch_ref[
            pl.ds(pl.multiple_of(at, 8), hid_shard), :
        ].astype(BF)
    bias_ref[...] = jnp.sum(grad_ref[...].astype(F32), axis=0, keepdims=True)


def norm_back(upstream, unit, inv_std, gain):
    scaled = upstream * gain
    return inv_std * (
        scaled
        - jnp.mean(scaled, axis=-1, keepdims=True)
        - unit * jnp.mean(scaled * unit, axis=-1, keepdims=True)
    )


def branch_kernel(high, low, middle_ref, vec_ref, encoded_ref, mixed_ref, *refs):
    parts, dealt = refs[:high], refs[high : high + low]
    grad_ref, sums_ref, reduce_ref = refs[high + low : high + low + 3]
    outs = refs[high + low + 3 :]
    inner = plane_total(parts)
    unit, inv_std = unit_rows_of(middle_ref[...])
    grad = encoded_ref[...] + norm_back(inner, unit, inv_std, vec_ref[5:6, :])
    grad_ref[...] = grad
    branch = grad.astype(BF)
    rows = branch.shape[0]
    shard = outs[0].shape[0] - rows
    for m in range(high):
        outs[m][:rows, :] = branch
        total = dealt[0][m * shard : (m + 1) * shard, :].astype(F32)
        for ref in dealt[1:]:
            total = total + ref[m * shard : (m + 1) * shard, :].astype(F32)
        outs[m][rows:, :] = total.astype(BF)
    total = dealt[0][high * shard :, :].astype(F32)
    for ref in dealt[1:]:
        total = total + ref[high * shard :, :].astype(F32)
    reduce_ref[...] = total.astype(BF)
    sums_ref[...] = jnp.zeros_like(sums_ref)
    sums_ref[4:5, :] = jnp.sum(branch.astype(F32), axis=0, keepdims=True)
    sums_ref[5:6, :] = jnp.sum(inner * unit, axis=0, keepdims=True)
    sums_ref[6:7, :] = jnp.sum(inner, axis=0, keepdims=True)
    sums_ref[7:8, :] = jnp.sum(mixed_ref[...].astype(F32), axis=0, keepdims=True)


def attend_back_kernel(high, low, head_dim, q_ref, crop_q, crop_k, log_ref, weight_ref, *refs):
    branches, kvs = refs[:high], refs[high : high + low]
    outs = refs[high + low :]
    span = q_ref.shape[1]
    rows = q_ref.shape[0]
    branch = jnp.concatenate([ref[: rows // high, :] for ref in branches], axis=0)
    attended = lax.dot_general(
        branch, weight_ref[:span, :], (((1,), (1,)), ((), ())), preferred_element_type=F32
    ).astype(BF)
    same = crop_k[...] == crop_q[...]
    scale = 1.0 / math.sqrt(head_dim)
    pieces = []
    for head in range(span // head_dim):
        at = head * head_dim
        queries = q_ref[:, at : at + head_dim] * jnp.asarray(scale, BF)
        keys = head_columns(kvs, at, head_dim)
        values = head_columns(kvs, span + at, head_dim)
        grad_out = attended[:, at : at + head_dim]
        share = jnp.exp(masked_scores(keys, queries, same) - log_ref[head : head + 1, :])
        weights = lax.dot_general(
            values, grad_out, (((1,), (1,)), ((), ())), preferred_element_type=F32
        )
        row_dot = jnp.sum(share * weights, axis=0, keepdims=True)
        grad_scores = (share * (weights - row_dot)).astype(BF)
        grad_keys = jnp.dot(grad_scores, queries, preferred_element_type=F32)
        grad_values = jnp.dot(share.astype(BF), grad_out, preferred_element_type=F32)
        for s in range(low):
            part = slice(s * rows, (s + 1) * rows)
            low_at = at + span if s == 0 else at
            outs[s][:, low_at : low_at + head_dim] = grad_keys[part, :].astype(BF)
            outs[s][:, span + low_at : span + low_at + head_dim] = grad_values[part, :].astype(BF)
        pieces.append(jnp.dot(keys.T, grad_scores, preferred_element_type=F32) * scale)
    outs[0][:, :span] = jnp.concatenate(pieces, axis=0).T.astype(BF)


def output_grad_kernel(high, low, info, *refs):
    attended = jnp.concatenate([ref[...] for ref in refs[:high]], axis=0)
    rows = refs[0].shape[0]
    branch = jnp.concatenate([ref[:rows, :] for ref in refs[high : 2 * high]], axis=0)
    outs, scratch_ref = refs[2 * high : -1], refs[-1]
    scratch_ref[...] = cross_rows(attended, branch)
    deal_chip(info, low, scratch_ref, outs)


def joint_back_kernel(high, low, info, own_ref, normed_ref, weight_ref, vec_ref, sums_ref,
                      bias_ref, *refs):
    dkvs, outs = refs[: low - 1], refs[low - 1 :]
    joint_ref, scratch_ref = outs[-2], outs[-1]
    backs, dealt = outs[:high], outs[high : high + low]
    span = own_ref.shape[1] // 3
    joint_ref[...] = jnp.zeros_like(joint_ref)
    joint_ref[:, :span] = own_ref[:, :span]
    total = own_ref[:, span:].astype(F32)
    for ref in dkvs:
        total = total + ref[...].astype(F32)
    joint_ref[:, span : 3 * span] = total.astype(BF)
    rows = backs[0].shape[0]
    gain_sum, shift_sum = 0.0, 0.0
    for m in range(high):
        part = lax.dot_general(
            joint_ref[m * rows : (m + 1) * rows, :], weight_ref[...], (((1,), (1,)), ((), ())),
            preferred_element_type=F32,
        )
        backs[m][...] = part.astype(backs[m].dtype)
        unit = normed_ref[(high + m) * rows : (high + m + 1) * rows, :].astype(F32)
        gain_sum = gain_sum + jnp.sum(part * unit, axis=0, keepdims=True)
        shift_sum = shift_sum + jnp.sum(part, axis=0, keepdims=True)
    wide = joint_ref.shape[1]
    width = normed_ref.shape[1]
    scratch_ref[...] = cross_rows(normed_ref[: high * rows, :], joint_ref[...])
    whole = jnp.concatenate(
        [
            jnp.zeros((64, width), F32), gain_sum, shift_sum, sums_ref[2:8, :],
            jnp.zeros((56, width), F32),
        ],
        axis=0,
    )
    scratch_ref[:, wide - 128 :] += whole.T
    sums = jnp.sum(joint_ref[...].astype(F32), axis=0, keepdims=True)
    own = jnp.concatenate(
        [
            jnp.zeros((66, span), F32), sums[:, :span], sums[:, 2 * span : 3 * span],
            jnp.zeros((4, span), F32), bias_ref[...],
            jnp.zeros((56 - bias_ref.shape[0], span), F32),
        ],
        axis=0,
    )
    at = pl.multiple_of(info[1] * span, 8)
    scratch_ref[pl.ds(at, span), wide - 128 :] += own.T
    deal_rows(info, high, low, scratch_ref, dealt)


def chip_add_kernel(high, low, *refs):
    parts, outs = refs[:-high], refs[-high:]
    for m in range(high):
        done = 0
        for start in range(0, len(parts), low):
            total = parts[start][m].astype(F32)
            for ref in parts[start + 1 : start + low]:
                total = total + ref[m].astype(F32)
            outs[m][done : done + total.shape[0], :] = total.astype(BF)
            done += total.shape[0]
        if done < outs[m].shape[0]:
            outs[m][done:, :] = jnp.zeros((outs[m].shape[0] - done, outs[m].shape[1]), BF)


def side_pack_kernel(high, low, info, *refs):
    joints, outputs = refs[:high], refs[high : high + low]
    pieces, pack_ref = refs[high + low : -1], refs[-1]
    chans = pack_ref.shape[1]
    rows, done = joints[0].shape[0], 0
    for m in range(high):
        for at in range(0, joints[m].shape[1], chans):
            pack_ref[done : done + rows, :] = joints[m][:, at : at + chans].astype(F32)
            done += rows
    total = outputs[0][...].astype(F32)
    for ref in outputs[1:]:
        total = total + ref[...].astype(F32)
    for at in range(0, total.shape[1], chans):
        pack_ref[done : done + rows, :] = total[:, at : at + chans]
        done += rows
    if done < pack_ref.shape[0]:
        pack_ref[done:, :] = jnp.zeros((pack_ref.shape[0] - done, chans), F32)
    size = pieces[0].shape[0]
    for t in range(len(pieces)):
        at = pl.multiple_of((info[3] ^ t) * size, 8)
        pieces[t][...] = pack_ref[pl.ds(at, size), :].astype(BF)


def conv_final_kernel(info, own_ref, other_ref, two_ref, resid_ref, one_ref, up_ref, whole_ref):
    joined_halves(info[4] == 1, own_ref, other_ref, whole_ref)
    chans = whole_ref.shape[1]
    rows, done = up_ref.shape[0], 0
    for ref in (two_ref, resid_ref, one_ref):
        ref[...] = whole_ref[done : done + ref.shape[0], :]
        done += ref.shape[0]
    for at in range(0, up_ref.shape[1], chans):
        up_ref[:, at : at + chans] = whole_ref[done : done + rows, :]
        done += rows


def mix_pack_kernel(high, rows, *refs):
    branches, pack_ref = refs[:high], refs[high]
    done = 0
    for ref in branches:
        size = ref.shape[0] - rows
        pack_ref[done : done + size, :] = ref[rows:, :]
        done += size


def joined_halves(upper, own_ref, other_ref, whole_ref):
    half = own_ref.shape[0]
    whole_ref[:half, :] = jnp.where(upper, other_ref[...], own_ref[...]).astype(F32)
    whole_ref[half:, :] = jnp.where(upper, own_ref[...], other_ref[...]).astype(F32)


def side_final_kernel(high, info, *refs):
    joint_ref, vec_ref, out_ref, whole_ref = refs[-4:]
    pieces = refs[:-4]
    size = pieces[0].shape[0]
    for t in range(len(pieces)):
        at = pl.multiple_of((info[3] ^ t) * size, 8)
        whole_ref[pl.ds(at, size), :] = pieces[t][...].astype(F32)
    chans = whole_ref.shape[1]
    rows = joint_ref.shape[0]
    span = joint_ref.shape[1] // (3 * high)
    third = joint_ref.shape[1] // 3
    tiles = -(-(3 * span + 64) // chans)

    def block(m):
        return jnp.concatenate(
            [
                whole_ref[(m * tiles + j) * rows : (m * tiles + j + 1) * rows, :]
                for j in range(tiles)
            ],
            axis=1,
        )

    for place in range(high):

        @pl.when(info[1] == place)
        def _():
            for group in range(high):
                values = block(place ^ group)
                for part in range(3):
                    at = part * third + group * span
                    joint_ref[:, at : at + span] = values[:, part * span : (part + 1) * span]

    total = block(0)[:, (tiles - 1) * chans :]
    for m in range(1, high):
        total = total + block(m)[:, (tiles - 1) * chans :]
    vec_ref[...] = total.T[64:80, :]
    done = high * tiles * rows
    for at in range(0, out_ref.shape[1], chans):
        out_ref[:, at : at + chans] = whole_ref[done : done + rows, :]
        done += rows


def mix_final_kernel(
    high, info, own_ref, other_ref, reduce_own, reduce_other, expand_ref, reduce_ref, whole_ref
):
    joined_halves(info[4] == 1, reduce_own, reduce_other, reduce_ref)
    joined_halves(info[4] == 1, own_ref, other_ref, whole_ref)
    wide = expand_ref.shape[1] // high
    rows = expand_ref.shape[0]
    for place in range(high):

        @pl.when(info[1] == place)
        def _():
            for group in range(high):
                m = place ^ group
                expand_ref[:, group * wide : (group + 1) * wide] = whole_ref[
                    m * rows : (m + 1) * rows, :
                ]


def tokens_kernel(high, grad_ref, token_ref, vec_ref, *refs):
    parts, out_ref = refs[:high], refs[high]
    unit, inv_std = unit_rows_of(token_ref[...].astype(F32))
    out_ref[...] = grad_ref[...] + norm_back(plane_total(parts), unit, inv_std, vec_ref[0:1, :])


def on_device(
    tokens,
    skip_features,
    out_grad,
    crop_lengths,
    attend_gain,
    attend_shift,
    joint_weight,
    query_bias,
    value_bias,
    output_weight,
    output_bias,
    mixer_gain,
    mixer_shift,
    expand_weight,
    expand_bias,
    reduce_weight,
    reduce_bias,
    upsample_weight,
    kernel_first,
    kernel_second,
    residual_weight,
):
    count = lax.axis_size("seq")
    nb = lax.axis_size("batch")
    high = math.gcd(HEADS, count)
    low = count // high
    seq_index = lax.axis_index("seq")
    batch_index = lax.axis_index("batch")
    hi = seq_index // low
    lo = seq_index % low
    width = tokens.shape[2]
    shard = joint_weight.shape[0]
    head_dim = width // HEADS
    span = HEADS // high * head_dim
    wide = -(-(3 * span + 64) // 128) * 128
    hidden = expand_weight.shape[1]
    hid_span = hidden // high
    hid_shard = hidden // count
    channels = residual_weight.shape[1]
    plane_size = PH * PH
    tok_rows = tokens.shape[1]
    rows = high * tok_rows
    slices = tok_rows // plane_size
    depth_total = 2 * slices
    positions = depth_total * 4 * plane_size
    lengths = crop_lengths[0]
    own_tokens = tokens[0]
    place = batch_index % 2 if nb == 4 else 0 * hi
    info = jnp.stack([seq_index % 2, hi, lo, batch_index, place]).astype(jnp.int32)

    def plane_swaps(blocks):
        return [swap(blocks[m], "seq", m * low) for m in range(1, high)]

    def plane_copies(block):
        return [block] + [swap(block, "seq", m * low) for m in range(1, high)]

    def gather_list(block):
        return [block] + [swap(block, "batch", t) for t in range(1, nb)]

    def chip_swaps(blocks):
        return [swap(blocks[s], "seq", s) for s in range(1, low)]

    def chip_copies(block):
        return [swap(block, "seq", s) for s in range(1, low)]

    def after(values, done):
        return lax.optimization_barrier((values, tuple(done)))[0]

    def owners(rel_hi, rel_lo):
        return (hi ^ rel_hi) * low + (lo ^ rel_lo)

    def odd_swap(values):
        pairs = [(i, i + 1) for i in range(1, count - 1, 2)]
        return lax.ppermute(values, "seq", pairs + [(j, i) for i, j in pairs])

    vectors = [
        attend_gain, attend_shift, query_bias, value_bias, output_bias, mixer_gain, mixer_shift,
        reduce_bias,
    ]
    vectors = [
        jnp.stack([vec.astype(F32) for vec in vectors]),
        expand_bias.astype(F32).reshape(hid_shard // shard, shard),
    ]
    packed = call(
        functools.partial(pack_kernel, high),
        [((tok_rows + shard, width), BF)] * high + [((2, shard, width), BF)] * high,
        [],
        info, own_tokens, joint_weight, expand_weight, output_weight, *vectors, smem=1,
    )
    all_tokens = list(packed[:1]) + plane_swaps(packed[:high])
    partners = chip_copies(jnp.concatenate([part[tok_rows:, :wide] for part in all_tokens], axis=0))
    q, kv, normed, joint_w, vecs, own_vecs = call(
        functools.partial(query_kernel, high, low),
        [((rows, span), BF), ((rows, 2 * span), BF), ((2 * rows, width), BF), ((width, wide), BF),
         ((16, width), F32), ((16, span), F32)],
        [((count, shard, wide), F32)],
        info, *all_tokens, *partners, smem=1,
    )
    kvs = [kv] + chip_copies(kv)

    def ordered(parts, natural, shape, block):
        kernel = functools.partial(order_kernel, block[0], low, natural)
        return call(
            kernel, [(shape, BF)], [((block[0] * low, block[1], shape[1]), F32)], info, *parts,
            smem=1,
        )[0]

    later_pairs = after(tuple(packed[high:]), all_tokens[1:])
    pairs = [later_pairs[0]] + plane_swaps(later_pairs)
    kvs, pairs[1] = lax.optimization_barrier((kvs, pairs[1]))
    expand_b = own_vecs[8 : 8 + hid_shard // shard].reshape(hid_shard // shard, low, shard)
    expand_b = expand_b.transpose(1, 0, 2).reshape(1, hid_span)
    later_up, later_conv = after(
        (upsample_weight, (kernel_first, kernel_second, residual_weight)), ()
    )
    upsample_w = lax.all_gather(later_up, "seq", axis=0, tiled=True)
    conv_all = lax.all_gather(
        jnp.concatenate(later_conv, axis=0), "seq", axis=0
    )
    cut_one = kernel_first.shape[0]
    cut_two = cut_one + kernel_second.shape[0]
    kernel_one = conv_all[:, :cut_one].reshape(-1, channels)
    kernel_two = conv_all[:, cut_one:cut_two].reshape(-1, channels)
    residual_w = conv_all[:, cut_two:].reshape(-1, channels)

    def token_crops(rel_lo):
        starts = jnp.stack([owners(m, rel_lo) for m in range(high)]) * slices
        ids = starts[:, None] + jnp.arange(tok_rows, dtype=jnp.int32)[None, :] // plane_size
        return crops_of(lengths, ids.reshape(-1))

    crop_q = token_crops(0).reshape(1, rows)
    crop_k = jnp.concatenate([token_crops(s) for s in range(low)]).reshape(low * rows, 1)
    *attended, log_total = call(
        functools.partial(attend_kernel, high, head_dim),
        [((tok_rows, span), BF)] * high + [((8, rows), F32)],
        [],
        q, crop_q, crop_k, *kvs,
    )
    arrived = [attended[0]] + plane_swaps(attended)
    pairs = list(after(tuple(pairs), (arrived[1],)))
    pairs += chip_copies(jnp.stack(pairs))
    expand_w, out_w = call(
        functools.partial(pair_kernel, high, low),
        [((width, hid_span), BF), ((width, width), BF)],
        [((count, shard, width), F32)],
        info, *pairs, smem=1,
    )
    middle, inner = call(
        functools.partial(middle_kernel, high),
        [((tok_rows, width), F32), ((tok_rows, width), BF)],
        [],
        own_tokens, out_w, vecs, *arrived,
    )
    inners = plane_copies(inner)
    reduces = [reduce_weight] + chip_copies(after(reduce_weight, (inner,)))
    reduce_w = ordered(reduces, False, (hid_span, width), (1, hid_shard))
    partial_kinds = [((tok_rows, width), F32)] + [((tok_rows, width), BF)] * (high - 1)
    inners[1], (kernel_one, kernel_two) = lax.optimization_barrier(
        (inners[1], (kernel_one, kernel_two))
    )
    *mixed, act, slope = call(
        functools.partial(mix_kernel, high),
        partial_kinds + [((rows, hid_span), BF), ((rows, hid_span), F32)],
        [],
        middle, expand_w, reduce_w, expand_b, *inners,
    )
    mixed = [mixed[0]] + plane_swaps(mixed)

    def to_cells(values):
        cells = values.reshape(slices, 2, CELLS, channels)
        return cells.transpose(2, 1, 0, 3).reshape(positions, channels)

    def from_cells(values):
        cells = values.reshape(CELLS, 2, slices, channels)
        return cells.transpose(2, 1, 0, 3).reshape(positions, channels)

    late_lengths, late_skip, late_cot = after((lengths, skip_features[0], out_grad[0]), (act,))
    slice_ids = seq_index * slices - 1 + jnp.arange(slices + 2, dtype=jnp.int32)
    crop_ids = jnp.where(slice_ids < 0, -1, crops_of(late_lengths, slice_ids))
    here = crop_ids[1:-1]
    masks = jnp.stack([crop_ids[:-2] == here, crop_ids[2:] == here]).astype(F32)
    masks = jnp.broadcast_to(masks[:, :, None], (2, slices, channels))
    onehot = (jnp.arange(CROPS, dtype=jnp.int32)[:, None] == here[None, :]).astype(F32)
    onehot = jnp.broadcast_to(
        jnp.tile(onehot, (1, 2))[:, :, None], (CROPS, depth_total, channels)
    )
    total = jnp.broadcast_to(
        (late_lengths * 8 * plane_size).astype(F32)[:, None], (CROPS, channels)
    )
    crop_ends = jnp.cumsum(late_lengths)
    dev_rel = jnp.stack([owners(m, s) for s in range(low) for m in range(high)])
    first = (dev_rel * slices)[:, None]
    shared = jnp.minimum(crop_ends[None], first + slices) - jnp.maximum(
        (crop_ends - late_lengths)[None], first
    )
    held = (jnp.maximum(shared, 0) * 8 * plane_size).astype(F32)
    held = jnp.broadcast_to(held[:, :, None], (count, CROPS, channels))
    skip_cells = to_cells(late_skip)
    cot_cells = to_cells(late_cot)
    sides = jnp.concatenate([late_skip, late_cot], axis=1)
    sides = jnp.concatenate([sides[:CELLS], sides[-CELLS:]], axis=0)
    prepared = (
        onehot, held, masks, total, skip_cells, cot_cells, sides, kernel_one, kernel_two,
        residual_w, upsample_w,
    )
    mixed[1], prepared = lax.optimization_barrier((mixed[1], prepared))
    onehot, held, masks, total, skip_cells, cot_cells, sides = prepared[:7]
    kernel_one, kernel_two, residual_w, upsample_w = prepared[7:]

    cells_bf = ((positions, channels), BF)
    cells_f = ((positions, channels), F32)
    slab_f = ((CELLS, channels), F32)
    slab_bf = ((CELLS, 3 * channels), BF)
    slabs_f = ((2 * CELLS, channels), F32)
    tile = ((2 * CROPS, channels), F32)
    grid_acc = ((GRID, GRID, depth_total, channels), F32)

    def exchange(own_tile, even_slab=None, odd_slab=None):
        tiles = plane_copies(own_tile)
        if even_slab is None:
            return tiles + chip_copies(jnp.concatenate(tiles, axis=0)), None
        odd_slab = odd_swap(odd_slab)
        even_slab, odd_slab = lax.optimization_barrier((even_slab, odd_slab))
        return tiles + chip_copies(jnp.concatenate(tiles + [even_slab], axis=0)), odd_slab

    encoded, upsampled, up_even, up_odd = call(
        functools.partial(up_kernel, high, slices),
        [((tok_rows, width), BF), cells_bf, slab_bf, slab_bf],
        [cells_f],
        info, vecs, upsample_w, sides, *mixed, smem=1,
    )
    up_even, up_odd = swap(up_even, "seq", 1), odd_swap(up_odd)
    first_conv, tile_one, even_one, odd_one, joined_stack, joined_halo = call(
        first_kernel,
        [cells_f, tile, slab_f, slab_f, ((positions, 6 * channels), BF),
         ((2 * CELLS, 2 * channels), BF)],
        [grid_acc],
        info, onehot, held, masks, upsampled, up_even, up_odd, skip_cells,
        kernel_one, smem=1,
    )
    tiles, odd_one = exchange(tile_one, even_one, odd_one)
    (second_conv, tile_two, even_two, odd_two, act_stack, first_unit, slab_unit, scale_one) = call(
        functools.partial(second_kernel, high),
        [cells_f, tile, slab_f, slab_f, ((positions, 3 * channels), BF), cells_f, slabs_f,
         ((2, depth_total, channels), F32)],
        [grid_acc],
        info, onehot, held, total, masks, first_conv, odd_one, kernel_two, *tiles, smem=1,
    )
    tiles, odd_two = exchange(tile_two, even_two, odd_two)
    decoded_cells, grad_summed, grad_resid, second_unit, slab_two, tile_three, inv_two = call(
        functools.partial(third_kernel, high),
        [cells_bf, cells_f, cells_bf, cells_f, ((2 * CELLS, 2 * channels), F32), tile,
         ((depth_total, channels), F32)],
        [],
        info, onehot, held, total, second_conv, odd_two, joined_stack, joined_halo,
        residual_w, cot_cells, up_even, up_odd, *tiles, smem=1,
    )
    decoded = from_cells(decoded_cells)
    tiles, _ = exchange(tile_three)
    grad_second, grad_back, tile_four, even_four, odd_four = call(
        functools.partial(fourth_kernel, high),
        [cells_bf, cells_f, tile, slab_f, slab_f],
        [grid_acc],
        info, onehot, total, masks, grad_summed, second_unit, inv_two, slab_two, first_unit,
        kernel_two, *tiles, smem=1,
    )

    def tap_grad(stack, upstream, in_chans, left, right, wide_blocks, extra_shape):
        part = 27 * in_chans // count
        extra = extra_shape[0] // count
        dealt = call(
            functools.partial(tap_grad_kernel, in_chans, high, low, wide_blocks),
            [((high, part + wide_blocks * extra, channels), BF)] * low,
            [((9 * channels, positions), BF),
             ((GRID + 2, GRID + 2, depth_total, channels), BF),
             ((count, -(-part // 8) * 8, channels), F32),
             ((count, extra, extra_shape[1]), F32)],
            info, stack, upstream, left, right, smem=1,
        )
        return dealt

    def chip_add(*groups):
        held = sum(group[0].shape[1] for group in groups)
        held = -(-held // 32) * 32 if len(groups) > 1 else held
        kind = [((held, groups[0][0].shape[2]), BF)] * high
        parts = [part for group in groups for part in group]
        return call(functools.partial(chip_add_kernel, high, low), kind, [], *parts)

    class Cube:
        def __init__(self, values):
            self.stage, self.values = 0, values
            if nb == 4:
                self.got = self.split(batch_index % 2, 1)
            else:
                whole = lax.psum(values, "batch")
                half = whole.shape[0] // 2
                self.values, self.got = whole[:half], whole[half:]

        def split(self, bit, mask):
            half = self.values.shape[0] // 2
            sent = lax.dynamic_slice_in_dim(self.values, (1 - bit) * half, half)
            self.values = lax.dynamic_slice_in_dim(self.values, bit * half, half)
            return swap(sent, "batch", mask)

        def step(self):
            if nb != 4:
                return
            self.stage += 1
            if self.stage < 3:
                self.values = sum_list([self.values, self.got]).astype(BF)
            if self.stage == 1:
                self.got = self.split(batch_index // 2, 2)
            elif self.stage == 2:
                self.got = swap(self.values, "batch", 2)
            else:
                self.values = jnp.where(
                    batch_index // 2 == 1,
                    jnp.concatenate([self.got, self.values], axis=0),
                    jnp.concatenate([self.values, self.got], axis=0),
                )
                self.got = swap(self.values, "batch", 1)

    tiles, odd_four = exchange(tile_four, even_four, odd_four)
    two_dealt = tap_grad(
        act_stack, grad_second, channels, joined_stack, grad_resid, 1, (2 * channels, channels)
    )
    grad_first, skip_cells_grad, grad_up_rows, grad_encoded, own_mixed = call(
        functools.partial(fifth_kernel, high, slices),
        [cells_bf, cells_f, ((tok_rows, 8 * channels), BF), ((tok_rows, width), F32),
         ((tok_rows, width), BF)],
        [((GRID, GRID, depth_total, 2 * channels), F32)],
        info, onehot, total, masks, grad_back, first_unit, scale_one, slab_unit, odd_four,
        grad_resid, kernel_one, residual_w, upsample_w, *tiles, smem=1,
    )
    skip_grad = from_cells(skip_cells_grad)

    def pin(first, second):
        if not isinstance(first, (list, tuple)):
            return lax.optimization_barrier((first, second))
        last, second = lax.optimization_barrier((first[-1], second))
        return list(first[:-1]) + [last], second

    grads_mixed = plane_copies(own_mixed)
    two_dealt = list(two_dealt)
    one_dealt = list(tap_grad(
        joined_stack, grad_first, 2 * channels, encoded, grad_up_rows, 8, (width, 8 * channels)
    ))
    grads_mixed, (one_dealt[0], two_dealt[0]) = pin(grads_mixed, (one_dealt[0], two_dealt[0]))
    *inner_parts, grad_expanded = call(
        functools.partial(mix_back_kernel, high),
        partial_kinds + [((rows, hid_span), BF)],
        [],
        reduce_w, expand_w, slope, *grads_mixed,
    )
    inner_parts = [inner_parts[0]] + plane_swaps(inner_parts)
    *mix_dealt, expand_bias_part = call(
        functools.partial(mix_grad_kernel, high, low),
        [((high * shard + hid_shard, width), BF)] * low + [((1, hid_span), F32)],
        [((width, hid_span), F32)],
        info, act, grad_expanded, *grads_mixed, *inners, smem=1,
    )
    mix_dealt = [mix_dealt[0]] + chip_swaps(mix_dealt)
    one_dealt = after(tuple(one_dealt), (grad_expanded,))
    one_dealt = [one_dealt[0]] + chip_swaps(one_dealt)
    inner_parts, one_dealt[1] = pin(inner_parts, one_dealt[1])
    grad_middle, sums, reduce_sum, *branches = call(
        functools.partial(branch_kernel, high, low),
        [((tok_rows, width), F32), ((8, width), F32), ((hid_shard, width), BF)]
        + [((tok_rows + shard, width), BF)] * high,
        [],
        middle, vecs, grad_encoded, own_mixed, *inner_parts, *mix_dealt,
    )
    two_dealt, one_dealt = after((tuple(two_dealt), tuple(one_dealt)), (sums,))
    two_dealt = [two_dealt[0]] + chip_swaps(two_dealt)
    branches = [branches[0]] + plane_swaps(branches)
    reduce_cube = Cube(reduce_sum)
    conv_blocks = chip_add(two_dealt, one_dealt)
    conv_blocks = list(conv_blocks)
    branches, (conv_blocks[1], reduce_cube.got) = pin(
        branches, (conv_blocks[1], reduce_cube.got)
    )
    reduce_cube.step()
    conv_blocks = [conv_blocks[0]] + plane_swaps(conv_blocks)
    mix_cube = Cube(
        call(
            functools.partial(mix_pack_kernel, high, tok_rows),
            [((high * shard, width), BF)],
            [],
            *branches,
        )[0]
    )
    own_dqkv, *dkvs = call(
        functools.partial(attend_back_kernel, high, low, head_dim),
        [((rows, 3 * span), BF)] + [((rows, 2 * span), BF)] * (low - 1),
        [],
        q, crop_q, crop_k, log_total, out_w, *branches, *kvs,
    )
    dkvs[-1], (mix_cube.got, reduce_cube.got) = pin(
        dkvs[-1], (mix_cube.got, reduce_cube.got)
    )
    reduce_cube.step()
    dkvs = chip_swaps([own_dqkv] + dkvs)
    mix_cube.step()
    dkvs, (conv_blocks[1:], reduce_cube.got) = pin(dkvs, (conv_blocks[1:], reduce_cube.got))
    reduce_cube.step()
    conv_cube = Cube(sum_list(conv_blocks).astype(BF))
    expand_bias_part = expand_bias_part.reshape(low, hid_shard // shard, shard)
    expand_bias_part = expand_bias_part.transpose(1, 0, 2).reshape(hid_shard // shard, span)
    joint_outs = call(
        functools.partial(joint_back_kernel, high, low),
        partial_kinds + [((high, shard, wide), BF)] * low,
        [((rows, wide), BF), ((width, wide), F32)],
        info, own_dqkv, normed, joint_w, vecs, sums, expand_bias_part, *dkvs, smem=1,
    )
    normed_parts, joint_dealt = joint_outs[:high], joint_outs[high:]
    joint_dealt, (mix_cube.got, conv_cube.got, reduce_cube.got) = pin(
        joint_dealt, (mix_cube.got, conv_cube.got, reduce_cube.got)
    )
    conv_cube.step()
    mix_cube.step()

    blocks = chip_add([joint_dealt[0]] + chip_swaps(joint_dealt))
    blocks = [blocks[0]] + plane_swaps(blocks)
    out_dealt = call(
        functools.partial(output_grad_kernel, high, low),
        [((shard, width), BF)] * low,
        [((span, width), F32)],
        info, *attended, *branches, smem=1,
    )
    out_dealt = [out_dealt[0]] + chip_swaps(out_dealt)
    blocks, conv_cube.got, mix_cube.got, out_dealt[1] = lax.optimization_barrier(
        (blocks, conv_cube.got, mix_cube.got, out_dealt[1])
    )
    conv_cube.step()
    mix_cube.step()
    tiles = wide // channels
    side_rows = (high * tiles + width // channels) * shard
    side_size = -(-side_rows // (16 * nb)) * 16
    pieces = call(
        functools.partial(side_pack_kernel, high, low),
        [((side_size, channels), BF)] * nb,
        [((side_size * nb, channels), F32)],
        info, *blocks, *out_dealt, smem=1,
    )
    pieces = [pieces[0]] + [swap(pieces[t], "batch", t) for t in range(1, nb)]
    normed_parts = after(tuple(normed_parts), blocks[1:])
    normed_parts = [normed_parts[0]] + plane_swaps(normed_parts)
    pieces, (mix_cube.got, conv_cube.got) = pin(pieces, (mix_cube.got, conv_cube.got))
    conv_cube.step()
    pieces = gather_list(sum_list(pieces).astype(BF))
    tokens_grad = call(
        functools.partial(tokens_kernel, high),
        [((tok_rows, width), F32)],
        [],
        grad_middle, own_tokens, vecs, *normed_parts,
    )[0]
    expand_grad, reduce_grad = call(
        functools.partial(mix_final_kernel, high),
        [((shard, hidden), F32), ((hid_shard, width), F32)],
        [((high * shard, width), F32)],
        info, mix_cube.values, mix_cube.got, reduce_cube.values, reduce_cube.got, smem=1,
    )
    pieces, (expand_grad, reduce_grad, tokens_grad) = pin(
        pieces, (expand_grad, reduce_grad, tokens_grad)
    )
    kernel_two_grad, residual_grad, kernel_one_grad, upsample_grad = call(
        conv_final_kernel,
        [(kernel_second.shape, F32), (residual_weight.shape, F32), (kernel_first.shape, F32),
         ((shard, 8 * channels), F32)],
        [((2 * conv_cube.values.shape[0], channels), F32)],
        info, conv_cube.values, conv_cube.got, smem=1,
    )
    joint_grad, vec_grads, output_grad = call(
        functools.partial(side_final_kernel, high),
        [((shard, 3 * width), F32), ((16, shard), F32), ((shard, width), F32)],
        [((side_size * nb, channels), F32)],
        info, *pieces, smem=1,
    )
    return (
        decoded[None],
        tokens_grad[None],
        skip_grad[None],
        vec_grads[0],
        vec_grads[1],
        joint_grad,
        vec_grads[2],
        vec_grads[3],
        output_grad,
        vec_grads[4],
        vec_grads[5],
        vec_grads[6],
        expand_grad,
        vec_grads[8 : 8 + hid_shard // shard].reshape(hid_shard),
        reduce_grad,
        vec_grads[7],
        upsample_grad,
        kernel_one_grad,
        kernel_two_grad,
        residual_grad,
    )


def solution(mesh):
    rows = P("batch", "seq", None)
    vec = P("seq")
    mat = P("seq", None)
    in_specs = (rows, rows, rows, P("batch", None))
    in_specs += (vec, vec, mat, vec, vec, mat, vec, vec, vec, mat, vec, mat, vec)
    in_specs += (mat, mat, mat, mat)
    out_specs = (rows, rows, rows)
    out_specs += (vec, vec, mat, vec, vec, mat, vec, vec, vec, mat, vec, mat, vec)
    out_specs += (mat, mat, mat, mat)
    return jax.shard_map(
        on_device, mesh=mesh, in_specs=in_specs, out_specs=out_specs, check_vma=False
    )
```

```python
import functools
import math

import jax
import jax.numpy as jnp
from jax import lax
from jax.experimental import pallas as pl
from jax.experimental.pallas import tpu as pltpu
from jax.sharding import PartitionSpec as P

HEADS = 12
PH = 4
CROPS = 4


LIMITS = {
    "attend_back_kernel": 60,
    "joint_back_kernel": 60,
    "attend_kernel": 22,
    "tap_grad_kernel": 18,
}
EPS_LAYER = 1e-06
EPS_CROP = 1e-05
BF = jnp.bfloat16
F32 = jnp.float32


def crops_of(lengths, indices):
    crop_ends = jnp.cumsum(lengths)
    return jnp.sum((indices[:, None] >= crop_ends[None, :]).astype(jnp.int32), axis=1)


def swap(values, axis, mask):
    count = lax.axis_size(axis)
    return lax.ppermute(values, axis, [(i, i ^ mask) for i in range(count)])


def gather_rel(values, axis, stride, count):
    return jnp.stack([values] + [swap(values, axis, m * stride) for m in range(1, count)])


def pick(blocks, index):
    return lax.dynamic_index_in_dim(blocks, index, 0, keepdims=False)


def unxor(blocks, index):
    count = blocks.shape[0]
    bits = count.bit_length() - 1
    tail = blocks.shape[1:]
    cube = blocks.reshape((2,) * bits + tail)
    for bit in range(bits):
        dim = bits - 1 - bit
        cube = jnp.where(((index >> bit) & 1) == 1, jnp.flip(cube, dim), cube)
    return cube.reshape(blocks.shape)


def deal_rel(blocks, axis, stride, index):
    count = blocks.shape[0]
    return [pick(blocks, index)] + [
        swap(pick(blocks, index ^ m), axis, m * stride) for m in range(1, count)
    ]


def sum_list(parts):
    total = parts[0].astype(F32)
    for part in parts[1:]:
        total = total + part.astype(F32)
    return total


def batch_sum(values):
    count = lax.axis_size("batch")
    if count == 1:
        return values.astype(F32)
    index = lax.axis_index("batch")
    rows = values.shape[0]
    piece = -(-rows // count)
    if piece * count > rows:
        values = jnp.pad(values, ((0, piece * count - rows), (0, 0)))
    pieces = values.reshape((count, piece) + values.shape[1:])
    own = sum_list(deal_rel(pieces, "batch", 1, index)).astype(BF)
    total = unxor(gather_rel(own, "batch", 1, count), index)
    return total.reshape(values.shape)[:rows].astype(F32)


def call(kernel, outs, scratch, *args, smem=0):
    name = getattr(kernel, "func", kernel).__name__
    limit = LIMITS.get(name, 12)
    return pl.pallas_call(
        kernel,
        out_shape=tuple(jax.ShapeDtypeStruct(shape, kind) for shape, kind in outs),
        in_specs=[pl.BlockSpec(memory_space=pltpu.SMEM)] * smem
        + [pl.BlockSpec(memory_space=pltpu.VMEM)] * (len(args) - smem),
        scratch_shapes=[pltpu.VMEM(shape, kind) for shape, kind in scratch],
        compiler_params=pltpu.CompilerParams(vmem_limit_bytes=limit * 1024 * 1024),
        name=name,
    )(*args)


GRID = 2 * PH
CELLS = GRID * GRID
ERF_TOP = (
    0.00022905065861350646,
    0.0034082910107109506,
    0.050955695062380861,
    0.18520832239976145,
    1.128379143519084,
)
ERF_LOW = (
    -1.1791602954361697e-7,
    0.000023547966471313185,
    0.0010179625278914885,
    0.014070470171167667,
    0.11098505178285362,
    0.49746925110067538,
    1.0,
)


def normal_cdf(values):
    arg = jnp.clip(values * math.sqrt(0.5), -3.832506856900711, 3.832506856900711)
    square = arg * arg
    top = jnp.full_like(square, ERF_TOP[0])
    for coef in ERF_TOP[1:]:
        top = top * square + coef
    bottom = jnp.full_like(square, ERF_LOW[0])
    for coef in ERF_LOW[1:]:
        bottom = bottom * square + coef
    return 0.5 + 0.5 * (arg * top / bottom)


def gelu_slope(values, cdf):
    return cdf + values * (jnp.exp(-0.5 * values * values) * (1.0 / math.sqrt(2.0 * math.pi)))


def depth_shifts(cells, prev, following, up, down):
    half = cells.shape[1] // 2
    even, odd = cells[:, :half], cells[:, half:]
    row = lax.broadcasted_iota(jnp.int32, even.shape, 1)
    ahead = jnp.where(row == half - 1, following[:, None, :], pltpu.roll(even, half - 1, 1))
    behind = jnp.where(row == 0, prev[:, None, :], pltpu.roll(odd, 1, 1))
    return (
        jnp.concatenate([behind * down[None], even], axis=1),
        jnp.concatenate([odd, ahead * up[None]], axis=1),
    )


def flat_rows(cells):
    return cells.reshape(cells.shape[0] * cells.shape[1], cells.shape[2])


def deep(rows):
    return rows.reshape(CELLS, rows.shape[0] // CELLS, rows.shape[1])


def tap_add(acc_ref, field, tap, sign):
    step_i, step_j = sign * (tap // 3 - 1), sign * (tap % 3 - 1)
    depth = acc_ref.shape[2]
    field = field.reshape(GRID, GRID, depth, field.shape[1])
    low_i, high_i = max(0, -step_i), GRID - max(0, step_i)
    low_j, high_j = max(0, -step_j), GRID - max(0, step_j)
    acc_ref[low_i:high_i, low_j:high_j] += field[
        low_i + step_i : high_i + step_i, low_j + step_j : high_j + step_j
    ]


def conv_into(acc_ref, stack, weight_ref, in_chans):
    taps = [4, 0, 1, 2, 3, 5, 6, 7, 8]

    def matrix(tap):
        return jnp.concatenate(
            [
                weight_ref[(layer * 9 + tap) * in_chans : (layer * 9 + tap + 1) * in_chans, :]
                for layer in range(3)
            ],
            axis=0,
        )

    out = weight_ref.shape[1]
    acc_ref[...] = jnp.zeros_like(acc_ref)
    for start in range(0, 9, 2):
        pair = taps[start : start + 2]
        rhs = jnp.concatenate([matrix(tap) for tap in pair], axis=1)
        field = jnp.dot(stack, rhs, preferred_element_type=F32)
        for place, tap in enumerate(pair):
            tap_add(acc_ref, field[:, place * out : (place + 1) * out], tap, 1)


def turned_into(acc_ref, stack, weight_ref, in_chans):
    taps = [4, 0, 1, 2, 3, 5, 6, 7, 8]

    def matrix(tap):
        return jnp.concatenate(
            [
                weight_ref[(layer * 9 + tap) * in_chans : (layer * 9 + tap + 1) * in_chans, :]
                for layer in (2, 1, 0)
            ],
            axis=1,
        )

    acc_ref[...] = jnp.zeros_like(acc_ref)
    step = max(1, 256 // in_chans)
    for start in range(0, 9, step):
        pair = taps[start : start + step]
        rhs = jnp.concatenate([matrix(tap) for tap in pair], axis=0)
        field = lax.dot_general(
            stack, rhs, (((1,), (1,)), ((), ())), preferred_element_type=F32
        )
        for place, tap in enumerate(pair):
            tap_add(acc_ref, field[:, place * in_chans : (place + 1) * in_chans], tap, -1)


def send_slabs(values_ref, parity, even_ref, odd_ref):
    depth = values_ref.shape[0] // CELLS
    top = values_ref[pl.ds(depth - 1, CELLS, stride=depth), :]
    bottom = values_ref[pl.ds(0, CELLS, stride=depth), :]
    even_ref[...] = jnp.where(parity == 0, top, bottom)
    odd_ref[...] = jnp.where(parity == 0, bottom, top)


def place_slabs(parity, from_even, from_odd):
    return (
        jnp.where(parity == 0, from_odd, from_even),
        jnp.where(parity == 0, from_even, from_odd),
    )


def spread(onehot_ref, per_crop):
    total = onehot_ref[0] * per_crop[0:1]
    for crop in range(1, CROPS):
        total = total + onehot_ref[crop] * per_crop[crop : crop + 1]
    return total


def crop_fold(onehot_ref, per_depth):
    return [
        jnp.sum(onehot_ref[crop] * per_depth, axis=0, keepdims=True) for crop in range(CROPS)
    ]


def moment_tile(onehot_ref, count_ref, cells, tile_ref):
    per_slice = float(cells.shape[0])
    sums = jnp.sum(cells, axis=0)
    about = cells - (sums * (1.0 / per_slice))[None]
    devs = jnp.sum(about * about, axis=0)
    totals = crop_fold(onehot_ref, sums)
    for crop in range(CROPS):
        mean = totals[crop] / jnp.maximum(count_ref[0, crop : crop + 1], 1.0)
        off = sums * (1.0 / per_slice) - mean
        tile_ref[crop : crop + 1] = totals[crop]
        tile_ref[CROPS + crop : CROPS + crop + 1] = jnp.sum(
            onehot_ref[crop] * (devs + per_slice * off * off), axis=0, keepdims=True
        )


def sum_tile(onehot_ref, first, second, tile_ref):
    for start, field in ((0, first), (CROPS, second)):
        totals = crop_fold(onehot_ref, jnp.sum(field, axis=0))
        for crop in range(CROPS):
            tile_ref[start + crop : start + crop + 1] = totals[crop]


def tile_list(tile_refs, high):
    tiles = [ref[...] for ref in tile_refs[:high]]
    for ref in tile_refs[high:]:
        tiles += [ref[8 * m : 8 * m + 8, :] for m in range(high)]
    return tiles


def merged_moments(tiles, count_ref, total_ref):
    total = total_ref[...]
    sums = tiles[0][:CROPS]
    devs = tiles[0][CROPS:]
    for tile in tiles[1:]:
        sums = sums + tile[:CROPS]
        devs = devs + tile[CROPS:]
    mean = sums / total
    for place, tile in enumerate(tiles):
        held = count_ref[place]
        off = tile[:CROPS] / jnp.maximum(held, 1.0) - mean
        devs = devs + held * off * off
    return mean, lax.rsqrt(devs / total + EPS_CROP)


def merged_sums(tiles, total_ref):
    both = tiles[0]
    for tile in tiles[1:]:
        both = both + tile
    total = total_ref[...]
    return both[:CROPS] / total, both[CROPS:] / total


def stack_rows(cells, prev, following, up, down):
    behind, ahead = depth_shifts(cells, prev, following, up, down)
    return [flat_rows(part).astype(BF) for part in (behind, cells, ahead)]


def up_kernel(
    high, slices, info, vec_ref, weight_ref, side_ref, *refs
):
    parts, (enc_ref, up_ref, even_ref, odd_ref, grid_ref) = refs[:high], refs[high:]
    encoded = (plane_total(parts) + vec_ref[7:8, :]).astype(BF)
    enc_ref[...] = encoded
    tok_rows = encoded.shape[0]
    plane = tok_rows // slices
    chans = up_ref.shape[1]
    ordered = jnp.dot(
        token_order(tok_rows, slices, False), encoded, preferred_element_type=F32
    ).astype(BF)
    rows = jnp.dot(ordered, weight_ref[...], preferred_element_type=F32)
    depth = 2 * slices
    for cell in range(plane):
        for place in range(8):
            part_a, part_b, part_e = place // 4, (place // 2) % 2, place % 2
            at = (2 * (cell // PH) + part_b) * GRID + 2 * (cell % PH) + part_e
            grid_ref[at * depth + part_a * slices : at * depth + (part_a + 1) * slices, :] = rows[
                cell * slices : (cell + 1) * slices, place * chans : (place + 1) * chans
            ]
    parity = info[0]
    top = grid_ref[pl.ds(depth - 1, CELLS, stride=depth), :]
    bottom = grid_ref[pl.ds(0, CELLS, stride=depth), :]
    even_ref[:, :chans] = jnp.where(parity == 0, top, bottom).astype(BF)
    odd_ref[:, :chans] = jnp.where(parity == 0, bottom, top).astype(BF)

    @pl.when(parity == 0)
    def _():
        even_ref[:, chans:] = side_ref[CELLS:, :]
        odd_ref[:, chans:] = side_ref[:CELLS, :]

    @pl.when(parity != 0)
    def _():
        even_ref[:, chans:] = side_ref[:CELLS, :]
        odd_ref[:, chans:] = side_ref[CELLS:, :]

    up_ref[...] = grid_ref[...].astype(BF)


def first_kernel(
    info, onehot, count_ref, masks, up_ref, from_even, from_odd, skip_ref,
    weight_ref, conv_ref, tile_ref, even_ref, odd_ref, stack_ref, halo_ref, acc_ref,
):
    parity = info[0]
    down, up = masks[0], masks[1]
    chans = up_ref.shape[1]
    up_halo = place_slabs(
        parity, from_even[:, :chans].astype(F32), from_odd[:, :chans].astype(F32)
    )
    skip_halo = place_slabs(
        parity,
        from_even[:, chans : 2 * chans].astype(F32),
        from_odd[:, chans : 2 * chans].astype(F32),
    )
    parts_up = stack_rows(deep(up_ref[...].astype(F32)), *up_halo, up, down)
    parts_skip = stack_rows(deep(skip_ref[...].astype(F32)), *skip_halo, up, down)
    for layer in range(3):
        at = 2 * layer * chans
        stack_ref[:, at : at + chans] = parts_up[layer]
        stack_ref[:, at + chans : at + 2 * chans] = parts_skip[layer]
    for side in range(2):
        halo_ref[side * CELLS : (side + 1) * CELLS, :chans] = up_halo[side].astype(BF)
        halo_ref[side * CELLS : (side + 1) * CELLS, chans:] = skip_halo[side].astype(BF)
    conv_into(acc_ref, stack_ref[...], weight_ref, 2 * chans)
    conv_ref[...] = acc_ref[...].reshape(conv_ref.shape)
    moment_tile(onehot, count_ref, deep(conv_ref[...]), tile_ref)
    send_slabs(conv_ref, parity, even_ref, odd_ref)


def second_kernel(
    high, info, onehot, count_ref, total_ref, masks, conv_one, odd_slab, weight_ref, *refs
):
    n_out = 8
    tiles, outs = refs[: -n_out - 1], refs[-n_out - 1 :]
    conv_ref, tile_ref, even_ref, odd_ref, stack_ref, unit_ref, slab_unit_ref, scale_ref, acc_ref = outs
    parity = info[0]
    down, up = masks[0], masks[1]
    mean, inv = merged_moments(tile_list(tiles, high), count_ref, total_ref)
    mean_z, inv_z = spread(onehot, mean), spread(onehot, inv)
    scale_ref[0] = mean_z
    scale_ref[1] = inv_z
    unit = (deep(conv_one[...]) - mean_z[None]) * inv_z[None]
    unit_ref[...] = flat_rows(unit)
    act = unit * normal_cdf(unit)
    halo = place_slabs(parity, tiles[high][8 * high :, :], odd_slab[...])
    depth = mean_z.shape[0]
    sides = []
    for side, at in ((0, 0), (1, depth - 1)):
        part = (halo[side] - mean_z[at : at + 1]) * inv_z[at : at + 1]
        slab_unit_ref[side * CELLS : (side + 1) * CELLS, :] = part
        sides.append(part * normal_cdf(part))
    parts = stack_rows(act, sides[0], sides[1], up, down)
    chans = conv_one.shape[1]
    for layer in range(3):
        stack_ref[:, layer * chans : (layer + 1) * chans] = parts[layer]
    conv_into(acc_ref, stack_ref[...], weight_ref, chans)
    conv_ref[...] = acc_ref[...].reshape(conv_ref.shape)
    moment_tile(onehot, count_ref, deep(conv_ref[...]), tile_ref)
    send_slabs(conv_ref, parity, even_ref, odd_ref)


def third_kernel(
    high, info, onehot, count_ref, total_ref, conv_two, odd_slab, stack_ref, halo_ref,
    weight_ref, cot_ref, cot_even, cot_odd, *refs
):
    n_out = 7
    tiles, outs = refs[:-n_out], refs[-n_out:]
    decoded_ref, grad_ref, low_ref, unit_ref, slab_ref, tile_ref, inv_ref = outs
    parity = info[0]
    chans = conv_two.shape[1]
    mean, inv = merged_moments(tile_list(tiles, high), count_ref, total_ref)
    mean_z, inv_z = spread(onehot, mean), spread(onehot, inv)
    inv_ref[...] = inv_z
    unit = flat_rows((deep(conv_two[...]) - mean_z[None]) * inv_z[None])
    unit_ref[...] = unit
    joined = stack_ref[:, 2 * chans : 4 * chans]
    summed = unit + jnp.dot(joined, weight_ref[...], preferred_element_type=F32)
    cdf = normal_cdf(summed)
    decoded_ref[...] = (summed * cdf).astype(BF)
    grad = cot_ref[...].astype(F32) * gelu_slope(summed, cdf)
    grad_ref[...] = grad
    low_ref[...] = grad.astype(BF)
    sum_tile(onehot, deep(grad), deep(grad * unit), tile_ref)
    halo = place_slabs(parity, tiles[high][8 * high :, :], odd_slab[...])
    cots = place_slabs(
        parity, cot_even[:, 2 * chans :].astype(F32), cot_odd[:, 2 * chans :].astype(F32)
    )
    depth = mean_z.shape[0]
    for side, at in ((0, 0), (1, depth - 1)):
        rows = slice(side * CELLS, (side + 1) * CELLS)
        part = (halo[side] - mean_z[at : at + 1]) * inv_z[at : at + 1]
        both = part + jnp.dot(halo_ref[rows, :], weight_ref[...], preferred_element_type=F32)
        slab_ref[rows, :chans] = part
        slab_ref[rows, chans:] = cots[side] * gelu_slope(both, normal_cdf(both))


def fourth_kernel(
    high, info, onehot, total_ref, masks, grad_ref, unit_two, inv_two, slab_two, unit_one,
    weight_ref, *refs
):
    n_out = 5
    tiles, outs = refs[: -n_out - 1], refs[-n_out - 1 :]
    second_ref, back_ref, tile_ref, even_ref, odd_ref, acc_ref = outs
    parity = info[0]
    down, up = masks[0], masks[1]
    chans = grad_ref.shape[1]
    first, cross = merged_sums(tile_list(tiles, high), total_ref)
    first_z, cross_z, inv_z = spread(onehot, first), spread(onehot, cross), inv_two[...]
    grad = deep(grad_ref[...]) - first_z[None] - deep(unit_two[...]) * cross_z[None]
    grad = grad * inv_z[None]
    depth = inv_z.shape[0]
    sides = []
    for side, at in ((0, 0), (1, depth - 1)):
        rows = slice(side * CELLS, (side + 1) * CELLS)
        part = slab_two[rows, chans:] - first_z[at : at + 1]
        part = part - slab_two[rows, :chans] * cross_z[at : at + 1]
        sides.append(part * inv_z[at : at + 1])
    parts = stack_rows(grad, sides[0], sides[1], up, down)
    second_ref[...] = parts[1]
    turned_into(acc_ref, jnp.concatenate(parts, axis=1), weight_ref, chans)
    unit = unit_one[...]
    back = acc_ref[...].reshape(back_ref.shape) * gelu_slope(unit, normal_cdf(unit))
    back_ref[...] = back
    sum_tile(onehot, deep(back), deep(back * unit), tile_ref)
    send_slabs(back_ref, parity, even_ref, odd_ref)


def fifth_kernel(
    high, slices, info, onehot, total_ref, masks, back_ref, unit_one, scale_one, slab_one,
    odd_slab, low_ref, weight_ref, resid_ref, up_weight_ref, *refs
):
    n_out = 5
    tiles, outs = refs[: -n_out - 1], refs[-n_out - 1 :]
    first_ref, skip_ref, rows_ref, encoded_ref, mixed_ref, acc_ref = outs
    parity = info[0]
    down, up = masks[0], masks[1]
    chans = back_ref.shape[1]
    first, cross = merged_sums(tile_list(tiles, high), total_ref)
    first_z, cross_z, inv_z = spread(onehot, first), spread(onehot, cross), scale_one[1]
    grad = deep(back_ref[...]) - first_z[None] - deep(unit_one[...]) * cross_z[None]
    grad = grad * inv_z[None]
    halo = place_slabs(parity, tiles[high][8 * high :, :], odd_slab[...])
    depth = inv_z.shape[0]
    sides = []
    for side, at in ((0, 0), (1, depth - 1)):
        rows = slice(side * CELLS, (side + 1) * CELLS)
        part = halo[side] - first_z[at : at + 1] - slab_one[rows, :] * cross_z[at : at + 1]
        sides.append(part * inv_z[at : at + 1])
    parts = stack_rows(grad, sides[0], sides[1], up, down)
    first_ref[...] = parts[1]
    turned_into(acc_ref, jnp.concatenate(parts, axis=1), weight_ref, 2 * chans)
    field = acc_ref[...].reshape(back_ref.shape[0], 2 * chans) + lax.dot_general(
        low_ref[...], resid_ref[...], (((1,), (1,)), ((), ())), preferred_element_type=F32
    )
    skip_ref[...] = field[:, chans:]
    plane = PH * PH
    columns = []
    for place in range(8):
        part_a, part_b, part_e = place // 4, (place // 2) % 2, place % 2
        pieces = []
        for cell in range(plane):
            at = (2 * (cell // PH) + part_b) * GRID + 2 * (cell % PH) + part_e
            low = at * depth + part_a * slices
            pieces.append(field[low : low + slices, :chans])
        columns.append(jnp.concatenate(pieces, axis=0))
    up_rows = jnp.concatenate(columns, axis=1).astype(BF)
    rows_ref[...] = jnp.dot(
        token_order(plane * slices, slices, True), up_rows, preferred_element_type=F32
    ).astype(BF)
    encoded = lax.dot_general(
        rows_ref[...], up_weight_ref[...], (((1,), (1,)), ((), ())), preferred_element_type=F32
    )
    encoded_ref[...] = encoded
    mixed_ref[...] = encoded.astype(BF)


def tap_grad_kernel(
    in_chans, high, low, wide, info, stack_ref, grad_ref, left_ref, right_ref, *refs
):
    outs, (turned_ref, pad_ref, rows_ref, extra_ref) = refs[:low], refs[low:]
    chans = grad_ref.shape[1]
    count = high * low
    shard = 27 * in_chans // count
    depth = grad_ref.shape[0] // CELLS
    pad_ref[...] = jnp.zeros_like(pad_ref)
    pad_ref[1 : GRID + 1, 1 : GRID + 1] = grad_ref[...].reshape(GRID, GRID, depth, chans)
    for tap in range(9):
        low_i, low_j = 2 - tap // 3, 2 - tap % 3
        moved = pad_ref[low_i : low_i + GRID, low_j : low_j + GRID]
        turned_ref[tap * chans : (tap + 1) * chans, :] = moved.reshape(-1, chans).T
    for layer in range(3):
        at = layer * in_chans
        product = jnp.dot(
            turned_ref[...], stack_ref[:, at : at + in_chans], preferred_element_type=F32
        )
        for tap in range(9):
            block = product[tap * chans : (tap + 1) * chans, :].T
            start = (layer * 9 + tap) * in_chans
            done = 0
            while done < in_chans:
                owner, place = divmod(start + done, shard)
                size = min(in_chans - done, shard - place)
                rows_ref[owner, place : place + size, :] = block[done : done + size, :]
                done += size
    extra = extra_ref.shape[1]
    left = left_ref[...]
    if wide == 1:
        left = left[:, 2 * chans : 4 * chans]
    extra_ref[...] = cross_rows(left, right_ref[...]).reshape(extra_ref.shape)
    for s in range(low):
        for m in range(high):
            owner = (info[1] ^ m) * low + (info[2] ^ s)
            outs[s][m, :shard, :] = rows_ref[owner][:shard].astype(BF)
            other = extra_ref[owner].astype(BF)
            for place in range(wide):
                start = shard + place * extra
                outs[s][m, start : start + extra, :] = other[
                    :, place * chans : (place + 1) * chans
                ]


def pack_kernel(high, info, token_ref, joint_ref, expand_ref, out_w_ref, *refs):
    vecs, joints, expands = refs[: -2 * high], refs[-2 * high : -high], refs[-high:]
    span = joint_ref.shape[1] // (3 * high)
    third = joint_ref.shape[1] // 3
    wide = expand_ref.shape[1] // high
    rows = token_ref.shape[0]
    shard = joint_ref.shape[0]
    lines = [ref[...] for ref in vecs]
    lines.append(jnp.zeros((128 - sum(line.shape[0] for line in lines), shard), F32))
    columns = jnp.concatenate(lines, axis=0).T[:, :64].astype(BF)
    top = 3 * span + 64
    for own in range(high):

        @pl.when(info[1] == own)
        def _():
            for m in range(high):
                group = own ^ m
                joints[m][:rows, :] = token_ref[...]
                for part in range(3):
                    joints[m][rows:, part * span : (part + 1) * span] = joint_ref[
                        :, part * third + group * span : part * third + (group + 1) * span
                    ]
                joints[m][rows:, 3 * span : top] = columns
                if top < joints[m].shape[1]:
                    joints[m][rows:, top:] = jnp.zeros(
                        (joint_ref.shape[0], joints[m].shape[1] - top), BF
                    )
                expands[m][0] = expand_ref[:, group * wide : (group + 1) * wide]
                expands[m][1] = out_w_ref[...]


def assembled(info, high, low, natural, parts, scratch_ref):
    rows = scratch_ref.shape[1]
    for s in range(low):
        for m in range(high):
            block = parts[m][...] if s == 0 else parts[high + s - 1][m * rows : (m + 1) * rows, :]
            major = (info[1] ^ m) if natural else m
            scratch_ref[major * low + (info[2] ^ s)] = block.astype(F32)


def order_kernel(high, low, natural, info, *refs):
    parts, out_ref, scratch_ref = refs[:-2], refs[-2], refs[-1]
    assembled(info, high, low, natural, parts, scratch_ref)
    out_ref[...] = scratch_ref[...].reshape(out_ref.shape).astype(BF)


def pair_kernel(high, low, info, *refs):
    parts, (expand_ref, out_ref, scratch_ref) = refs[:-3], refs[-3:]
    for slab, natural, place in ((0, True, expand_ref), (1, False, out_ref)):
        for s in range(low):
            for m in range(high):
                block = parts[m][slab] if s == 0 else parts[high + s - 1][m, slab]
                major = (info[1] ^ m) if natural else m
                scratch_ref[major * low + (info[2] ^ s)] = block.astype(F32)
        place[...] = scratch_ref[...].reshape(place.shape).astype(BF)


def unit_rows_of(values):
    average = jnp.mean(values, axis=-1, keepdims=True)
    centred = values - average
    inv_std = lax.rsqrt(jnp.mean(centred * centred, axis=-1, keepdims=True) + EPS_LAYER)
    return centred * inv_std, inv_std


def query_kernel(high, low, info, *refs):
    tokens, partners = refs[:high], refs[high : high + low - 1]
    q_ref, kv_ref, normed_ref, weight_ref, vec_ref, own_vec_ref, scratch_ref = refs[-7:]
    width = normed_ref.shape[1]
    wide = weight_ref.shape[1]
    span = q_ref.shape[1]
    rows = normed_ref.shape[0] // (2 * high)
    own_parts = [ref.at[rows:, :wide] for ref in tokens]
    assembled(info, high, low, True, own_parts + list(partners), scratch_ref)
    weight = scratch_ref[...].reshape(width, wide)
    weight_ref[...] = weight.astype(BF)
    turned = weight[:, wide - 128 :].T
    vec_ref[...] = turned[64:80, :]
    own = scratch_ref[pl.ds(info[1] * low, low), :, :][:, :, wide - 128 :]
    own_turned = own.reshape(width // high, 128).T
    own_vec_ref[...] = own_turned[64:80, :]
    gain, shift = turned[64:65, :], turned[65:66, :]
    for m in range(high):
        unit, _ = unit_rows_of(tokens[m][:rows, :].astype(F32))
        normed_ref[m * rows : (m + 1) * rows, :] = (unit * gain + shift).astype(BF)
        normed_ref[(high + m) * rows : (high + m + 1) * rows, :] = unit.astype(BF)
    joint = jnp.dot(
        normed_ref[: high * rows, :], weight_ref[...], preferred_element_type=F32
    )
    q_ref[...] = (joint[:, :span] + own_turned[66:67, :]).astype(BF)
    kv_ref[:, :span] = joint[:, span : 2 * span].astype(BF)
    kv_ref[:, span:] = (joint[:, 2 * span : 3 * span] + own_turned[67:68, :]).astype(BF)


def head_columns(refs, start, head_dim):
    return jnp.concatenate([ref[:, start : start + head_dim] for ref in refs], axis=0)


def masked_scores(keys, queries, same):
    scores = lax.dot_general(
        keys, queries, (((1,), (1,)), ((), ())), preferred_element_type=F32
    )
    return jnp.where(same, scores, -1000000000.0)


def attend_kernel(high, head_dim, q_ref, crop_q, crop_k, *refs):
    kvs, outs = refs[: -high - 1], refs[-high - 1 :]
    log_ref = outs[-1]
    span = q_ref.shape[1]
    same = crop_k[...] == crop_q[...]
    scale = 1.0 / math.sqrt(head_dim)
    pieces = []
    for head in range(span // head_dim):
        at = head * head_dim
        queries = q_ref[:, at : at + head_dim] * jnp.asarray(scale, BF)
        scores = masked_scores(head_columns(kvs, at, head_dim), queries, same)
        highest = jnp.max(scores, axis=0, keepdims=True)
        powers = jnp.exp(scores - highest)
        sums = jnp.sum(powers, axis=0, keepdims=True)
        log_ref[head : head + 1, :] = highest + jnp.log(sums)
        share = (powers * (1.0 / sums)).astype(BF)
        values = head_columns(kvs, span + at, head_dim)
        pieces.append(jnp.dot(values.T, share, preferred_element_type=F32))
    attended = jnp.concatenate(pieces, axis=0).T.astype(BF)
    rows = outs[0].shape[0]
    for m in range(high):
        outs[m][...] = attended[m * rows : (m + 1) * rows, :]


def middle_kernel(high, token_ref, weight_ref, vec_ref, *refs):
    parts, (middle_ref, inner_ref) = refs[:high], refs[high:]
    span = parts[0].shape[1]
    middle = token_ref[...].astype(F32) + vec_ref[4:5, :]
    for m in range(high):
        middle = middle + jnp.dot(
            parts[m][...], weight_ref[m * span : (m + 1) * span, :], preferred_element_type=F32
        )
    middle_ref[...] = middle
    unit, _ = unit_rows_of(middle)
    inner_ref[...] = (unit * vec_ref[5:6, :] + vec_ref[6:7, :]).astype(BF)


def mix_kernel(high, middle_ref, expand_ref, reduce_ref, bias_ref, *refs):
    parts, outs = refs[:high], refs[high:]
    act_ref, slope_ref = outs[high], outs[high + 1]
    rows = parts[0].shape[0]
    for m in range(high):
        at = slice(m * rows, (m + 1) * rows)
        expanded = bias_ref[...] + jnp.dot(
            parts[m][...], expand_ref[...], preferred_element_type=F32
        )
        cdf = normal_cdf(expanded)
        act = (expanded * cdf).astype(BF)
        act_ref[at, :] = act
        slope_ref[at, :] = gelu_slope(expanded, cdf)
        mixed = jnp.dot(act, reduce_ref[...], preferred_element_type=F32)
        if m == 0:
            mixed = mixed + middle_ref[...]
        outs[m][...] = mixed.astype(outs[m].dtype)


def plane_total(parts):
    total = parts[0][...]
    for ref in parts[1:]:
        total = total + ref[...].astype(F32)
    return total


def token_order(tok_rows, slices, back):
    plane = tok_rows // slices
    row = lax.broadcasted_iota(jnp.int32, (tok_rows, tok_rows), 0)
    col = lax.broadcasted_iota(jnp.int32, (tok_rows, tok_rows), 1)
    if back:
        row, col = col, row
    return jnp.where(col == (row % slices) * plane + row // slices, 1.0, 0.0).astype(BF)


def mix_back_kernel(high, reduce_ref, expand_ref, slope_ref, *refs):
    parts, outs = refs[:high], refs[high:]
    grad_ref = outs[high]
    rows = parts[0].shape[0]
    for m in range(high):
        at = slice(m * rows, (m + 1) * rows)
        grad = lax.dot_general(
            parts[m][...], reduce_ref[...], (((1,), (1,)), ((), ())), preferred_element_type=F32
        )
        grad = (grad * slope_ref[at, :]).astype(BF)
        grad_ref[at, :] = grad
        back = lax.dot_general(
            grad, expand_ref[...], (((1,), (1,)), ((), ())), preferred_element_type=F32
        )
        outs[m][...] = back.astype(outs[m].dtype)


def cross_rows(first, second):
    return lax.dot_general(first, second, (((0,), (0,)), ((), ())), preferred_element_type=F32)


def deal_rows(info, high, low, scratch_ref, outs):
    shard = outs[0].shape[1]
    for s in range(low):
        for m in range(high):
            at = ((info[1] ^ m) * low + (info[2] ^ s)) * shard
            outs[s][m] = scratch_ref[pl.ds(pl.multiple_of(at, 8), shard), :].astype(BF)


def deal_chip(info, low, scratch_ref, outs):
    shard = outs[0].shape[0]
    for s in range(low):
        at = (info[2] ^ s) * shard
        outs[s][...] = scratch_ref[pl.ds(pl.multiple_of(at, 8), shard), :].astype(BF)


def mix_grad_kernel(high, low, info, act_ref, grad_ref, *refs):
    mixed = jnp.concatenate([ref[...] for ref in refs[:high]], axis=0)
    inner = jnp.concatenate([ref[...] for ref in refs[high : 2 * high]], axis=0)
    outs = refs[2 * high :]
    bias_ref, scratch_ref = outs[low], outs[low + 1]
    hid_shard = scratch_ref.shape[0] // low
    shard = (outs[0].shape[0] - hid_shard) // high
    scratch_ref[...] = cross_rows(inner, grad_ref[...])
    for s in range(low):
        for m in range(high):
            at = ((info[1] ^ m) * low + (info[2] ^ s)) * shard
            outs[s][m * shard : (m + 1) * shard, :] = scratch_ref[
                pl.ds(pl.multiple_of(at, 8), shard), :
            ].astype(BF)
    scratch_ref[...] = cross_rows(act_ref[...], mixed)
    for s in range(low):
        at = (info[2] ^ s) * hid_shard
        outs[s][high * shard :, :] = scratch_ref[
            pl.ds(pl.multiple_of(at, 8), hid_shard), :
        ].astype(BF)
    bias_ref[...] = jnp.sum(grad_ref[...].astype(F32), axis=0, keepdims=True)


def norm_back(upstream, unit, inv_std, gain):
    scaled = upstream * gain
    return inv_std * (
        scaled
        - jnp.mean(scaled, axis=-1, keepdims=True)
        - unit * jnp.mean(scaled * unit, axis=-1, keepdims=True)
    )


def branch_kernel(high, low, middle_ref, vec_ref, encoded_ref, mixed_ref, *refs):
    parts, dealt = refs[:high], refs[high : high + low]
    grad_ref, sums_ref, reduce_ref = refs[high + low : high + low + 3]
    outs = refs[high + low + 3 :]
    inner = plane_total(parts)
    unit, inv_std = unit_rows_of(middle_ref[...])
    grad = encoded_ref[...] + norm_back(inner, unit, inv_std, vec_ref[5:6, :])
    grad_ref[...] = grad
    branch = grad.astype(BF)
    rows = branch.shape[0]
    shard = outs[0].shape[0] - rows
    for m in range(high):
        outs[m][:rows, :] = branch
        total = dealt[0][m * shard : (m + 1) * shard, :].astype(F32)
        for ref in dealt[1:]:
            total = total + ref[m * shard : (m + 1) * shard, :].astype(F32)
        outs[m][rows:, :] = total.astype(BF)
    total = dealt[0][high * shard :, :].astype(F32)
    for ref in dealt[1:]:
        total = total + ref[high * shard :, :].astype(F32)
    reduce_ref[...] = total.astype(BF)
    sums_ref[...] = jnp.zeros_like(sums_ref)
    sums_ref[4:5, :] = jnp.sum(branch.astype(F32), axis=0, keepdims=True)
    sums_ref[5:6, :] = jnp.sum(inner * unit, axis=0, keepdims=True)
    sums_ref[6:7, :] = jnp.sum(inner, axis=0, keepdims=True)
    sums_ref[7:8, :] = jnp.sum(mixed_ref[...].astype(F32), axis=0, keepdims=True)


def attend_back_kernel(high, low, head_dim, q_ref, crop_q, crop_k, log_ref, weight_ref, *refs):
    branches, kvs = refs[:high], refs[high : high + low]
    outs = refs[high + low :]
    span = q_ref.shape[1]
    rows = q_ref.shape[0]
    branch = jnp.concatenate([ref[: rows // high, :] for ref in branches], axis=0)
    attended = lax.dot_general(
        branch, weight_ref[:span, :], (((1,), (1,)), ((), ())), preferred_element_type=F32
    ).astype(BF)
    same = crop_k[...] == crop_q[...]
    scale = 1.0 / math.sqrt(head_dim)
    pieces = []
    for head in range(span // head_dim):
        at = head * head_dim
        queries = q_ref[:, at : at + head_dim] * jnp.asarray(scale, BF)
        keys = head_columns(kvs, at, head_dim)
        values = head_columns(kvs, span + at, head_dim)
        grad_out = attended[:, at : at + head_dim]
        share = jnp.exp(masked_scores(keys, queries, same) - log_ref[head : head + 1, :])
        weights = lax.dot_general(
            values, grad_out, (((1,), (1,)), ((), ())), preferred_element_type=F32
        )
        row_dot = jnp.sum(share * weights, axis=0, keepdims=True)
        grad_scores = (share * (weights - row_dot)).astype(BF)
        grad_keys = jnp.dot(grad_scores, queries, preferred_element_type=F32)
        grad_values = jnp.dot(share.astype(BF), grad_out, preferred_element_type=F32)
        for s in range(low):
            part = slice(s * rows, (s + 1) * rows)
            low_at = at + span if s == 0 else at
            outs[s][:, low_at : low_at + head_dim] = grad_keys[part, :].astype(BF)
            outs[s][:, span + low_at : span + low_at + head_dim] = grad_values[part, :].astype(BF)
        pieces.append(jnp.dot(keys.T, grad_scores, preferred_element_type=F32) * scale)
    outs[0][:, :span] = jnp.concatenate(pieces, axis=0).T.astype(BF)


def output_grad_kernel(high, low, info, *refs):
    attended = jnp.concatenate([ref[...] for ref in refs[:high]], axis=0)
    rows = refs[0].shape[0]
    branch = jnp.concatenate([ref[:rows, :] for ref in refs[high : 2 * high]], axis=0)
    outs, scratch_ref = refs[2 * high : -1], refs[-1]
    scratch_ref[...] = cross_rows(attended, branch)
    deal_chip(info, low, scratch_ref, outs)


def joint_back_kernel(high, low, info, own_ref, normed_ref, weight_ref, vec_ref, sums_ref,
                      bias_ref, *refs):
    dkvs, outs = refs[: low - 1], refs[low - 1 :]
    joint_ref, scratch_ref = outs[-2], outs[-1]
    backs, dealt = outs[:high], outs[high : high + low]
    span = own_ref.shape[1] // 3
    joint_ref[...] = jnp.zeros_like(joint_ref)
    joint_ref[:, :span] = own_ref[:, :span]
    total = own_ref[:, span:].astype(F32)
    for ref in dkvs:
        total = total + ref[...].astype(F32)
    joint_ref[:, span : 3 * span] = total.astype(BF)
    rows = backs[0].shape[0]
    gain_sum, shift_sum = 0.0, 0.0
    for m in range(high):
        part = lax.dot_general(
            joint_ref[m * rows : (m + 1) * rows, :], weight_ref[...], (((1,), (1,)), ((), ())),
            preferred_element_type=F32,
        )
        backs[m][...] = part.astype(backs[m].dtype)
        unit = normed_ref[(high + m) * rows : (high + m + 1) * rows, :].astype(F32)
        gain_sum = gain_sum + jnp.sum(part * unit, axis=0, keepdims=True)
        shift_sum = shift_sum + jnp.sum(part, axis=0, keepdims=True)
    wide = joint_ref.shape[1]
    width = normed_ref.shape[1]
    scratch_ref[...] = cross_rows(normed_ref[: high * rows, :], joint_ref[...])
    whole = jnp.concatenate(
        [
            jnp.zeros((64, width), F32), gain_sum, shift_sum, sums_ref[2:8, :],
            jnp.zeros((56, width), F32),
        ],
        axis=0,
    )
    scratch_ref[:, wide - 128 :] += whole.T
    sums = jnp.sum(joint_ref[...].astype(F32), axis=0, keepdims=True)
    own = jnp.concatenate(
        [
            jnp.zeros((66, span), F32), sums[:, :span], sums[:, 2 * span : 3 * span],
            jnp.zeros((4, span), F32), bias_ref[...],
            jnp.zeros((56 - bias_ref.shape[0], span), F32),
        ],
        axis=0,
    )
    at = pl.multiple_of(info[1] * span, 8)
    scratch_ref[pl.ds(at, span), wide - 128 :] += own.T
    deal_rows(info, high, low, scratch_ref, dealt)


def chip_add_kernel(high, low, *refs):
    parts, outs = refs[:-high], refs[-high:]
    for m in range(high):
        done = 0
        for start in range(0, len(parts), low):
            total = parts[start][m].astype(F32)
            for ref in parts[start + 1 : start + low]:
                total = total + ref[m].astype(F32)
            outs[m][done : done + total.shape[0], :] = total.astype(BF)
            done += total.shape[0]
        if done < outs[m].shape[0]:
            outs[m][done:, :] = jnp.zeros((outs[m].shape[0] - done, outs[m].shape[1]), BF)


def side_pack_kernel(high, low, info, *refs):
    joints, outputs = refs[:high], refs[high : high + low]
    pieces, pack_ref = refs[high + low : -1], refs[-1]
    chans = pack_ref.shape[1]
    rows, done = joints[0].shape[0], 0
    for m in range(high):
        for at in range(0, joints[m].shape[1], chans):
            pack_ref[done : done + rows, :] = joints[m][:, at : at + chans].astype(F32)
            done += rows
    total = outputs[0][...].astype(F32)
    for ref in outputs[1:]:
        total = total + ref[...].astype(F32)
    for at in range(0, total.shape[1], chans):
        pack_ref[done : done + rows, :] = total[:, at : at + chans]
        done += rows
    if done < pack_ref.shape[0]:
        pack_ref[done:, :] = jnp.zeros((pack_ref.shape[0] - done, chans), F32)
    size = pieces[0].shape[0]
    for t in range(len(pieces)):
        at = pl.multiple_of((info[3] ^ t) * size, 8)
        pieces[t][...] = pack_ref[pl.ds(at, size), :].astype(BF)


def conv_final_kernel(info, own_ref, other_ref, two_ref, resid_ref, one_ref, up_ref, whole_ref):
    joined_halves(info[4] == 1, own_ref, other_ref, whole_ref)
    chans = whole_ref.shape[1]
    rows, done = up_ref.shape[0], 0
    for ref in (two_ref, resid_ref, one_ref):
        ref[...] = whole_ref[done : done + ref.shape[0], :]
        done += ref.shape[0]
    for at in range(0, up_ref.shape[1], chans):
        up_ref[:, at : at + chans] = whole_ref[done : done + rows, :]
        done += rows


def mix_pack_kernel(high, rows, *refs):
    branches, pack_ref = refs[:high], refs[high]
    done = 0
    for ref in branches:
        size = ref.shape[0] - rows
        pack_ref[done : done + size, :] = ref[rows:, :]
        done += size


def joined_halves(upper, own_ref, other_ref, whole_ref):
    half = own_ref.shape[0]
    whole_ref[:half, :] = jnp.where(upper, other_ref[...], own_ref[...]).astype(F32)
    whole_ref[half:, :] = jnp.where(upper, own_ref[...], other_ref[...]).astype(F32)


def side_final_kernel(high, info, *refs):
    joint_ref, vec_ref, out_ref, whole_ref = refs[-4:]
    pieces = refs[:-4]
    size = pieces[0].shape[0]
    for t in range(len(pieces)):
        at = pl.multiple_of((info[3] ^ t) * size, 8)
        whole_ref[pl.ds(at, size), :] = pieces[t][...].astype(F32)
    chans = whole_ref.shape[1]
    rows = joint_ref.shape[0]
    span = joint_ref.shape[1] // (3 * high)
    third = joint_ref.shape[1] // 3
    tiles = -(-(3 * span + 64) // chans)

    def block(m):
        return jnp.concatenate(
            [
                whole_ref[(m * tiles + j) * rows : (m * tiles + j + 1) * rows, :]
                for j in range(tiles)
            ],
            axis=1,
        )

    for place in range(high):

        @pl.when(info[1] == place)
        def _():
            for group in range(high):
                values = block(place ^ group)
                for part in range(3):
                    at = part * third + group * span
                    joint_ref[:, at : at + span] = values[:, part * span : (part + 1) * span]

    total = block(0)[:, (tiles - 1) * chans :]
    for m in range(1, high):
        total = total + block(m)[:, (tiles - 1) * chans :]
    vec_ref[...] = total.T[64:80, :]
    done = high * tiles * rows
    for at in range(0, out_ref.shape[1], chans):
        out_ref[:, at : at + chans] = whole_ref[done : done + rows, :]
        done += rows


def mix_final_kernel(
    high, info, own_ref, other_ref, reduce_own, reduce_other, expand_ref, reduce_ref, whole_ref
):
    joined_halves(info[4] == 1, reduce_own, reduce_other, reduce_ref)
    joined_halves(info[4] == 1, own_ref, other_ref, whole_ref)
    wide = expand_ref.shape[1] // high
    rows = expand_ref.shape[0]
    for place in range(high):

        @pl.when(info[1] == place)
        def _():
            for group in range(high):
                m = place ^ group
                expand_ref[:, group * wide : (group + 1) * wide] = whole_ref[
                    m * rows : (m + 1) * rows, :
                ]


def tokens_kernel(high, grad_ref, token_ref, vec_ref, *refs):
    parts, out_ref = refs[:high], refs[high]
    unit, inv_std = unit_rows_of(token_ref[...].astype(F32))
    out_ref[...] = grad_ref[...] + norm_back(plane_total(parts), unit, inv_std, vec_ref[0:1, :])


def on_device(
    tokens,
    skip_features,
    out_grad,
    crop_lengths,
    attend_gain,
    attend_shift,
    joint_weight,
    query_bias,
    value_bias,
    output_weight,
    output_bias,
    mixer_gain,
    mixer_shift,
    expand_weight,
    expand_bias,
    reduce_weight,
    reduce_bias,
    upsample_weight,
    kernel_first,
    kernel_second,
    residual_weight,
):
    count = lax.axis_size("seq")
    nb = lax.axis_size("batch")
    high = math.gcd(HEADS, count)
    low = count // high
    seq_index = lax.axis_index("seq")
    batch_index = lax.axis_index("batch")
    hi = seq_index // low
    lo = seq_index % low
    width = tokens.shape[2]
    shard = joint_weight.shape[0]
    head_dim = width // HEADS
    span = HEADS // high * head_dim
    wide = -(-(3 * span + 64) // 128) * 128
    hidden = expand_weight.shape[1]
    hid_span = hidden // high
    hid_shard = hidden // count
    channels = residual_weight.shape[1]
    plane_size = PH * PH
    tok_rows = tokens.shape[1]
    rows = high * tok_rows
    slices = tok_rows // plane_size
    depth_total = 2 * slices
    positions = depth_total * 4 * plane_size
    lengths = crop_lengths[0]
    own_tokens = tokens[0]
    place = batch_index % 2 if nb == 4 else 0 * hi
    info = jnp.stack([seq_index % 2, hi, lo, batch_index, place]).astype(jnp.int32)

    def plane_swaps(blocks):
        return [swap(blocks[m], "seq", m * low) for m in range(1, high)]

    def plane_copies(block):
        return [block] + [swap(block, "seq", m * low) for m in range(1, high)]

    def gather_list(block):
        return [block] + [swap(block, "batch", t) for t in range(1, nb)]

    def chip_swaps(blocks):
        return [swap(blocks[s], "seq", s) for s in range(1, low)]

    def chip_copies(block):
        return [swap(block, "seq", s) for s in range(1, low)]

    def after(values, done):
        return lax.optimization_barrier((values, tuple(done)))[0]

    def owners(rel_hi, rel_lo):
        return (hi ^ rel_hi) * low + (lo ^ rel_lo)

    def odd_swap(values):
        pairs = [(i, i + 1) for i in range(1, count - 1, 2)]
        return lax.ppermute(values, "seq", pairs + [(j, i) for i, j in pairs])

    vectors = [
        attend_gain, attend_shift, query_bias, value_bias, output_bias, mixer_gain, mixer_shift,
        reduce_bias,
    ]
    vectors = [
        jnp.stack([vec.astype(F32) for vec in vectors]),
        expand_bias.astype(F32).reshape(hid_shard // shard, shard),
    ]
    packed = call(
        functools.partial(pack_kernel, high),
        [((tok_rows + shard, width), BF)] * high + [((2, shard, width), BF)] * high,
        [],
        info, own_tokens, joint_weight, expand_weight, output_weight, *vectors, smem=1,
    )
    all_tokens = list(packed[:1]) + plane_swaps(packed[:high])
    partners = chip_copies(jnp.concatenate([part[tok_rows:, :wide] for part in all_tokens], axis=0))
    q, kv, normed, joint_w, vecs, own_vecs = call(
        functools.partial(query_kernel, high, low),
        [((rows, span), BF), ((rows, 2 * span), BF), ((2 * rows, width), BF), ((width, wide), BF),
         ((16, width), F32), ((16, span), F32)],
        [((count, shard, wide), F32)],
        info, *all_tokens, *partners, smem=1,
    )
    kvs = [kv] + chip_copies(kv)

    def ordered(parts, natural, shape, block):
        kernel = functools.partial(order_kernel, block[0], low, natural)
        return call(
            kernel, [(shape, BF)], [((block[0] * low, block[1], shape[1]), F32)], info, *parts,
            smem=1,
        )[0]

    later_pairs = after(tuple(packed[high:]), all_tokens[1:])
    pairs = [later_pairs[0]] + plane_swaps(later_pairs)
    kvs, pairs[1] = lax.optimization_barrier((kvs, pairs[1]))
    expand_b = own_vecs[8 : 8 + hid_shard // shard].reshape(hid_shard // shard, low, shard)
    expand_b = expand_b.transpose(1, 0, 2).reshape(1, hid_span)
    later_up, later_conv = after(
        (upsample_weight, (kernel_first, kernel_second, residual_weight)), ()
    )
    upsample_w = lax.all_gather(later_up, "seq", axis=0, tiled=True)
    conv_all = lax.all_gather(
        jnp.concatenate(later_conv, axis=0), "seq", axis=0
    )
    cut_one = kernel_first.shape[0]
    cut_two = cut_one + kernel_second.shape[0]
    kernel_one = conv_all[:, :cut_one].reshape(-1, channels)
    kernel_two = conv_all[:, cut_one:cut_two].reshape(-1, channels)
    residual_w = conv_all[:, cut_two:].reshape(-1, channels)

    def token_crops(rel_lo):
        starts = jnp.stack([owners(m, rel_lo) for m in range(high)]) * slices
        ids = starts[:, None] + jnp.arange(tok_rows, dtype=jnp.int32)[None, :] // plane_size
        return crops_of(lengths, ids.reshape(-1))

    crop_q = token_crops(0).reshape(1, rows)
    crop_k = jnp.concatenate([token_crops(s) for s in range(low)]).reshape(low * rows, 1)
    *attended, log_total = call(
        functools.partial(attend_kernel, high, head_dim),
        [((tok_rows, span), BF)] * high + [((8, rows), F32)],
        [],
        q, crop_q, crop_k, *kvs,
    )
    arrived = [attended[0]] + plane_swaps(attended)
    pairs = list(after(tuple(pairs), (arrived[1],)))
    pairs += chip_copies(jnp.stack(pairs))
    expand_w, out_w = call(
        functools.partial(pair_kernel, high, low),
        [((width, hid_span), BF), ((width, width), BF)],
        [((count, shard, width), F32)],
        info, *pairs, smem=1,
    )
    middle, inner = call(
        functools.partial(middle_kernel, high),
        [((tok_rows, width), F32), ((tok_rows, width), BF)],
        [],
        own_tokens, out_w, vecs, *arrived,
    )
    inners = plane_copies(inner)
    reduces = [reduce_weight] + chip_copies(after(reduce_weight, (inner,)))
    reduce_w = ordered(reduces, False, (hid_span, width), (1, hid_shard))
    partial_kinds = [((tok_rows, width), F32)] + [((tok_rows, width), BF)] * (high - 1)
    inners[1], (kernel_one, kernel_two) = lax.optimization_barrier(
        (inners[1], (kernel_one, kernel_two))
    )
    *mixed, act, slope = call(
        functools.partial(mix_kernel, high),
        partial_kinds + [((rows, hid_span), BF), ((rows, hid_span), F32)],
        [],
        middle, expand_w, reduce_w, expand_b, *inners,
    )
    mixed = [mixed[0]] + plane_swaps(mixed)

    def to_cells(values):
        cells = values.reshape(slices, 2, CELLS, channels)
        return cells.transpose(2, 1, 0, 3).reshape(positions, channels)

    def from_cells(values):
        cells = values.reshape(CELLS, 2, slices, channels)
        return cells.transpose(2, 1, 0, 3).reshape(positions, channels)

    late_lengths, late_skip, late_cot = after((lengths, skip_features[0], out_grad[0]), (act,))
    slice_ids = seq_index * slices - 1 + jnp.arange(slices + 2, dtype=jnp.int32)
    crop_ids = jnp.where(slice_ids < 0, -1, crops_of(late_lengths, slice_ids))
    here = crop_ids[1:-1]
    masks = jnp.stack([crop_ids[:-2] == here, crop_ids[2:] == here]).astype(F32)
    masks = jnp.broadcast_to(masks[:, :, None], (2, slices, channels))
    onehot = (jnp.arange(CROPS, dtype=jnp.int32)[:, None] == here[None, :]).astype(F32)
    onehot = jnp.broadcast_to(
        jnp.tile(onehot, (1, 2))[:, :, None], (CROPS, depth_total, channels)
    )
    total = jnp.broadcast_to(
        (late_lengths * 8 * plane_size).astype(F32)[:, None], (CROPS, channels)
    )
    crop_ends = jnp.cumsum(late_lengths)
    dev_rel = jnp.stack([owners(m, s) for s in range(low) for m in range(high)])
    first = (dev_rel * slices)[:, None]
    shared = jnp.minimum(crop_ends[None], first + slices) - jnp.maximum(
        (crop_ends - late_lengths)[None], first
    )
    held = (jnp.maximum(shared, 0) * 8 * plane_size).astype(F32)
    held = jnp.broadcast_to(held[:, :, None], (count, CROPS, channels))
    skip_cells = to_cells(late_skip)
    cot_cells = to_cells(late_cot)
    sides = jnp.concatenate([late_skip, late_cot], axis=1)
    sides = jnp.concatenate([sides[:CELLS], sides[-CELLS:]], axis=0)
    prepared = (
        onehot, held, masks, total, skip_cells, cot_cells, sides, kernel_one, kernel_two,
        residual_w, upsample_w,
    )
    mixed[1], prepared = lax.optimization_barrier((mixed[1], prepared))
    onehot, held, masks, total, skip_cells, cot_cells, sides = prepared[:7]
    kernel_one, kernel_two, residual_w, upsample_w = prepared[7:]

    cells_bf = ((positions, channels), BF)
    cells_f = ((positions, channels), F32)
    slab_f = ((CELLS, channels), F32)
    slab_bf = ((CELLS, 3 * channels), BF)
    slabs_f = ((2 * CELLS, channels), F32)
    tile = ((2 * CROPS, channels), F32)
    grid_acc = ((GRID, GRID, depth_total, channels), F32)

    def exchange(own_tile, even_slab=None, odd_slab=None):
        tiles = plane_copies(own_tile)
        if even_slab is None:
            return tiles + chip_copies(jnp.concatenate(tiles, axis=0)), None
        odd_slab = odd_swap(odd_slab)
        even_slab, odd_slab = lax.optimization_barrier((even_slab, odd_slab))
        return tiles + chip_copies(jnp.concatenate(tiles + [even_slab], axis=0)), odd_slab

    encoded, upsampled, up_even, up_odd = call(
        functools.partial(up_kernel, high, slices),
        [((tok_rows, width), BF), cells_bf, slab_bf, slab_bf],
        [cells_f],
        info, vecs, upsample_w, sides, *mixed, smem=1,
    )
    up_even, up_odd = swap(up_even, "seq", 1), odd_swap(up_odd)
    first_conv, tile_one, even_one, odd_one, joined_stack, joined_halo = call(
        first_kernel,
        [cells_f, tile, slab_f, slab_f, ((positions, 6 * channels), BF),
         ((2 * CELLS, 2 * channels), BF)],
        [grid_acc],
        info, onehot, held, masks, upsampled, up_even, up_odd, skip_cells,
        kernel_one, smem=1,
    )
    tiles, odd_one = exchange(tile_one, even_one, odd_one)
    (second_conv, tile_two, even_two, odd_two, act_stack, first_unit, slab_unit, scale_one) = call(
        functools.partial(second_kernel, high),
        [cells_f, tile, slab_f, slab_f, ((positions, 3 * channels), BF), cells_f, slabs_f,
         ((2, depth_total, channels), F32)],
        [grid_acc],
        info, onehot, held, total, masks, first_conv, odd_one, kernel_two, *tiles, smem=1,
    )
    tiles, odd_two = exchange(tile_two, even_two, odd_two)
    decoded_cells, grad_summed, grad_resid, second_unit, slab_two, tile_three, inv_two = call(
        functools.partial(third_kernel, high),
        [cells_bf, cells_f, cells_bf, cells_f, ((2 * CELLS, 2 * channels), F32), tile,
         ((depth_total, channels), F32)],
        [],
        info, onehot, held, total, second_conv, odd_two, joined_stack, joined_halo,
        residual_w, cot_cells, up_even, up_odd, *tiles, smem=1,
    )
    decoded = from_cells(decoded_cells)
    tiles, _ = exchange(tile_three)
    grad_second, grad_back, tile_four, even_four, odd_four = call(
        functools.partial(fourth_kernel, high),
        [cells_bf, cells_f, tile, slab_f, slab_f],
        [grid_acc],
        info, onehot, total, masks, grad_summed, second_unit, inv_two, slab_two, first_unit,
        kernel_two, *tiles, smem=1,
    )

    def tap_grad(stack, upstream, in_chans, left, right, wide_blocks, extra_shape):
        part = 27 * in_chans // count
        extra = extra_shape[0] // count
        dealt = call(
            functools.partial(tap_grad_kernel, in_chans, high, low, wide_blocks),
            [((high, part + wide_blocks * extra, channels), BF)] * low,
            [((9 * channels, positions), BF),
             ((GRID + 2, GRID + 2, depth_total, channels), BF),
             ((count, -(-part // 8) * 8, channels), F32),
             ((count, extra, extra_shape[1]), F32)],
            info, stack, upstream, left, right, smem=1,
        )
        return dealt

    def chip_add(*groups):
        held = sum(group[0].shape[1] for group in groups)
        held = -(-held // 32) * 32 if len(groups) > 1 else held
        kind = [((held, groups[0][0].shape[2]), BF)] * high
        parts = [part for group in groups for part in group]
        return call(functools.partial(chip_add_kernel, high, low), kind, [], *parts)

    class Cube:
        def __init__(self, values):
            self.stage, self.values = 0, values
            if nb == 4:
                self.got = self.split(batch_index % 2, 1)
            else:
                whole = lax.psum(values, "batch")
                half = whole.shape[0] // 2
                self.values, self.got = whole[:half], whole[half:]

        def split(self, bit, mask):
            half = self.values.shape[0] // 2
            sent = lax.dynamic_slice_in_dim(self.values, (1 - bit) * half, half)
            self.values = lax.dynamic_slice_in_dim(self.values, bit * half, half)
            return swap(sent, "batch", mask)

        def step(self):
            if nb != 4:
                return
            self.stage += 1
            if self.stage < 3:
                self.values = sum_list([self.values, self.got]).astype(BF)
            if self.stage == 1:
                self.got = self.split(batch_index // 2, 2)
            elif self.stage == 2:
                self.got = swap(self.values, "batch", 2)
            else:
                self.values = jnp.where(
                    batch_index // 2 == 1,
                    jnp.concatenate([self.got, self.values], axis=0),
                    jnp.concatenate([self.values, self.got], axis=0),
                )
                self.got = swap(self.values, "batch", 1)

    tiles, odd_four = exchange(tile_four, even_four, odd_four)
    two_dealt = tap_grad(
        act_stack, grad_second, channels, joined_stack, grad_resid, 1, (2 * channels, channels)
    )
    grad_first, skip_cells_grad, grad_up_rows, grad_encoded, own_mixed = call(
        functools.partial(fifth_kernel, high, slices),
        [cells_bf, cells_f, ((tok_rows, 8 * channels), BF), ((tok_rows, width), F32),
         ((tok_rows, width), BF)],
        [((GRID, GRID, depth_total, 2 * channels), F32)],
        info, onehot, total, masks, grad_back, first_unit, scale_one, slab_unit, odd_four,
        grad_resid, kernel_one, residual_w, upsample_w, *tiles, smem=1,
    )
    skip_grad = from_cells(skip_cells_grad)

    def pin(first, second):
        if not isinstance(first, (list, tuple)):
            return lax.optimization_barrier((first, second))
        last, second = lax.optimization_barrier((first[-1], second))
        return list(first[:-1]) + [last], second

    grads_mixed = plane_copies(own_mixed)
    two_dealt = list(two_dealt)
    one_dealt = list(tap_grad(
        joined_stack, grad_first, 2 * channels, encoded, grad_up_rows, 8, (width, 8 * channels)
    ))
    grads_mixed, (one_dealt[0], two_dealt[0]) = pin(grads_mixed, (one_dealt[0], two_dealt[0]))
    *inner_parts, grad_expanded = call(
        functools.partial(mix_back_kernel, high),
        partial_kinds + [((rows, hid_span), BF)],
        [],
        reduce_w, expand_w, slope, *grads_mixed,
    )
    inner_parts = [inner_parts[0]] + plane_swaps(inner_parts)
    *mix_dealt, expand_bias_part = call(
        functools.partial(mix_grad_kernel, high, low),
        [((high * shard + hid_shard, width), BF)] * low + [((1, hid_span), F32)],
        [((width, hid_span), F32)],
        info, act, grad_expanded, *grads_mixed, *inners, smem=1,
    )
    mix_dealt = [mix_dealt[0]] + chip_swaps(mix_dealt)
    one_dealt = after(tuple(one_dealt), (grad_expanded,))
    one_dealt = [one_dealt[0]] + chip_swaps(one_dealt)
    inner_parts, one_dealt[1] = pin(inner_parts, one_dealt[1])
    grad_middle, sums, reduce_sum, *branches = call(
        functools.partial(branch_kernel, high, low),
        [((tok_rows, width), F32), ((8, width), F32), ((hid_shard, width), BF)]
        + [((tok_rows + shard, width), BF)] * high,
        [],
        middle, vecs, grad_encoded, own_mixed, *inner_parts, *mix_dealt,
    )
    two_dealt, one_dealt = after((tuple(two_dealt), tuple(one_dealt)), (sums,))
    two_dealt = [two_dealt[0]] + chip_swaps(two_dealt)
    branches = [branches[0]] + plane_swaps(branches)
    reduce_cube = Cube(reduce_sum)
    conv_blocks = chip_add(two_dealt, one_dealt)
    conv_blocks = list(conv_blocks)
    branches, (conv_blocks[1], reduce_cube.got) = pin(
        branches, (conv_blocks[1], reduce_cube.got)
    )
    reduce_cube.step()
    conv_blocks = [conv_blocks[0]] + plane_swaps(conv_blocks)
    mix_cube = Cube(
        call(
            functools.partial(mix_pack_kernel, high, tok_rows),
            [((high * shard, width), BF)],
            [],
            *branches,
        )[0]
    )
    own_dqkv, *dkvs = call(
        functools.partial(attend_back_kernel, high, low, head_dim),
        [((rows, 3 * span), BF)] + [((rows, 2 * span), BF)] * (low - 1),
        [],
        q, crop_q, crop_k, log_total, out_w, *branches, *kvs,
    )
    dkvs[-1], (mix_cube.got, reduce_cube.got) = pin(
        dkvs[-1], (mix_cube.got, reduce_cube.got)
    )
    reduce_cube.step()
    dkvs = chip_swaps([own_dqkv] + dkvs)
    mix_cube.step()
    dkvs, reduce_cube.got = pin(dkvs, reduce_cube.got)
    reduce_cube.step()
    conv_cube = Cube(sum_list(conv_blocks).astype(BF))
    expand_bias_part = expand_bias_part.reshape(low, hid_shard // shard, shard)
    expand_bias_part = expand_bias_part.transpose(1, 0, 2).reshape(hid_shard // shard, span)
    joint_outs = call(
        functools.partial(joint_back_kernel, high, low),
        partial_kinds + [((high, shard, wide), BF)] * low,
        [((rows, wide), BF), ((width, wide), F32)],
        info, own_dqkv, normed, joint_w, vecs, sums, expand_bias_part, *dkvs, smem=1,
    )
    normed_parts, joint_dealt = joint_outs[:high], joint_outs[high:]
    joint_dealt, (mix_cube.got, conv_cube.got, reduce_cube.got) = pin(
        joint_dealt, (mix_cube.got, conv_cube.got, reduce_cube.got)
    )
    conv_cube.step()
    mix_cube.step()

    blocks = chip_add([joint_dealt[0]] + chip_swaps(joint_dealt))
    blocks = [blocks[0]] + plane_swaps(blocks)
    out_dealt = call(
        functools.partial(output_grad_kernel, high, low),
        [((shard, width), BF)] * low,
        [((span, width), F32)],
        info, *attended, *branches, smem=1,
    )
    out_dealt = [out_dealt[0]] + chip_swaps(out_dealt)
    blocks, conv_cube.got, mix_cube.got, out_dealt[1] = lax.optimization_barrier(
        (blocks, conv_cube.got, mix_cube.got, out_dealt[1])
    )
    conv_cube.step()
    mix_cube.step()
    tiles = wide // channels
    side_rows = (high * tiles + width // channels) * shard
    side_size = -(-side_rows // (16 * nb)) * 16
    pieces = call(
        functools.partial(side_pack_kernel, high, low),
        [((side_size, channels), BF)] * nb,
        [((side_size * nb, channels), F32)],
        info, *blocks, *out_dealt, smem=1,
    )
    pieces = [pieces[0]] + [swap(pieces[t], "batch", t) for t in range(1, nb)]
    normed_parts = after(tuple(normed_parts), blocks[1:])
    normed_parts = [normed_parts[0]] + plane_swaps(normed_parts)
    pieces, (mix_cube.got, conv_cube.got) = pin(pieces, (mix_cube.got, conv_cube.got))
    conv_cube.step()
    pieces = gather_list(sum_list(pieces).astype(BF))
    tokens_grad = call(
        functools.partial(tokens_kernel, high),
        [((tok_rows, width), F32)],
        [],
        grad_middle, own_tokens, vecs, *normed_parts,
    )[0]
    expand_grad, reduce_grad = call(
        functools.partial(mix_final_kernel, high),
        [((shard, hidden), F32), ((hid_shard, width), F32)],
        [((high * shard, width), F32)],
        info, mix_cube.values, mix_cube.got, reduce_cube.values, reduce_cube.got, smem=1,
    )
    pieces, (expand_grad, reduce_grad, tokens_grad) = pin(
        pieces, (expand_grad, reduce_grad, tokens_grad)
    )
    kernel_two_grad, residual_grad, kernel_one_grad, upsample_grad = call(
        conv_final_kernel,
        [(kernel_second.shape, F32), (residual_weight.shape, F32), (kernel_first.shape, F32),
         ((shard, 8 * channels), F32)],
        [((2 * conv_cube.values.shape[0], channels), F32)],
        info, conv_cube.values, conv_cube.got, smem=1,
    )
    joint_grad, vec_grads, output_grad = call(
        functools.partial(side_final_kernel, high),
        [((shard, 3 * width), F32), ((16, shard), F32), ((shard, width), F32)],
        [((side_size * nb, channels), F32)],
        info, *pieces, smem=1,
    )
    return (
        decoded[None],
        tokens_grad[None],
        skip_grad[None],
        vec_grads[0],
        vec_grads[1],
        joint_grad,
        vec_grads[2],
        vec_grads[3],
        output_grad,
        vec_grads[4],
        vec_grads[5],
        vec_grads[6],
        expand_grad,
        vec_grads[8 : 8 + hid_shard // shard].reshape(hid_shard),
        reduce_grad,
        vec_grads[7],
        upsample_grad,
        kernel_one_grad,
        kernel_two_grad,
        residual_grad,
    )


def solution(mesh):
    rows = P("batch", "seq", None)
    vec = P("seq")
    mat = P("seq", None)
    in_specs = (rows, rows, rows, P("batch", None))
    in_specs += (vec, vec, mat, vec, vec, mat, vec, vec, vec, mat, vec, mat, vec)
    in_specs += (mat, mat, mat, mat)
    out_specs = (rows, rows, rows)
    out_specs += (vec, vec, mat, vec, vec, mat, vec, vec, vec, mat, vec, mat, vec)
    out_specs += (mat, mat, mat, mat)
    return jax.shard_map(
        on_device, mesh=mesh, in_specs=in_specs, out_specs=out_specs, check_vma=False
    )
```
